128 devices in a mesh: sfc: 128 (over y, z, x, core).
Axes of the slice: x: 4, y: 4, z: 4, core: 2. Of those that a mesh axis runs over, the one named last changes fastest.
Arguments:
- state: float32 [5, 4, 4, 4, 65536], P(None, None, None, None, 'sfc'), may hold values from -6 to 6
- neighbour_map: int32 [6, 65536], P(None, 'sfc'), may hold values from 0 to 767, as said below
- layer_lists: int32 [2, 32768], P(None, 'sfc'), may hold values from 0 to 511, as said below
- forces: float32 [5, 65536], P(None, 'sfc'), may hold values from -24 to 24
- positions: float32 [3, 65536], P(None, 'sfc'), may hold values from -1 to 1
- route: int32 [65536, 1], P('sfc'), may hold values from 0 to 127; in each aligned block of 512 rows (0 to 511, 512 to 1023, ...) at most 8 rows name the same one
- element_slot: int32 [65536], P('sfc'), may hold values from 0 to 511
Outputs:
- new_state: float32 [5, 4, 4, 4, 65536], P(None, None, None, None, 'sfc')
The draws below stay inside these ranges and needn't reach their ends.
Inputs may be any that keep to these rules, and one draw needn't show every extreme that they name: `neighbour_map`: each device's elements form a block of 16 x 16 x 2 elements, periodic in x and y, numbered in a drawn order; layer order is x fastest, then y. Faces along x and y name elements of the same device; -z faces of the bottom layer and +z faces of the top layer name 512 + the element's position in layer order, other z faces the element across on the same device. The connection is symmetric, devices in a loop along z. `layer_lists`: row 0 lists the bottom layer, row 1 the top layer of each device. `route`: among the points of one device, at most 8 name the same device.
All inputs are finite; a program needn't handle non-finite values.
Results may differ from the reference program's by a relative error of at most 0.0001.
Values sent between devices are 32-bit elements; how exact they have to be, the bound alone decides.
No kernel may reach another device: no remote copies, remote signals or barrier semaphores. Data moves between devices by JAX's collectives and lax.ppermute only.
A program may use at most 64 MiB of HBM per device.

```python
import math
import jax
import jax.numpy as jnp
import numpy as np
from jax import lax

VARS = 5
NODE_LINE = 4
NEX = 16
LAYERS = 2
P_DEV = 512
PLANE = 256
E_DEV = 512
ELEMS = 65536
CAP = 8
P_TOTAL = 65536
N_SFC = 128


def layer_numbers(key):
    devices = ELEMS // (NEX * NEX * LAYERS)
    keys = jax.random.split(key, devices)
    return jax.vmap(lambda one_key: jax.random.permutation(one_key, NEX * NEX * LAYERS))(keys).astype(jnp.int32)


def draw_neighbour_map(key, part):
    numbers = layer_numbers(key)
    plane = NEX * NEX
    cells = plane * LAYERS
    spot = jnp.arange(cells, dtype=jnp.int32)
    col_x = spot % NEX
    col_y = spot // NEX % NEX
    col_z = spot // plane
    in_plane = col_x + NEX * col_y

    def structural(x_pos, y_pos, z_pos):
        return x_pos % NEX + NEX * (y_pos % NEX + NEX * z_pos)
    below = jnp.clip(col_z - 1, 0, LAYERS - 1)
    above = jnp.clip(col_z + 1, 0, LAYERS - 1)
    spots = [structural(col_x - 1, col_y, col_z), structural(col_x + 1, col_y, col_z), structural(col_x, col_y - 1, col_z), structural(col_x, col_y + 1, col_z), structural(col_x, col_y, below), structural(col_x, col_y, above)]
    tables = [jnp.take(numbers, where_at, axis=1) for where_at in spots]
    tables[4] = jnp.where((col_z == 0)[None, :], (cells + in_plane)[None, :], tables[4])
    tables[5] = jnp.where((col_z == LAYERS - 1)[None, :], (cells + in_plane)[None, :], tables[5])
    inverse = jnp.argsort(numbers, axis=1, stable=True).astype(jnp.int32)
    rows = [jnp.take_along_axis(table, inverse, axis=1) for table in tables]
    stacked = jnp.stack(rows, axis=0)
    return stacked.reshape(6, -1).astype(jnp.int32)


def draw_layer_lists(key, part):
    numbers = layer_numbers(key)
    plane = NEX * NEX
    cells = plane * LAYERS
    bottom = numbers[:, :plane]
    top_layer = numbers[:, cells - plane:]
    return jnp.stack([bottom, top_layer], axis=0).reshape(2, -1).astype(jnp.int32)


def place_ends(values, own_key, low, high):
    place = [jax.random.randint(jax.random.fold_in(own_key, axis), (), 0, length) for axis, length in enumerate(values.shape)]
    widest = values.shape.index(max(values.shape))
    next_to = place[:widest] + [(place[widest] + 1) % values.shape[widest]] + place[widest + 1:]
    return values.at[tuple(place)].set(low).at[tuple(next_to)].set(high)


def level_of(stream_key, dims, cuts, low, high):
    factor_of, own = 1.0, jax.random.fold_in(stream_key, 6)
    for position, shards_of in cuts:
        steps = jnp.exp(jax.random.uniform(jax.random.fold_in(own, position), (shards_of,), jnp.float32, low / len(cuts), high / len(cuts)))
        factor_of = factor_of * jnp.repeat(steps, dims[position] // shards_of).reshape([-1 if axis == position else 1 for axis in range(len(dims))])
    return factor_of


def routed_block(rng, own, number, rows, amount, top, most, skew):
    order = jax.random.permutation(rng, amount)
    packed, usual = shares(amount, rows * top, most, skew, True), shares(amount, rows * top, most, skew, False)
    places = jnp.arange(amount)

    def named(lengths, rotation):
        used = int((lengths > 0).sum())
        fixed = max(1, used // 4)
        moved = fixed + (places - fixed + rotation * (used - fixed)) % max(1, amount - fixed)
        return jnp.zeros((amount,), jnp.int32).at[order[jnp.where(places < fixed, places, moved)]].set(jnp.asarray(lengths, jnp.int32))

    lengths = jnp.where(number % 4 == 0, named(packed, number // 4), named(usual, number - number // 4 - 1))
    mixed = jax.random.permutation(jax.random.fold_in(own, 3), amount)
    source_of, taker = mixed[0:amount // 2 * 2:2], mixed[1:amount // 2 * 2:2]
    slack = jnp.minimum(lengths[source_of] - 1, most - lengths[taker]) // 2
    slack = jnp.where((source_of == order[0]) | (taker == order[0]) | (lengths[taker] == 0), 0, jnp.maximum(slack, 0))
    moved = jax.random.randint(jax.random.fold_in(own, 4), (amount // 2,), 0, 1 << 20) % (slack + 1)
    lengths = lengths.at[source_of].add(-moved).at[taker].add(moved)
    members = jnp.searchsorted(jnp.cumsum(lengths), jnp.arange(rows * top), side="right").astype(jnp.int32)
    listing = members.reshape(top, rows).T
    listing = listing[jax.random.permutation(jax.random.fold_in(own, 1), rows)]
    rotation = jax.random.randint(jax.random.fold_in(own, 2), (rows, 1), 0, top)
    return jnp.take_along_axis(listing, (jnp.arange(top)[None, :] + rotation) % top, axis=1)


def shares(amount, total, most, lean, full):
    loads = [(1 << 20) // math.isqrt(rank ** lean) + 1 for rank in range(1, amount + 1)]
    largest = most if full else min(most, max(-(-total // amount), total * loads[0] // sum(loads)))
    least = 1 if total - largest >= amount - 1 else 0
    counts, spare = [largest] + [least] * (amount - 1), total - largest - least * (amount - 1)
    while spare > 0:
        movable = [i for i in range(1, amount) if counts[i] < largest] or [i for i in range(1, amount) if counts[i] < most]
        pool, remaining = sum([loads[i] for i in movable]), spare
        for i in movable:
            more = min(most - counts[i], max(1, remaining * loads[i] // pool), spare)
            counts[i] = counts[i] + more
            spare = spare - more
    return np.array(counts)


def bell_draw(stream_key, extent, spread, limit, cuts=(), kind=jnp.bfloat16):
    values = jax.random.normal(stream_key, extent, jnp.float32) * spread
    if len(cuts) > 0:
        values = level_of(stream_key, extent, cuts, -0.22, 0.18) * values
    return jnp.clip(values, min=-limit, max=limit).astype(kind)


def setup_inputs(seed: int = 0) -> dict:
    streams_of = jax.random.split(jax.random.key(seed), 8)
    state = bell_draw(streams_of[0], (VARS, NODE_LINE, NODE_LINE, NODE_LINE, ELEMS), 1.0, 6.0, ((4, 128),), jnp.float32)
    neighbour_map = draw_neighbour_map(jax.random.fold_in(streams_of[7], 71), 0)
    layer_lists = draw_layer_lists(jax.random.fold_in(streams_of[7], 71), 0)
    forces = bell_draw(streams_of[3], (VARS, P_TOTAL), 4.0, 24.0, ((1, 128),), jnp.float32)
    positions = jnp.clip(jax.random.uniform(streams_of[4], (3, P_TOTAL), jnp.float32, -1.0, 1.0) * level_of(streams_of[4], (3, P_TOTAL), ((1, 128),), -0.4, 0.0), -1.0, 1.0)
    route_keys = jax.random.split(jax.random.fold_in(streams_of[5], 1), P_TOTAL // P_DEV)
    route_turns = jax.random.permutation(jax.random.fold_in(streams_of[5], 3), P_TOTAL // P_DEV)
    route = jax.vmap(lambda own, number: routed_block(jax.random.fold_in(streams_of[5], 2), own, number, P_DEV, N_SFC, 1, CAP, 2))(route_keys, route_turns).reshape((P_TOTAL, 1))
    element_slot = place_ends(jax.random.randint(streams_of[6], (P_TOTAL,), 0, E_DEV), jax.random.fold_in(streams_of[6], 1), 0, E_DEV - 1).astype(jnp.int32)
    return {"state": state, "neighbour_map": neighbour_map, "layer_lists": layer_lists, "forces": forces, "positions": positions, "route": route, "element_slot": element_slot}


NODE_POINTS = (-1.0, -0.4472135954999579, 0.4472135954999579, 1.0)
GSCALE = 2.0
HALF_LIFT = 6.0
ADVECT = (0.6, -0.4, 0.8)
VISCOSITY = 0.02
TIME_STEP = 0.04


def diff_table():
    factor = [float(np.prod([NODE_POINTS[a] - NODE_POINTS[k] for k in range(4) if k != a])) for a in range(4)]
    table = np.zeros((4, 4))
    for a in range(4):
        for b in range(4):
            if a != b:
                table[a, b] = (factor[a] / factor[b]) / (NODE_POINTS[a] - NODE_POINTS[b])
            else:
                table[a, b] = sum(1.0 / (NODE_POINTS[a] - NODE_POINTS[k]) for k in range(4) if k != a)
    return table


def derivative(values, axis_d):
    table = jnp.asarray(diff_table(), dtype=jnp.float32)
    forms = ("ab,vbjke->vajke", "ab,vibke->viake", "ab,vijbe->vijae")
    return jnp.einsum(forms[axis_d], table, values, precision=lax.Precision.HIGHEST)


def face_of(values, axis_d, node_at):
    return lax.index_in_dim(values, node_at, axis_d + 1, keepdims=False)


def add_face(values, axis_d, node_at, extra):
    if axis_d == 0:
        return values.at[:, node_at].add(extra)
    if axis_d == 1:
        return values.at[:, :, node_at].add(extra)
    return values.at[:, :, :, node_at].add(extra)


def boundary(values, lists):
    bottom = jnp.take(face_of(values, 2, 0), lists[0], axis=-1)
    top_layer = jnp.take(face_of(values, 2, 3), lists[1], axis=-1)
    return bottom, top_layer


def outer_traces(fields, neighbour_map, lower_side, upper_side):
    return [
        jnp.take(face_of(fields[0], 0, 3), neighbour_map[0], axis=-1),
        jnp.take(face_of(fields[0], 0, 0), neighbour_map[1], axis=-1),
        jnp.take(face_of(fields[1], 1, 3), neighbour_map[2], axis=-1),
        jnp.take(face_of(fields[1], 1, 0), neighbour_map[3], axis=-1),
        jnp.take(jnp.concatenate([face_of(fields[2], 2, 3), lower_side], axis=-1), neighbour_map[4], axis=-1),
        jnp.take(jnp.concatenate([face_of(fields[2], 2, 0), upper_side], axis=-1), neighbour_map[5], axis=-1),
    ]


def gradient(values, outer_u, scaled):
    slopes = []
    for d in range(3):
        slope = add_face(scaled[d], d, 0, (-HALF_LIFT) * (outer_u[2 * d] - face_of(values, d, 0)))
        slope = add_face(slope, d, 3, HALF_LIFT * (outer_u[2 * d + 1] - face_of(values, d, 3)))
        slopes.append(slope)
    return slopes


def operator(values, slopes, outer_u, outer_q, source):
    flux = [ADVECT[d] * values - VISCOSITY * slopes[d] for d in range(3)]
    result = source - GSCALE * (derivative(flux[0], 0) + derivative(flux[1], 1) + derivative(flux[2], 2))
    for d in range(3):
        for s, node_at, normal in ((0, 0, -1.0), (1, 3, 1.0)):
            along = normal * ADVECT[d]
            coeff_u = -HALF_LIFT * (along - abs(along))
            coeff_q = HALF_LIFT * VISCOSITY * normal
            jump_u = outer_u[2 * d + s] - face_of(values, d, node_at)
            jump_q = outer_q[2 * d + s] - face_of(slopes[d], d, node_at)
            result = add_face(result, d, node_at, coeff_u * jump_u + coeff_q * jump_q)
    return result


def line_basis(coords):
    rows = []
    for a in range(4):
        term = jnp.ones_like(coords)
        for k in range(4):
            if k != a:
                term = term * ((coords - float(NODE_POINTS[k])) / float(NODE_POINTS[a] - NODE_POINTS[k]))
        rows.append(term)
    return jnp.stack(rows, axis=0)


def nodal_terms(payload):
    basis_x = line_basis(payload[5])
    basis_y = line_basis(payload[6])
    basis_z = line_basis(payload[7])
    nodal_shape = (basis_x[:, None, None, :] * basis_y[None, :, None, :]) * basis_z[None, None, :, :]
    return (payload[0:5][:, None, :] * nodal_shape.reshape(64, -1)[None, :, :]).reshape(320, -1)


def scaled_derivs(values):
    return [GSCALE * derivative(values, d) for d in range(3)]


def state_traces(values, maps, lower_side, upper_side):
    return outer_traces((values, values, values), maps, lower_side, upper_side)


def rk_section(values, source, maps, lists):
    scaled = jax.vmap(scaled_derivs)(values)
    bottom, top_layer = jax.vmap(boundary)(values, lists)
    lower_side = jnp.roll(top_layer, 1, axis=0)
    upper_side = jnp.roll(bottom, -1, axis=0)
    outer_u = jax.vmap(state_traces)(values, maps, lower_side, upper_side)
    slopes = jax.vmap(gradient)(values, outer_u, scaled)
    slope_bottom, slope_top = jax.vmap(boundary)(slopes[2], lists)
    lower_q = jnp.roll(slope_top, 1, axis=0)
    upper_q = jnp.roll(slope_bottom, -1, axis=0)
    outer_q = jax.vmap(outer_traces)(slopes, maps, lower_q, upper_q)
    return jax.vmap(operator)(values, slopes, outer_u, outer_q, source)


def reference(state, neighbour_map, layer_lists, forces, positions, route, element_slot):
    count = N_SFC
    per_device = jnp.moveaxis(state.reshape(5, 4, 4, 4, count, E_DEV), 4, 0)
    maps = jnp.transpose(neighbour_map.reshape(6, count, E_DEV), (1, 0, 2))
    lists = jnp.transpose(layer_lists.reshape(2, count, PLANE), (1, 0, 2))
    payload = jnp.concatenate([forces, positions], axis=0)
    contrib = nodal_terms(payload)
    owner = (route[:, 0] * E_DEV + element_slot).astype(jnp.int32)
    summed = jax.ops.segment_sum(contrib.T, owner, num_segments=count * E_DEV).T
    source = jnp.moveaxis(summed.reshape(5, 4, 4, 4, count, E_DEV), 4, 0)
    change = rk_section(per_device, source, maps, lists)
    middle = per_device + TIME_STEP * change
    again = rk_section(middle, source, maps, lists)
    final = 0.5 * (per_device + (middle + TIME_STEP * again))
    return jnp.moveaxis(final, 0, 4).reshape(5, 4, 4, 4, count * E_DEV)
```

```python
import functools

import jax
import jax.numpy as jnp
import numpy as np
from jax import lax
from jax.experimental import pallas as pl
from jax.experimental.pallas import tpu as pltpu
from jax.sharding import PartitionSpec as P

NODE_POINTS = (-1.0, -0.4472135954999579, 0.4472135954999579, 1.0)
GSCALE = 2.0
HALF_LIFT = 6.0
ADVECT = (0.6, -0.4, 0.8)
VISCOSITY = 0.02
TIME_STEP = 0.04

VARS = 5
CAP = 8
FIELDS = 9
GROUP = FIELDS * CAP
COLS = VARS * 4 * 2
TILES = COLS * 4
VMEM_LIMIT = 24 * 1024 * 1024
F32 = jnp.float32
BF16 = jnp.bfloat16


def diff_table():
    factor = [
        float(np.prod([NODE_POINTS[a] - NODE_POINTS[k] for k in range(4) if k != a]))
        for a in range(4)
    ]
    table = np.zeros((4, 4))
    for a in range(4):
        for b in range(4):
            if a != b:
                table[a, b] = factor[a] / factor[b] / (NODE_POINTS[a] - NODE_POINTS[b])
            else:
                table[a, b] = sum(
                    (1.0 / (NODE_POINTS[a] - NODE_POINTS[k]) for k in range(4) if k != a)
                )
    return table


SLOPE = GSCALE * diff_table()


def line_operator(direction):
    a, nu = ADVECT[direction], VISCOSITY
    out = np.zeros((4, 8))
    for col in range(8):
        value = np.zeros(8)
        value[col] = 1.0
        u, (um, gm, up, gp) = value[:4], value[4:]
        q = SLOPE @ u
        q[0] -= HALF_LIFT * (um - u[0])
        q[3] += HALF_LIFT * (up - u[3])
        qm = gm + HALF_LIFT * (u[0] - um)
        qp = gp - HALF_LIFT * (u[3] - up)
        res = -SLOPE @ (a * u - nu * q)
        for node, normal, ou, oq in ((0, -1.0, um, qm), (3, 1.0, up, qp)):
            along = normal * a
            res[node] += -HALF_LIFT * (along - abs(along)) * (ou - u[node])
            res[node] += HALF_LIFT * nu * normal * (oq - q[node])
        out[:, col] = res
    return out


LINES = [line_operator(d) for d in range(3)]
UM, GM, UP, GP = 4, 5, 6, 7


def rolled(x, shift):
    return pltpu.roll(x, shift % 8, 0)


def lanes(x, shift):
    return pltpu.roll(x, shift % 128, 1)


def combine(pairs):
    total = None
    for coef, value in pairs:
        if isinstance(coef, (float, np.floating)):
            if coef == 0.0:
                continue
            term = value if coef == 1.0 else value * float(coef)
        else:
            term = value * coef
        total = term if total is None else total + term
    return total


class Masks:
    def __init__(self):
        sub = lax.broadcasted_iota(jnp.int32, (8, 128), 0)
        lane = lax.broadcasted_iota(jnp.int32, (8, 128), 1)
        self.h0 = sub < 4
        self.l0 = (sub & 2) == 0
        self.r0 = (sub & 1) == 0
        self.x_first = (lane & 15) == 0
        self.x_last = (lane & 15) == 15
        self.y_wrap = (self.h0 & (lane < 16)) | (~self.h0 & (lane >= 112))
        self.sign = jnp.where(self.h0, 1.0, -1.0).astype(F32)

    def by_half(self, low, high):
        if low == high:
            return float(low)
        return jnp.where(self.h0, float(low), float(high)).astype(F32)


def transpose4(tiles, mk):
    v0, v1, v2, v3 = tiles
    x0 = jnp.where(mk.r0, v0, rolled(v1, 1))
    x1 = jnp.where(mk.r0, rolled(v0, -1), v1)
    x2 = jnp.where(mk.r0, v2, rolled(v3, 1))
    x3 = jnp.where(mk.r0, rolled(v2, -1), v3)
    w0 = jnp.where(mk.l0, x0, rolled(x2, 2))
    w2 = jnp.where(mk.l0, rolled(x0, -2), x2)
    w1 = jnp.where(mk.l0, x1, rolled(x3, 2))
    w3 = jnp.where(mk.l0, rolled(x1, -2), x3)
    return w0, w1, w2, w3


def rows8(index):
    return pl.ds(pl.multiple_of(index * 8, 8), 8)


def x_line(u, mk, mat):
    g0 = combine((SLOPE[0, b], u[b]) for b in range(4))
    g3 = combine((SLOPE[3, b], u[b]) for b in range(4))

    def before(t):
        return jnp.where(mk.x_first, lanes(t, -15), lanes(t, 1))

    def after(t):
        return jnp.where(mk.x_last, lanes(t, 15), lanes(t, -1))

    um, gm, up, gp = before(u[3]), before(g3), after(u[0]), after(g0)
    terms = list(u) + [um, gm, up, gp]
    return [combine((mat[a, c], terms[c]) for c in range(8)) for a in range(4)]


def y_coefs(mk, mat):
    out = []
    for jj in range(2):
        o = 3 - jj
        row = [mk.by_half(mat[jj, b], mat[o, 3 - b]) for b in range(4)]
        row.append(mk.by_half(mat[jj, UM], mat[o, UP]))
        row.append(mk.by_half(mat[jj, UP], mat[o, UM]))
        row.append(mk.by_half(mat[jj, GM], mat[o, GP]))
        out.append(row)
    return out


def y_line(u0, u1, mk, coefs):
    r0, r1 = rolled(u0, 4), rolled(u1, 4)
    g = combine(((SLOPE[0, 0], u0), (SLOPE[0, 1], u1), (SLOPE[0, 2], r1), (SLOPE[0, 3], r0)))
    g = rolled(g * mk.sign, 4)

    def outer(t):
        near = jnp.where(mk.h0, lanes(t, 16), lanes(t, -16))
        far = jnp.where(mk.r0, rolled(near, -1), rolled(near, 1))
        return jnp.where(mk.y_wrap, far, near)

    n, gn = outer(r0), outer(g)
    nr = rolled(n, 4)
    return [
        combine(zip(coefs[0], (u0, u1, r1, r0, n, nr, gn))),
        combine(zip(coefs[1][:6], (u0, u1, r1, r0, n, nr))),
    ]


def z_line(u, hu, hg, mk, mat):
    g0 = combine((SLOPE[0, b], u[b]) for b in range(4))
    g3 = combine((SLOPE[3, b], u[b]) for b in range(4))
    um = jnp.where(mk.l0, hu, rolled(u[3], 2))
    gm = jnp.where(mk.l0, hg, rolled(g3, 2))
    up = jnp.where(mk.l0, rolled(u[0], -2), hu)
    gp = jnp.where(mk.l0, rolled(g0, -2), hg)
    terms = list(u) + [um, gm, up, gp]
    return [combine((mat[a, c], terms[c]) for c in range(8)) for a in range(4)]


def apply_operator(src, dst, hu, hg, mk, scale, ident):
    mats = [scale * m for m in LINES]
    mats[2][:, :4] += ident * np.eye(4)
    coefs = y_coefs(mk, mats[1])

    def per_variable(v, carry):
        col = v * 8
        for c in range(8):
            u = [src[rows8((col + c) * 4 + k), :] for k in range(4)]
            new = z_line(u, hu[rows8(col + c), :], hg[rows8(col + c), :], mk, mats[2])
            for k in range(4):
                dst[rows8((col + c) * 4 + k), :] = new[k]
        for i in range(4):
            for k in range(4):
                at = [rows8((col + 2 * i + jj) * 4 + k) for jj in range(2)]
                new = y_line(src[at[0], :], src[at[1], :], mk, coefs)
                for jj in range(2):
                    dst[at[jj], :] += new[jj]
        for jj in range(2):
            for k in range(4):
                at = [rows8((col + 2 * i + jj) * 4 + k) for i in range(4)]
                new = x_line([src[a, :] for a in at], mk, mats[0])
                for i in range(4):
                    dst[at[i], :] += new[i]
        return carry

    lax.fori_loop(0, VARS, per_variable, 0)


def split2(x):
    hi = x.astype(BF16)
    return hi, (x - hi.astype(F32)).astype(BF16)


def nt_dot(a, b):
    return lax.dot_general(a, b, (((1,), (1,)), ((), ())), preferred_element_type=F32)


def fill_order(lists_ref, order):
    ids = lax.broadcasted_iota(jnp.int32, (512, 128), 0)
    for t in range(4):
        row = lists_ref[t // 2 : t // 2 + 1, (t % 2) * 128 : (t % 2) * 128 + 128]
        order[:, t * 128 : t * 128 + 128] = jnp.where(ids == row, 1.0, 0.0).astype(BF16)


def pack_points(route, payload, pack_ref):
    dest = lax.broadcasted_iota(jnp.int32, (128, 128), 0)
    lane = lax.broadcasted_iota(jnp.int32, (128, 128), 1)
    slot = lax.broadcasted_iota(jnp.int32, (8, 128), 0).astype(F32)
    to_device = [jnp.where(dest == route[:, t * 128 : t * 128 + 128], 1.0, 0.0) for t in range(4)]
    stacked = jnp.concatenate(to_device, axis=0).astype(BF16)
    before = jnp.where(dest < lane, 1.0, 0.0).astype(BF16)
    inside = jnp.dot(stacked, before, preferred_element_type=F32)
    totals = jnp.dot(stacked, jnp.ones((128, 128), BF16), preferred_element_type=F32)
    base = jnp.zeros((128, 128), F32)
    out = jnp.zeros((128, 128), F32)
    for t in range(4):
        here = slice(t * 128, t * 128 + 128)
        count = inside[here] + base
        base = base + totals[here]
        within = jnp.sum(count * to_device[t], axis=0, keepdims=True)
        chosen = slot == within
        rows = [jnp.where(chosen, p[:, here], 0.0) for p in payload]
        rows.append(jnp.zeros((128 - GROUP, 128), F32))
        rest = jnp.concatenate(rows, axis=0)
        for _ in range(3):
            part = rest.astype(BF16)
            rest = rest - part.astype(F32)
            out = out + nt_dot(stacked[here], part)
    low = pltpu.roll(pltpu.roll(out, 1, 0), GROUP, 1)
    up = pltpu.roll(pltpu.roll(out, 127, 0), 2 * GROUP - 128, 1)
    pack_ref[pl.ds(0, 128, stride=2), :] = jnp.where(lane < GROUP, out, low)
    pack_ref[pl.ds(1, 128, stride=2), :] = jnp.where(lane < 2 * GROUP - 128, low, up)


def entry_kernel(
    par_ref, route_ref, slot_ref, forces_ref, coords_ref, lists_ref, state_ref,
    pack_ref, u_ref, first_ref, second_ref, inv_ref, order, lhs,
):
    mk = Masks()
    payload = [forces_ref[f : f + 1, :] for f in range(5)]
    payload += [coords_ref[f : f + 1, :] for f in range(3)]
    payload.append(slot_ref[...].astype(F32))
    pack_points(route_ref[...], payload, pack_ref)

    fill_order(lists_ref, order)
    for vi in range(VARS * 4):
        x = jnp.concatenate([state_ref[vi * 4 + j] for j in (0, 3, 1, 2)], axis=0)
        hi, lo = split2(x)
        lhs[vi * 16 : vi * 16 + 16, :] = hi
        lhs[320 + vi * 16 : 336 + vi * 16, :] = lo
    res = jnp.dot(lhs[...], order[...], preferred_element_type=F32)
    val = res[:320] + res[320:]
    for g in range(COLS):
        tiles = [val[g * 8 : g * 8 + 8, t * 128 : t * 128 + 128] for t in range(4)]
        for k, tile in enumerate(transpose4(tiles, mk)):
            u_ref[(g * 4 + k) * 8 : (g * 4 + k) * 8 + 8, :] = tile

    place = lax.broadcasted_iota(jnp.int32, (16, 512), 1)
    digit = lax.broadcasted_iota(jnp.int32, (16, 512), 0)
    digits = jnp.where(digit == 0, place >> 4, place & 15).astype(F32).astype(BF16)
    where = nt_dot(digits, order[...])
    inv = where[0:1, :] * 16.0 + where[1:2, :]
    inv = jnp.concatenate([inv[:, t * 128 : t * 128 + 128] for t in range(4)] * 2, axis=0)
    inv_ref[...] = inv
    first_ref[2 * COLS * 8 :, :] = inv
    second_ref[2 * COLS * 8 :, :] = inv

    even = jnp.full((8, 128), par_ref[0], jnp.int32) == 0
    mat = TIME_STEP * LINES[2]
    top, bottom = np.eye(4)[3], np.eye(4)[0]

    def per_variable(v, carry):
        for c in range(8):
            col = v * 8 + c
            u = [u_ref[rows8(col * 4 + k), :] for k in range(4)]
            g0 = combine((SLOPE[0, b], u[b]) for b in range(4))
            g3 = combine((SLOPE[3, b], u[b]) for b in range(4))
            um, gm = rolled(u[3], 2), rolled(g3, 2)
            up, gp = rolled(u[0], -2), rolled(g0, -2)
            for part, (f_top, f_bottom, a_top, a_bottom) in enumerate(
                ((top, bottom, u[3], u[0]), (SLOPE[3], SLOPE[0], g3, g0))
            ):
                own = [u[0], u[1], u[2], u[3]]
                b_top = combine(
                    list(zip(f_top + f_top @ mat[:, :4], own))
                    + [(f_top @ mat[:, UM], um), (f_top @ mat[:, GM], gm)]
                )
                b_bottom = combine(
                    list(zip(f_bottom + f_bottom @ mat[:, :4], own))
                    + [(f_bottom @ mat[:, UP], up), (f_bottom @ mat[:, GP], gp)]
                )
                to_upper = jnp.where(mk.l0, rolled(a_top, -2), b_top)
                to_lower = jnp.where(mk.l0, b_bottom, rolled(a_bottom, 2))
                at = rows8(part * COLS + col)
                first_ref[at, :] = jnp.where(even, to_upper, to_lower)
                second_ref[at, :] = jnp.where(even, to_lower, to_upper)
        return carry

    lax.fori_loop(0, VARS, per_variable, 0)


def state_kernel(
    par_ref, u_ref, first_ref, second_ref, base_ref, au, ag, hu, hg, m0
):
    mk = Masks()
    even = jnp.full((8, 128), par_ref[0], jnp.int32) == 0
    mat = TIME_STEP * LINES[2]
    top, bottom = np.eye(4)[3], np.eye(4)[0]
    from_second = mk.l0 == even

    def unpack(col, carry):
        for part, (a, h) in enumerate(((au, hu), (ag, hg))):
            one = first_ref[rows8(part * COLS + col), :]
            two = second_ref[rows8(part * COLS + col), :]
            a[rows8(col), :] = jnp.where(from_second, two, one)
            rest = jnp.where(from_second, one, two)
            h[rows8(col), :] = jnp.where(mk.l0, rolled(rest, -2), rolled(rest, 2))
        return carry

    lax.fori_loop(0, COLS, unpack, 0, unroll=8)
    apply_operator(u_ref, m0, au, ag, mk, TIME_STEP, 1.0)

    x_mat, coefs = TIME_STEP * LINES[0], y_coefs(mk, TIME_STEP * LINES[1])

    def halo(v, carry):
        for c in range(8):
            col = v * 8 + c
            u = [u_ref[rows8(col * 4 + k), :] for k in range(4)]
            g0 = combine((SLOPE[0, b], u[b]) for b in range(4))
            g3 = combine((SLOPE[3, b], u[b]) for b in range(4))
            for h, f_low, f_high in ((hu, top, bottom), (hg, SLOPE[3], SLOPE[0])):
                low = combine(((f_low @ mat[:, UP], u[0]), (f_low @ mat[:, GP], g0)))
                high = combine(((f_high @ mat[:, UM], u[3]), (f_high @ mat[:, GM], g3)))
                h[rows8(col), :] += jnp.where(mk.l0, low, high)
        for a, h in ((au, hu), (ag, hg)):
            for i in range(4):
                at = [rows8(v * 8 + 2 * i + jj) for jj in range(2)]
                new = y_line(a[at[0], :], a[at[1], :], mk, coefs)
                for jj in range(2):
                    h[at[jj], :] += new[jj]
            for jj in range(2):
                at = [rows8(v * 8 + 2 * i + jj) for i in range(4)]
                new = x_line([a[r, :] for r in at], mk, x_mat)
                for i in range(4):
                    h[at[i], :] += new[i]
        return carry

    lax.fori_loop(0, VARS, halo, 0)
    apply_operator(m0, base_ref, hu, hg, mk, 0.5 * TIME_STEP, 0.5)

    def finish(n, carry):
        base_ref[rows8(n), :] += 0.5 * u_ref[rows8(n), :]
        return carry

    lax.fori_loop(0, TILES, finish, 0, unroll=16)


def line_basis(coords):
    rows = []
    for a in range(4):
        term = None
        for k in range(4):
            if k != a:
                factor = (coords - NODE_POINTS[k]) * (1.0 / (NODE_POINTS[a] - NODE_POINTS[k]))
                term = factor if term is None else term * factor
        rows.append(term)
    return rows


def place_of(slots, table, row):
    number = slots.astype(jnp.int32)
    inner, outer = number & 127, number >> 7
    found = jnp.zeros((8, 128), F32)
    for t in range(4):
        line = jnp.broadcast_to(table[row + t : row + t + 1, :], (8, 128))
        found = jnp.where(outer == t, jnp.take_along_axis(line, inner, axis=1), found)
    return found.astype(jnp.int32)


def source_kernel(
    par_ref, pts_ref, inv_ref, first_ref, second_ref, base_ref, lists_ref, out_ref,
    order, hot, hot_low, hot_up, lhs, lhs_low, lhs_up, grid, strength, su, sg, s_ref, new_ref,
):
    mk = Masks()
    even = jnp.full((8, 128), par_ref[0], jnp.int32) == 0
    halves = [pts_ref[pl.ds(h, 128, stride=2), :].T for h in range(2)]
    data = jnp.concatenate(halves, axis=0)
    tables = [
        inv_ref[...],
        jnp.where(even, second_ref[...], first_ref[...]),
        jnp.where(even, first_ref[...], second_ref[...]),
    ]
    ids = lax.broadcasted_iota(jnp.int32, (512, 128), 0)
    for group in range(3):
        field = [data[group * GROUP + f * 8 : group * GROUP + f * 8 + 8] for f in range(FIELDS)]
        forces = field[:5]
        bx, by, bz = [line_basis(field[5 + d]) for d in range(3)]
        place = place_of(field[8], tables[group], 0)
        if group == 0:
            columns = [forces[v] * bx[i] for v in range(VARS) for i in range(4)]
            nodes = [by[j] * bz[k] for j in (0, 3, 1, 2) for k in range(4)]
            goal, matrix, size, shift = hot, lhs, 512, 0
        else:
            node = 3 if group == 1 else 0
            slope = combine((SLOPE[node, b], bz[b]) for b in range(4))
            columns = [forces[v] * bz[node] for v in range(VARS)]
            columns += [forces[v] * slope for v in range(VARS)]
            nodes = [by[j] * bx[i] for j in (0, 3, 1, 2) for i in range(4)]
            goal, matrix, size = (hot_low, lhs_low, 256) if group == 1 else (hot_up, lhs_up, 256)
            shift = 256 if group == 1 else 0
        for n, tile in enumerate(nodes):
            grid[group, n * 8 : n * 8 + 8, :] = tile
        for n, tile in enumerate(columns):
            strength[group, n * 8 : n * 8 + 8, :] = tile
        count = len(columns) * 16
        for c in range(CAP):
            here = slice(c * 128, c * 128 + 128)
            node_rows = grid[group, pl.ds(c, 16, stride=8), :]
            for n in range(len(columns)):
                row = strength[group, n * 8 + c : n * 8 + c + 1, :]
                hi, lo = split2(node_rows * row)
                matrix[n * 16 : n * 16 + 16, here] = hi
                matrix[count + n * 16 : count + n * 16 + 16, here] = lo
            found = place[c : c + 1, :] - shift
            goal[:, here] = jnp.where(ids[:size] == found, 1.0, 0.0).astype(BF16)

    res = nt_dot(lhs[...], hot[...])
    val = res[:320] + res[320:]
    for g in range(COLS):
        tiles = [val[g * 8 : g * 8 + 8, t * 128 : t * 128 + 128] for t in range(4)]
        for k, tile in enumerate(transpose4(tiles, mk)):
            s_ref[(g * 4 + k) * 8 : (g * 4 + k) * 8 + 8, :] = tile
    res_low = nt_dot(lhs_low[...], hot_low[...])
    res_up = nt_dot(lhs_up[...], hot_up[...])
    val_low, val_up = res_low[:160] + res_low[160:], res_up[:160] + res_up[160:]
    for part, goal in ((0, su), (1, sg)):
        for v in range(VARS):
            for jj in range(2):
                at = (part * VARS + v) * 16 + jj * 8
                tiles = [
                    val[at : at + 8, t * 128 : t * 128 + 128]
                    for val in (val_low, val_up)
                    for t in range(2)
                ]
                for i, tile in enumerate(transpose4(tiles, mk)):
                    col = (v * 4 + i) * 2 + jj
                    goal[col * 8 : col * 8 + 8, :] = tile

    apply_operator(s_ref, new_ref, su, sg, mk, 0.5 * TIME_STEP * TIME_STEP, TIME_STEP)
    fill_order(lists_ref, order)
    for vi in range(VARS * 4):
        for jj in range(2):
            g = vi * 2 + jj
            at = [slice((g * 4 + k) * 8, (g * 4 + k) * 8 + 8) for k in range(4)]
            tiles = transpose4([new_ref[a, :] + base_ref[a, :] for a in at], mk)
            for t in range(4):
                new_ref[(g * 4 + t) * 8 : (g * 4 + t) * 8 + 8, :] = tiles[t]
        for t in range(4):
            x = jnp.concatenate(
                [new_ref[((vi * 2 + jj) * 4 + t) * 8 : ((vi * 2 + jj) * 4 + t) * 8 + 8, :] for jj in range(2)],
                axis=0,
            )
            hi, lo = split2(x)
            lhs[vi * 16 : vi * 16 + 16, t * 128 : t * 128 + 128] = hi
            lhs[320 + vi * 16 : 336 + vi * 16, t * 128 : t * 128 + 128] = lo
    res = nt_dot(lhs[:, :512], order[...])
    val = res[:320] + res[320:]
    for vi in range(VARS * 4):
        for n, j in enumerate((0, 3, 1, 2)):
            out_ref[vi * 4 + j] = val[vi * 16 + n * 4 : vi * 16 + n * 4 + 4, :]


def call(kernel, outs, scratch, specs):
    return pl.pallas_call(
        kernel,
        out_shape=outs,
        in_specs=specs,
        out_specs=jax.tree.map(lambda _: pl.BlockSpec(memory_space=pltpu.VMEM), outs),
        scratch_shapes=scratch,
        compiler_params=pltpu.CompilerParams(vmem_limit_bytes=VMEM_LIMIT),
    )


def tile_array(count):
    return jax.ShapeDtypeStruct((count * 8, 128), F32)


SMEM = pl.BlockSpec(memory_space=pltpu.SMEM)
VMEM = pl.BlockSpec(memory_space=pltpu.VMEM)


def entry_call(par, route, slots, forces, coords, lists, state):
    halo = tile_array(2 * COLS + 1)
    return call(
        entry_kernel,
        (jax.ShapeDtypeStruct((256, 128), F32), tile_array(TILES), halo, halo, tile_array(1)),
        [pltpu.VMEM((512, 512), BF16), pltpu.VMEM((640, 512), BF16)],
        [SMEM] + [VMEM] * 6,
    )(par, route, slots, forces, coords, lists, state)


def state_call(par, u, first, second):
    cols = pltpu.VMEM((COLS * 8, 128), F32)
    return call(
        state_kernel,
        tile_array(TILES),
        [cols, cols, cols, cols, pltpu.VMEM((TILES * 8, 128), F32)],
        [SMEM] + [VMEM] * 3,
    )(par, u, first, second)


def source_call(par, pts, inv, first, second, base, lists):
    cols = pltpu.VMEM((COLS * 8, 128), F32)
    field = pltpu.VMEM((TILES * 8, 128), F32)
    return call(
        source_kernel,
        jax.ShapeDtypeStruct((VARS * 16, 4, 512), F32),
        [
            pltpu.VMEM((512, 512), BF16),
            pltpu.VMEM((512, 1024), BF16),
            pltpu.VMEM((256, 1024), BF16),
            pltpu.VMEM((256, 1024), BF16),
            pltpu.VMEM((640, 1024), BF16),
            pltpu.VMEM((320, 1024), BF16),
            pltpu.VMEM((320, 1024), BF16),
            pltpu.VMEM((3, 128, 128), F32),
            pltpu.VMEM((3, 160, 128), F32),
            cols,
            cols,
            field,
            field,
        ],
        [SMEM] + [VMEM] * 6,
    )(par, pts, inv, first, second, base, lists)


def on_device(state, neighbour_map, layer_lists, forces, positions, route, element_slot):
    count = lax.axis_size("sfc")
    inside = [(d, d ^ 1) for d in range(count)]
    across = [(d, (d + 1) % count if d % 2 else (d - 1) % count) for d in range(count)]
    par = (lax.axis_index("sfc") & 1).astype(jnp.int32).reshape(1)
    pack, u, first, second, inv = entry_call(
        par,
        route.reshape(1, -1),
        element_slot.reshape(1, -1),
        forces,
        positions,
        layer_lists,
        state.reshape(VARS * 16, 4, -1),
    )
    first = lax.ppermute(first, "sfc", inside)
    second = lax.ppermute(second, "sfc", across)
    pts = lax.all_to_all(pack, "sfc", split_axis=0, concat_axis=0, tiled=True)
    base = state_call(par, u, first, second)
    tail = slice(2 * COLS * 8, None)
    out = source_call(par, pts, inv, first[tail], second[tail], base, layer_lists)
    return out.reshape(state.shape)


def solution(mesh):
    in_specs = (
        P(None, None, None, None, "sfc"),
        P(None, "sfc"),
        P(None, "sfc"),
        P(None, "sfc"),
        P(None, "sfc"),
        P("sfc", None),
        P("sfc"),
    )
    out_specs = P(None, None, None, None, "sfc")
    return jax.shard_map(
        on_device, mesh=mesh, in_specs=in_specs, out_specs=out_specs, check_vma=False
    )
```

```python
import functools

import jax
import jax.numpy as jnp
import numpy as np
from jax import lax
from jax.experimental import pallas as pl
from jax.experimental.pallas import tpu as pltpu
from jax.sharding import PartitionSpec as P

NODE_POINTS = (-1.0, -0.4472135954999579, 0.4472135954999579, 1.0)
GSCALE = 2.0
HALF_LIFT = 6.0
ADVECT = (0.6, -0.4, 0.8)
VISCOSITY = 0.02
TIME_STEP = 0.04

VARS = 5
CAP = 8
FIELDS = 9
GROUP = FIELDS * CAP
COLS = VARS * 4 * 2
TILES = COLS * 4
VMEM_LIMIT = 24 * 1024 * 1024
F32 = jnp.float32
BF16 = jnp.bfloat16


def diff_table():
    factor = [
        float(np.prod([NODE_POINTS[a] - NODE_POINTS[k] for k in range(4) if k != a]))
        for a in range(4)
    ]
    table = np.zeros((4, 4))
    for a in range(4):
        for b in range(4):
            if a != b:
                table[a, b] = factor[a] / factor[b] / (NODE_POINTS[a] - NODE_POINTS[b])
            else:
                table[a, b] = sum(
                    (1.0 / (NODE_POINTS[a] - NODE_POINTS[k]) for k in range(4) if k != a)
                )
    return table


SLOPE = GSCALE * diff_table()


def line_operator(direction):
    a, nu = ADVECT[direction], VISCOSITY
    out = np.zeros((4, 8))
    for col in range(8):
        value = np.zeros(8)
        value[col] = 1.0
        u, (um, gm, up, gp) = value[:4], value[4:]
        q = SLOPE @ u
        q[0] -= HALF_LIFT * (um - u[0])
        q[3] += HALF_LIFT * (up - u[3])
        qm = gm + HALF_LIFT * (u[0] - um)
        qp = gp - HALF_LIFT * (u[3] - up)
        res = -SLOPE @ (a * u - nu * q)
        for node, normal, ou, oq in ((0, -1.0, um, qm), (3, 1.0, up, qp)):
            along = normal * a
            res[node] += -HALF_LIFT * (along - abs(along)) * (ou - u[node])
            res[node] += HALF_LIFT * nu * normal * (oq - q[node])
        out[:, col] = res
    return out


LINES = [line_operator(d) for d in range(3)]
UM, GM, UP, GP = 4, 5, 6, 7


def rolled(x, shift):
    return pltpu.roll(x, shift % 8, 0)


def lanes(x, shift):
    return pltpu.roll(x, shift % 128, 1)


def combine(pairs):
    total = None
    for coef, value in pairs:
        if isinstance(coef, (float, np.floating)):
            if coef == 0.0:
                continue
            term = value if coef == 1.0 else value * float(coef)
        else:
            term = value * coef
        total = term if total is None else total + term
    return total


class Masks:
    def __init__(self):
        sub = lax.broadcasted_iota(jnp.int32, (8, 128), 0)
        lane = lax.broadcasted_iota(jnp.int32, (8, 128), 1)
        self.h0 = sub < 4
        self.l0 = (sub & 2) == 0
        self.r0 = (sub & 1) == 0
        self.x_first = (lane & 15) == 0
        self.x_last = (lane & 15) == 15
        self.y_wrap = (self.h0 & (lane < 16)) | (~self.h0 & (lane >= 112))
        self.sign = jnp.where(self.h0, 1.0, -1.0).astype(F32)

    def by_half(self, low, high):
        if low == high:
            return float(low)
        return jnp.where(self.h0, float(low), float(high)).astype(F32)


def transpose4(tiles, mk):
    v0, v1, v2, v3 = tiles
    x0 = jnp.where(mk.r0, v0, rolled(v1, 1))
    x1 = jnp.where(mk.r0, rolled(v0, -1), v1)
    x2 = jnp.where(mk.r0, v2, rolled(v3, 1))
    x3 = jnp.where(mk.r0, rolled(v2, -1), v3)
    w0 = jnp.where(mk.l0, x0, rolled(x2, 2))
    w2 = jnp.where(mk.l0, rolled(x0, -2), x2)
    w1 = jnp.where(mk.l0, x1, rolled(x3, 2))
    w3 = jnp.where(mk.l0, rolled(x1, -2), x3)
    return w0, w1, w2, w3


def rows8(index):
    return pl.ds(pl.multiple_of(index * 8, 8), 8)


def x_line(u, mk, mat):
    g0 = combine((SLOPE[0, b], u[b]) for b in range(4))
    g3 = combine((SLOPE[3, b], u[b]) for b in range(4))

    def before(t):
        return jnp.where(mk.x_first, lanes(t, -15), lanes(t, 1))

    def after(t):
        return jnp.where(mk.x_last, lanes(t, 15), lanes(t, -1))

    um, gm, up, gp = before(u[3]), before(g3), after(u[0]), after(g0)
    terms = list(u) + [um, gm, up, gp]
    return [combine((mat[a, c], terms[c]) for c in range(8)) for a in range(4)]


def y_coefs(mk, mat):
    out = []
    for jj in range(2):
        o = 3 - jj
        row = [mk.by_half(mat[jj, b], mat[o, 3 - b]) for b in range(4)]
        row.append(mk.by_half(mat[jj, UM], mat[o, UP]))
        row.append(mk.by_half(mat[jj, UP], mat[o, UM]))
        row.append(mk.by_half(mat[jj, GM], mat[o, GP]))
        out.append(row)
    return out


def y_line(u0, u1, mk, coefs):
    r0, r1 = rolled(u0, 4), rolled(u1, 4)
    g = combine(((SLOPE[0, 0], u0), (SLOPE[0, 1], u1), (SLOPE[0, 2], r1), (SLOPE[0, 3], r0)))
    g = rolled(g * mk.sign, 4)

    def outer(t):
        near = jnp.where(mk.h0, lanes(t, 16), lanes(t, -16))
        far = jnp.where(mk.r0, rolled(near, -1), rolled(near, 1))
        return jnp.where(mk.y_wrap, far, near)

    n, gn = outer(r0), outer(g)
    nr = rolled(n, 4)
    return [
        combine(zip(coefs[0], (u0, u1, r1, r0, n, nr, gn))),
        combine(zip(coefs[1][:6], (u0, u1, r1, r0, n, nr))),
    ]


def z_line(u, hu, hg, mk, mat):
    g0 = combine((SLOPE[0, b], u[b]) for b in range(4))
    g3 = combine((SLOPE[3, b], u[b]) for b in range(4))
    um = jnp.where(mk.l0, hu, rolled(u[3], 2))
    gm = jnp.where(mk.l0, hg, rolled(g3, 2))
    up = jnp.where(mk.l0, rolled(u[0], -2), hu)
    gp = jnp.where(mk.l0, rolled(g0, -2), hg)
    terms = list(u) + [um, gm, up, gp]
    return [combine((mat[a, c], terms[c]) for c in range(8)) for a in range(4)]


def apply_operator(src, dst, hu, hg, mk, scale, ident):
    mats = [scale * m for m in LINES]
    mats[2][:, :4] += ident * np.eye(4)
    coefs = y_coefs(mk, mats[1])

    def per_variable(v, carry):
        col = v * 8
        for c in range(8):
            u = [src[rows8((col + c) * 4 + k), :] for k in range(4)]
            new = z_line(u, hu[rows8(col + c), :], hg[rows8(col + c), :], mk, mats[2])
            for k in range(4):
                dst[rows8((col + c) * 4 + k), :] = new[k]
        for i in range(4):
            for k in range(4):
                at = [rows8((col + 2 * i + jj) * 4 + k) for jj in range(2)]
                new = y_line(src[at[0], :], src[at[1], :], mk, coefs)
                for jj in range(2):
                    dst[at[jj], :] += new[jj]
        for jj in range(2):
            for k in range(4):
                at = [rows8((col + 2 * i + jj) * 4 + k) for i in range(4)]
                new = x_line([src[a, :] for a in at], mk, mats[0])
                for i in range(4):
                    dst[at[i], :] += new[i]
        return carry

    lax.fori_loop(0, VARS, per_variable, 0)


def split2(x):
    hi = x.astype(BF16)
    return hi, (x - hi.astype(F32)).astype(BF16)


def nt_dot(a, b):
    return lax.dot_general(a, b, (((1,), (1,)), ((), ())), preferred_element_type=F32)


def fill_order(rows, order):
    ids = lax.broadcasted_iota(jnp.int32, (512, 128), 0)
    for t in range(4):
        order[:, t * 128 : t * 128 + 128] = jnp.where(ids == rows[t], 1.0, 0.0).astype(BF16)


def pack_points(route, payload, pack_ref):
    dest = lax.broadcasted_iota(jnp.int32, (128, 128), 0)
    lane = lax.broadcasted_iota(jnp.int32, (128, 128), 1)
    slot = lax.broadcasted_iota(jnp.int32, (8, 128), 0).astype(F32)
    to_device = [jnp.where(dest == route[:, t * 128 : t * 128 + 128], 1.0, 0.0) for t in range(4)]
    stacked = jnp.concatenate(to_device, axis=0).astype(BF16)
    before = jnp.where(dest < lane, 1.0, 0.0).astype(BF16)
    inside = jnp.dot(stacked, before, preferred_element_type=F32)
    totals = jnp.dot(stacked, jnp.ones((128, 128), BF16), preferred_element_type=F32)
    base = jnp.zeros((128, 128), F32)
    out = jnp.zeros((128, 128), F32)
    for t in range(4):
        here = slice(t * 128, t * 128 + 128)
        count = inside[here] + base
        base = base + totals[here]
        within = jnp.sum(count * to_device[t], axis=0, keepdims=True)
        chosen = slot == within
        rows = [jnp.where(chosen, p[:, here], 0.0) for p in payload]
        rows.append(jnp.zeros((128 - GROUP, 128), F32))
        rest = jnp.concatenate(rows, axis=0)
        for _ in range(3):
            part = rest.astype(BF16)
            rest = rest - part.astype(F32)
            out = out + nt_dot(stacked[here], part)
    low = pltpu.roll(pltpu.roll(out, 1, 0), GROUP, 1)
    up = pltpu.roll(pltpu.roll(out, 127, 0), 2 * GROUP - 128, 1)
    pack_ref[pl.ds(0, 128, stride=2), :] = jnp.where(lane < GROUP, out, low)
    pack_ref[pl.ds(1, 128, stride=2), :] = jnp.where(lane < 2 * GROUP - 128, low, up)


def entry_kernel(
    par_ref, route_hbm, slot_hbm, forces_hbm, coords_hbm, lists_hbm, state_hbm,
    pack_ref, u_ref, first_ref, second_ref, inv_ref,
    route_ref, slot_ref, forces_ref, coords_ref, lists_ref, state_ref, order, lhs, sems,
):
    sources = (route_hbm, slot_hbm, forces_hbm, coords_hbm, lists_hbm, state_hbm)
    targets = (route_ref, slot_ref, forces_ref, coords_ref, lists_ref, state_ref)
    copies = [
        pltpu.make_async_copy(a, b, sems.at[n]) for n, (a, b) in enumerate(zip(sources, targets))
    ]
    for copy in copies:
        copy.start()
    mk = Masks()
    for copy in copies[:5]:
        copy.wait()
    payload = [forces_ref[f : f + 1, :] for f in range(5)]
    payload += [coords_ref[f : f + 1, :] for f in range(3)]
    payload.append(slot_ref[...].astype(F32))
    pack_points(route_ref[...], payload, pack_ref)

    rows = [
        lists_ref[t // 2 : t // 2 + 1, (t % 2) * 128 : (t % 2) * 128 + 128] for t in range(4)
    ]
    fill_order(rows, order)
    copies[5].wait()
    for vi in range(VARS * 4):
        x = jnp.concatenate([state_ref[vi * 4 + j] for j in (0, 3, 1, 2)], axis=0)
        hi, lo = split2(x)
        lhs[vi * 16 : vi * 16 + 16, :] = hi
        lhs[320 + vi * 16 : 336 + vi * 16, :] = lo
    res = jnp.dot(lhs[...], order[...], preferred_element_type=F32)
    val = res[:320] + res[320:]
    for g in range(COLS):
        tiles = [val[g * 8 : g * 8 + 8, t * 128 : t * 128 + 128] for t in range(4)]
        for k, tile in enumerate(transpose4(tiles, mk)):
            u_ref[(g * 4 + k) * 8 : (g * 4 + k) * 8 + 8, :] = tile

    place = lax.broadcasted_iota(jnp.int32, (16, 512), 1)
    digit = lax.broadcasted_iota(jnp.int32, (16, 512), 0)
    digits = jnp.where(digit == 0, place >> 4, place & 15).astype(F32).astype(BF16)
    where = nt_dot(digits, order[...])
    inv = where[0:1, :] * 16.0 + where[1:2, :]
    inv = [inv[:, t * 128 : t * 128 + 128] for t in range(4)]
    inv = jnp.concatenate(inv + [row.astype(F32) for row in rows], axis=0)
    inv_ref[...] = inv
    first_ref[2 * COLS * 8 :, :] = inv
    second_ref[2 * COLS * 8 :, :] = inv

    even = jnp.full((8, 128), par_ref[0], jnp.int32) == 0
    mat = TIME_STEP * LINES[2]
    top, bottom = np.eye(4)[3], np.eye(4)[0]

    def per_variable(v, carry):
        for c in range(8):
            col = v * 8 + c
            u = [u_ref[rows8(col * 4 + k), :] for k in range(4)]
            g0 = combine((SLOPE[0, b], u[b]) for b in range(4))
            g3 = combine((SLOPE[3, b], u[b]) for b in range(4))
            um, gm = rolled(u[3], 2), rolled(g3, 2)
            up, gp = rolled(u[0], -2), rolled(g0, -2)
            for part, (f_top, f_bottom, a_top, a_bottom) in enumerate(
                ((top, bottom, u[3], u[0]), (SLOPE[3], SLOPE[0], g3, g0))
            ):
                own = [u[0], u[1], u[2], u[3]]
                b_top = combine(
                    list(zip(f_top + f_top @ mat[:, :4], own))
                    + [(f_top @ mat[:, UM], um), (f_top @ mat[:, GM], gm)]
                )
                b_bottom = combine(
                    list(zip(f_bottom + f_bottom @ mat[:, :4], own))
                    + [(f_bottom @ mat[:, UP], up), (f_bottom @ mat[:, GP], gp)]
                )
                to_upper = jnp.where(mk.l0, rolled(a_top, -2), b_top)
                to_lower = jnp.where(mk.l0, b_bottom, rolled(a_bottom, 2))
                at = rows8(part * COLS + col)
                first_ref[at, :] = jnp.where(even, to_upper, to_lower)
                second_ref[at, :] = jnp.where(even, to_lower, to_upper)
        return carry

    lax.fori_loop(0, VARS, per_variable, 0)


def state_kernel(
    par_ref, u_ref, first_ref, second_ref, base_ref, au, ag, hu, hg, m0
):
    mk = Masks()
    even = jnp.full((8, 128), par_ref[0], jnp.int32) == 0
    mat = TIME_STEP * LINES[2]
    top, bottom = np.eye(4)[3], np.eye(4)[0]
    from_second = mk.l0 == even

    def unpack(col, carry):
        for part, (a, h) in enumerate(((au, hu), (ag, hg))):
            one = first_ref[rows8(part * COLS + col), :]
            two = second_ref[rows8(part * COLS + col), :]
            a[rows8(col), :] = jnp.where(from_second, two, one)
            rest = jnp.where(from_second, one, two)
            h[rows8(col), :] = jnp.where(mk.l0, rolled(rest, -2), rolled(rest, 2))
        return carry

    lax.fori_loop(0, COLS, unpack, 0, unroll=8)
    apply_operator(u_ref, m0, au, ag, mk, TIME_STEP, 1.0)

    x_mat, coefs = TIME_STEP * LINES[0], y_coefs(mk, TIME_STEP * LINES[1])

    def halo(v, carry):
        for c in range(8):
            col = v * 8 + c
            u = [u_ref[rows8(col * 4 + k), :] for k in range(4)]
            g0 = combine((SLOPE[0, b], u[b]) for b in range(4))
            g3 = combine((SLOPE[3, b], u[b]) for b in range(4))
            for h, f_low, f_high in ((hu, top, bottom), (hg, SLOPE[3], SLOPE[0])):
                low = combine(((f_low @ mat[:, UP], u[0]), (f_low @ mat[:, GP], g0)))
                high = combine(((f_high @ mat[:, UM], u[3]), (f_high @ mat[:, GM], g3)))
                h[rows8(col), :] += jnp.where(mk.l0, low, high)
        for a, h in ((au, hu), (ag, hg)):
            for i in range(4):
                at = [rows8(v * 8 + 2 * i + jj) for jj in range(2)]
                new = y_line(a[at[0], :], a[at[1], :], mk, coefs)
                for jj in range(2):
                    h[at[jj], :] += new[jj]
            for jj in range(2):
                at = [rows8(v * 8 + 2 * i + jj) for i in range(4)]
                new = x_line([a[r, :] for r in at], mk, x_mat)
                for i in range(4):
                    h[at[i], :] += new[i]
        return carry

    lax.fori_loop(0, VARS, halo, 0)
    apply_operator(m0, base_ref, hu, hg, mk, 0.5 * TIME_STEP, 0.5)

    def finish(n, carry):
        base_ref[rows8(n), :] += 0.5 * u_ref[rows8(n), :]
        return carry

    lax.fori_loop(0, TILES, finish, 0, unroll=16)


def line_basis(coords):
    rows = []
    for a in range(4):
        term = None
        for k in range(4):
            if k != a:
                factor = (coords - NODE_POINTS[k]) * (1.0 / (NODE_POINTS[a] - NODE_POINTS[k]))
                term = factor if term is None else term * factor
        rows.append(term)
    return rows


def place_of(slots, table, row):
    number = slots.astype(jnp.int32)
    inner, outer = number & 127, number >> 7
    found = jnp.zeros((8, 128), F32)
    for t in range(4):
        line = jnp.broadcast_to(table[row + t : row + t + 1, :], (8, 128))
        found = jnp.where(outer == t, jnp.take_along_axis(line, inner, axis=1), found)
    return found.astype(jnp.int32)


def source_kernel(
    par_ref, pts_ref, inv_ref, first_ref, second_ref, base_ref, out_ref,
    order, hot, hot_low, hot_up, lhs, lhs_low, lhs_up, grid, strength, su, sg, s_ref, new_ref,
):
    mk = Masks()
    even = jnp.full((8, 128), par_ref[0], jnp.int32) == 0
    halves = [pts_ref[pl.ds(h, 128, stride=2), :].T for h in range(2)]
    data = jnp.concatenate(halves, axis=0)
    tables = [
        inv_ref[...],
        jnp.where(even, second_ref[...], first_ref[...]),
        jnp.where(even, first_ref[...], second_ref[...]),
    ]
    ids = lax.broadcasted_iota(jnp.int32, (512, 128), 0)
    for group in range(3):
        field = [data[group * GROUP + f * 8 : group * GROUP + f * 8 + 8] for f in range(FIELDS)]
        forces = field[:5]
        bx, by, bz = [line_basis(field[5 + d]) for d in range(3)]
        place = place_of(field[8], tables[group], 0)
        if group == 0:
            columns = [forces[v] * bx[i] for v in range(VARS) for i in range(4)]
            nodes = [by[j] * bz[k] for j in (0, 3, 1, 2) for k in range(4)]
            goal, matrix, size, shift = hot, lhs, 512, 0
        else:
            node = 3 if group == 1 else 0
            slope = combine((SLOPE[node, b], bz[b]) for b in range(4))
            columns = [forces[v] * bz[node] for v in range(VARS)]
            columns += [forces[v] * slope for v in range(VARS)]
            nodes = [by[j] * bx[i] for j in (0, 3, 1, 2) for i in range(4)]
            goal, matrix, size = (hot_low, lhs_low, 256) if group == 1 else (hot_up, lhs_up, 256)
            shift = 256 if group == 1 else 0
        for n, tile in enumerate(nodes):
            grid[group, n * 8 : n * 8 + 8, :] = tile
        for n, tile in enumerate(columns):
            strength[group, n * 8 : n * 8 + 8, :] = tile
        count = len(columns) * 16
        for c in range(CAP):
            here = slice(c * 128, c * 128 + 128)
            node_rows = grid[group, pl.ds(c, 16, stride=8), :]
            for n in range(len(columns)):
                row = strength[group, n * 8 + c : n * 8 + c + 1, :]
                hi, lo = split2(node_rows * row)
                matrix[n * 16 : n * 16 + 16, here] = hi
                matrix[count + n * 16 : count + n * 16 + 16, here] = lo
            found = place[c : c + 1, :] - shift
            goal[:, here] = jnp.where(ids[:size] == found, 1.0, 0.0).astype(BF16)

    res = nt_dot(lhs[...], hot[...])
    val = res[:320] + res[320:]
    for g in range(COLS):
        tiles = [val[g * 8 : g * 8 + 8, t * 128 : t * 128 + 128] for t in range(4)]
        for k, tile in enumerate(transpose4(tiles, mk)):
            s_ref[(g * 4 + k) * 8 : (g * 4 + k) * 8 + 8, :] = tile
    res_low = nt_dot(lhs_low[...], hot_low[...])
    res_up = nt_dot(lhs_up[...], hot_up[...])
    val_low, val_up = res_low[:160] + res_low[160:], res_up[:160] + res_up[160:]
    for part, goal in ((0, su), (1, sg)):
        for v in range(VARS):
            for jj in range(2):
                at = (part * VARS + v) * 16 + jj * 8
                tiles = [
                    val[at : at + 8, t * 128 : t * 128 + 128]
                    for val in (val_low, val_up)
                    for t in range(2)
                ]
                for i, tile in enumerate(transpose4(tiles, mk)):
                    col = (v * 4 + i) * 2 + jj
                    goal[col * 8 : col * 8 + 8, :] = tile

    apply_operator(s_ref, new_ref, su, sg, mk, 0.5 * TIME_STEP * TIME_STEP, TIME_STEP)
    fill_order([inv_ref[4 + t : 5 + t, :].astype(jnp.int32) for t in range(4)], order)
    for vi in range(VARS * 4):
        for jj in range(2):
            g = vi * 2 + jj
            at = [slice((g * 4 + k) * 8, (g * 4 + k) * 8 + 8) for k in range(4)]
            tiles = transpose4([new_ref[a, :] + base_ref[a, :] for a in at], mk)
            for t in range(4):
                new_ref[(g * 4 + t) * 8 : (g * 4 + t) * 8 + 8, :] = tiles[t]
        for t in range(4):
            x = jnp.concatenate(
                [new_ref[((vi * 2 + jj) * 4 + t) * 8 : ((vi * 2 + jj) * 4 + t) * 8 + 8, :] for jj in range(2)],
                axis=0,
            )
            hi, lo = split2(x)
            lhs[vi * 16 : vi * 16 + 16, t * 128 : t * 128 + 128] = hi
            lhs[320 + vi * 16 : 336 + vi * 16, t * 128 : t * 128 + 128] = lo
    res = nt_dot(lhs[:, :512], order[...])
    val = res[:320] + res[320:]
    for vi in range(VARS * 4):
        for n, j in enumerate((0, 3, 1, 2)):
            out_ref[vi * 4 + j] = val[vi * 16 + n * 4 : vi * 16 + n * 4 + 4, :]


def call(kernel, outs, scratch, specs):
    return pl.pallas_call(
        kernel,
        out_shape=outs,
        in_specs=specs,
        out_specs=jax.tree.map(lambda _: pl.BlockSpec(memory_space=pltpu.VMEM), outs),
        scratch_shapes=scratch,
        compiler_params=pltpu.CompilerParams(vmem_limit_bytes=VMEM_LIMIT),
    )


def tile_array(count):
    return jax.ShapeDtypeStruct((count * 8, 128), F32)


SMEM = pl.BlockSpec(memory_space=pltpu.SMEM)
VMEM = pl.BlockSpec(memory_space=pltpu.VMEM)


def entry_call(par, route, slots, forces, coords, lists, state):
    halo = tile_array(2 * COLS + 1)
    arrays = (route, slots, forces, coords, lists, state)
    return call(
        entry_kernel,
        (jax.ShapeDtypeStruct((256, 128), F32), tile_array(TILES), halo, halo, tile_array(1)),
        [pltpu.VMEM(x.shape, x.dtype) for x in arrays]
        + [
            pltpu.VMEM((512, 512), BF16),
            pltpu.VMEM((640, 512), BF16),
            pltpu.SemaphoreType.DMA((6,)),
        ],
        [SMEM] + [pl.BlockSpec(memory_space=pltpu.HBM)] * 6,
    )(par, *[pltpu.with_memory_space_constraint(x, pltpu.HBM) for x in arrays])


def state_call(par, u, first, second):
    cols = pltpu.VMEM((COLS * 8, 128), F32)
    return call(
        state_kernel,
        tile_array(TILES),
        [cols, cols, cols, cols, pltpu.VMEM((TILES * 8, 128), F32)],
        [SMEM] + [VMEM] * 3,
    )(par, u, first, second)


def source_call(par, pts, inv, first, second, base):
    cols = pltpu.VMEM((COLS * 8, 128), F32)
    field = pltpu.VMEM((TILES * 8, 128), F32)
    return call(
        source_kernel,
        jax.ShapeDtypeStruct((VARS * 16, 4, 512), F32),
        [
            pltpu.VMEM((512, 512), BF16),
            pltpu.VMEM((512, 1024), BF16),
            pltpu.VMEM((256, 1024), BF16),
            pltpu.VMEM((256, 1024), BF16),
            pltpu.VMEM((640, 1024), BF16),
            pltpu.VMEM((320, 1024), BF16),
            pltpu.VMEM((320, 1024), BF16),
            pltpu.VMEM((3, 128, 128), F32),
            pltpu.VMEM((3, 160, 128), F32),
            cols,
            cols,
            field,
            field,
        ],
        [SMEM] + [VMEM] * 5,
    )(par, pts, inv, first, second, base)


def on_device(state, neighbour_map, layer_lists, forces, positions, route, element_slot):
    count = lax.axis_size("sfc")
    inside = [(d, d ^ 1) for d in range(count)]
    across = [(d, (d + 1) % count if d % 2 else (d - 1) % count) for d in range(count)]
    par = (lax.axis_index("sfc") & 1).astype(jnp.int32).reshape(1)
    pack, u, first, second, inv = entry_call(
        par,
        route.reshape(1, -1),
        element_slot.reshape(1, -1),
        forces,
        positions,
        layer_lists,
        state.reshape(VARS * 16, 4, -1),
    )
    second = lax.ppermute(second, "sfc", across)
    first = lax.ppermute(first, "sfc", inside)
    pts = lax.all_to_all(pack, "sfc", split_axis=0, concat_axis=0, tiled=True)
    base = state_call(par, u, first, second)
    tail = slice(2 * COLS * 8, None)
    out = source_call(par, pts, inv, first[tail], second[tail], base)
    return out.reshape(state.shape)


def solution(mesh):
    in_specs = (
        P(None, None, None, None, "sfc"),
        P(None, "sfc"),
        P(None, "sfc"),
        P(None, "sfc"),
        P(None, "sfc"),
        P("sfc", None),
        P("sfc"),
    )
    out_specs = P(None, None, None, None, "sfc")
    return jax.shard_map(
        on_device, mesh=mesh, in_specs=in_specs, out_specs=out_specs, check_vma=False
    )
```

```python
import functools

import jax
import jax.numpy as jnp
import numpy as np
from jax import lax
from jax.experimental import pallas as pl
from jax.experimental.pallas import tpu as pltpu
from jax.sharding import PartitionSpec as P

NODE_POINTS = (-1.0, -0.4472135954999579, 0.4472135954999579, 1.0)
GSCALE = 2.0
HALF_LIFT = 6.0
ADVECT = (0.6, -0.4, 0.8)
VISCOSITY = 0.02
TIME_STEP = 0.04

VARS = 5
CAP = 8
FIELDS = 9
GROUP = FIELDS * CAP
COLS = VARS * 4 * 2
TILES = COLS * 4
VMEM_LIMIT = 24 * 1024 * 1024
F32 = jnp.float32
BF16 = jnp.bfloat16


def diff_table():
    factor = [
        float(np.prod([NODE_POINTS[a] - NODE_POINTS[k] for k in range(4) if k != a]))
        for a in range(4)
    ]
    table = np.zeros((4, 4))
    for a in range(4):
        for b in range(4):
            if a != b:
                table[a, b] = factor[a] / factor[b] / (NODE_POINTS[a] - NODE_POINTS[b])
            else:
                table[a, b] = sum(
                    (1.0 / (NODE_POINTS[a] - NODE_POINTS[k]) for k in range(4) if k != a)
                )
    return table


SLOPE = GSCALE * diff_table()


def line_operator(direction):
    a, nu = ADVECT[direction], VISCOSITY
    out = np.zeros((4, 8))
    for col in range(8):
        value = np.zeros(8)
        value[col] = 1.0
        u, (um, gm, up, gp) = value[:4], value[4:]
        q = SLOPE @ u
        q[0] -= HALF_LIFT * (um - u[0])
        q[3] += HALF_LIFT * (up - u[3])
        qm = gm + HALF_LIFT * (u[0] - um)
        qp = gp - HALF_LIFT * (u[3] - up)
        res = -SLOPE @ (a * u - nu * q)
        for node, normal, ou, oq in ((0, -1.0, um, qm), (3, 1.0, up, qp)):
            along = normal * a
            res[node] += -HALF_LIFT * (along - abs(along)) * (ou - u[node])
            res[node] += HALF_LIFT * nu * normal * (oq - q[node])
        out[:, col] = res
    return out


LINES = [line_operator(d) for d in range(3)]
UM, GM, UP, GP = 4, 5, 6, 7


def rolled(x, shift):
    return pltpu.roll(x, shift % 8, 0)


def lanes(x, shift):
    return pltpu.roll(x, shift % 128, 1)


def combine(pairs):
    total = None
    for coef, value in pairs:
        if isinstance(coef, (float, np.floating)):
            if coef == 0.0:
                continue
            term = value if coef == 1.0 else value * float(coef)
        else:
            term = value * coef
        total = term if total is None else total + term
    return total


class Masks:
    def __init__(self):
        sub = lax.broadcasted_iota(jnp.int32, (8, 128), 0)
        lane = lax.broadcasted_iota(jnp.int32, (8, 128), 1)
        self.h0 = sub < 4
        self.l0 = (sub & 2) == 0
        self.r0 = (sub & 1) == 0
        self.x_first = (lane & 15) == 0
        self.x_last = (lane & 15) == 15
        self.y_wrap = (self.h0 & (lane < 16)) | (~self.h0 & (lane >= 112))
        self.sign = jnp.where(self.h0, 1.0, -1.0).astype(F32)

    def by_half(self, low, high):
        if low == high:
            return float(low)
        return jnp.where(self.h0, float(low), float(high)).astype(F32)


def rows8(index):
    if isinstance(index, int):
        return slice(index * 8, index * 8 + 8)
    return pl.ds(pl.multiple_of(index * 8, 8), 8)


def x_line(u, mk, mat):
    g0 = combine((SLOPE[0, b], u[b]) for b in range(4))
    g3 = combine((SLOPE[3, b], u[b]) for b in range(4))

    def before(t):
        return jnp.where(mk.x_first, lanes(t, -15), lanes(t, 1))

    def after(t):
        return jnp.where(mk.x_last, lanes(t, 15), lanes(t, -1))

    um, gm, up, gp = before(u[3]), before(g3), after(u[0]), after(g0)
    terms = list(u) + [um, gm, up, gp]
    return [combine((mat[a, c], terms[c]) for c in range(8)) for a in range(4)]


def y_coefs(mk, mat):
    out = []
    for jj in range(2):
        o = 3 - jj
        row = [mk.by_half(mat[jj, b], mat[o, 3 - b]) for b in range(4)]
        row.append(mk.by_half(mat[jj, UM], mat[o, UP]))
        row.append(mk.by_half(mat[jj, UP], mat[o, UM]))
        row.append(mk.by_half(mat[jj, GM], mat[o, GP]))
        out.append(row)
    return out


def y_line(u0, u1, mk, coefs):
    r0, r1 = rolled(u0, 4), rolled(u1, 4)
    g = combine(((SLOPE[0, 0], u0), (SLOPE[0, 1], u1), (SLOPE[0, 2], r1), (SLOPE[0, 3], r0)))
    g = rolled(g * mk.sign, 4)

    def outer(t):
        near = jnp.where(mk.h0, lanes(t, 16), lanes(t, -16))
        far = jnp.where(mk.r0, rolled(near, -1), rolled(near, 1))
        return jnp.where(mk.y_wrap, far, near)

    n, gn = outer(r0), outer(g)
    nr = rolled(n, 4)
    return [
        combine(zip(coefs[0], (u0, u1, r1, r0, n, nr, gn))),
        combine(zip(coefs[1][:6], (u0, u1, r1, r0, n, nr))),
    ]


def z_line(u, hu, hg, mk, mat):
    g0 = combine((SLOPE[0, b], u[b]) for b in range(4))
    g3 = combine((SLOPE[3, b], u[b]) for b in range(4))
    um = jnp.where(mk.l0, hu, rolled(u[3], 2))
    gm = jnp.where(mk.l0, hg, rolled(g3, 2))
    up = jnp.where(mk.l0, rolled(u[0], -2), hu)
    gp = jnp.where(mk.l0, rolled(g0, -2), hg)
    terms = list(u) + [um, gm, up, gp]
    return [combine((mat[a, c], terms[c]) for c in range(8)) for a in range(4)]


def operator_of(src, dst, hu, hg, mk, scale, ident):
    mats = [scale * m for m in LINES]
    mats[2][:, :4] += ident * np.eye(4)
    coefs = y_coefs(mk, mats[1])

    def per_variable(v):
        col = v * 8
        for c in range(8):
            u = [src[rows8((col + c) * 4 + k), :] for k in range(4)]
            new = z_line(u, hu[rows8(col + c), :], hg[rows8(col + c), :], mk, mats[2])
            for k in range(4):
                dst[rows8((col + c) * 4 + k), :] = new[k]
        for i in range(4):
            for k in range(4):
                at = [rows8((col + 2 * i + jj) * 4 + k) for jj in range(2)]
                new = y_line(src[at[0], :], src[at[1], :], mk, coefs)
                for jj in range(2):
                    dst[at[jj], :] += new[jj]
        for jj in range(2):
            for k in range(4):
                at = [rows8((col + 2 * i + jj) * 4 + k) for i in range(4)]
                new = x_line([src[a, :] for a in at], mk, mats[0])
                for i in range(4):
                    dst[at[i], :] += new[i]

    return per_variable


def apply_operator(*args):
    one = operator_of(*args)

    def body(v, carry):
        one(v)
        return carry

    lax.fori_loop(0, VARS, body, 0)


def split2(x):
    hi = x.astype(BF16)
    return hi, (x - hi.astype(F32)).astype(BF16)


def both(res):
    half = res.shape[0] // 2
    return res[:half] + res[half:]


NODE_ROWS = (0, 1, 3, 2)


def spread(val, goal, first):
    for vi in range(val.shape[0] // 16):
        for h in range(2):
            for t in range(4):
                tile = val[vi * 16 + h * 8 : vi * 16 + h * 8 + 8, t * 128 : t * 128 + 128]
                goal[pl.ds((first + vi) * 64 + h * 4 + t, 8, stride=8), :] = tile


def nt_dot(a, b):
    return lax.dot_general(a, b, (((1,), (1,)), ((), ())), preferred_element_type=F32)


def fill_order(rows, order):
    ids = lax.broadcasted_iota(jnp.int32, (512, 128), 0)
    for t in range(4):
        order[:, t * 128 : t * 128 + 128] = jnp.where(ids == rows[t], 1.0, 0.0).astype(BF16)


def pack_points(route, payload, pack_ref):
    dest = lax.broadcasted_iota(jnp.int32, (128, 128), 0)
    lane = lax.broadcasted_iota(jnp.int32, (128, 128), 1)
    slot = lax.broadcasted_iota(jnp.int32, (8, 128), 0).astype(F32)
    to_device = [jnp.where(dest == route[:, t * 128 : t * 128 + 128], 1.0, 0.0) for t in range(4)]
    stacked = jnp.concatenate(to_device, axis=0).astype(BF16)
    before = jnp.where(dest < lane, 1.0, 0.0).astype(BF16)
    inside = jnp.dot(stacked, before, preferred_element_type=F32)
    totals = jnp.dot(stacked, jnp.ones((128, 128), BF16), preferred_element_type=F32)
    base = jnp.zeros((128, 128), F32)
    out = jnp.zeros((128, 128), F32)
    for t in range(4):
        here = slice(t * 128, t * 128 + 128)
        count = inside[here] + base
        base = base + totals[here]
        within = jnp.sum(count * to_device[t], axis=0, keepdims=True)
        chosen = slot == within
        rows = [jnp.where(chosen, p[:, here], 0.0) for p in payload]
        rows.append(jnp.zeros((128 - GROUP, 128), F32))
        rest = jnp.concatenate(rows, axis=0)
        for _ in range(3):
            part = rest.astype(BF16)
            rest = rest - part.astype(F32)
            out = out + nt_dot(stacked[here], part)
    low = pltpu.roll(pltpu.roll(out, 1, 0), GROUP, 1)
    up = pltpu.roll(pltpu.roll(out, 127, 0), 2 * GROUP - 128, 1)
    pack_ref[pl.ds(0, 128, stride=2), :] = jnp.where(lane < GROUP, out, low)
    pack_ref[pl.ds(1, 128, stride=2), :] = jnp.where(lane < 2 * GROUP - 128, low, up)


def fill_halo(u_ref, up_ref, down_ref, mk):
    mat = TIME_STEP * LINES[2]
    sides = ((3, 2, UM, GM, up_ref), (0, -2, UP, GP, down_ref))

    def per_variable(v, carry):
        for c in range(8):
            col = v * 8 + c
            u = [u_ref[rows8(col * 4 + k), :] for k in range(4)]
            for node, shift, near, slope, goal in sides:
                g = combine((SLOPE[node, b], u[b]) for b in range(4))
                near_u, near_g = rolled(u[node], shift), rolled(g, shift)
                for part, (row, a) in enumerate(((np.eye(4)[node], u[node]), (SLOPE[node], g))):
                    b = combine(
                        list(zip(row + row @ mat[:, :4], u))
                        + [(row @ mat[:, near], near_u), (row @ mat[:, slope], near_g)]
                    )
                    a = rolled(a, -shift)
                    tile = jnp.where(mk.l0, a, b) if node == 3 else jnp.where(mk.l0, b, a)
                    goal[rows8(part * COLS + col), :] = tile
        return carry

    lax.fori_loop(0, VARS, per_variable, 0)


def entry_kernel(
    route_hbm, slot_hbm, forces_hbm, coords_hbm, lists_hbm, state_hbm,
    pack_ref, u_ref, up_ref, down_ref, inv_ref, order,
    route_ref, slot_ref, forces_ref, coords_ref, lists_ref, state_ref, lhs, sems,
):
    sources = (route_hbm, slot_hbm, forces_hbm, coords_hbm, lists_hbm, state_hbm)
    targets = (route_ref, slot_ref, forces_ref, coords_ref, lists_ref, state_ref)
    copies = [
        pltpu.make_async_copy(a, b, sems.at[n]) for n, (a, b) in enumerate(zip(sources, targets))
    ]
    for copy in copies:
        copy.start()
    mk = Masks()
    for copy in copies[:5]:
        copy.wait()
    payload = [forces_ref[f : f + 1, :] for f in range(5)]
    payload += [coords_ref[f : f + 1, :] for f in range(3)]
    payload.append(slot_ref[...].astype(F32))
    pack_points(route_ref[...], payload, pack_ref)

    rows = [
        lists_ref[t // 2 : t // 2 + 1, (t % 2) * 128 : (t % 2) * 128 + 128] for t in range(4)
    ]
    fill_order(rows, order)
    copies[5].wait()
    for vi in range(VARS * 4):
        x = jnp.concatenate([state_ref[vi * 4 + j] for j in NODE_ROWS], axis=0)
        hi, lo = split2(x)
        lhs[vi * 16 : vi * 16 + 16, :] = hi
        lhs[320 + vi * 16 : 336 + vi * 16, :] = lo
    res = jnp.dot(lhs[...], order[...], preferred_element_type=F32)
    spread(both(res), u_ref, 0)

    place = lax.broadcasted_iota(jnp.int32, (16, 512), 1)
    digit = lax.broadcasted_iota(jnp.int32, (16, 512), 0)
    digits = jnp.where(digit == 0, place >> 4, place & 15).astype(F32).astype(BF16)
    where = nt_dot(digits, order[...])
    inv = where[0:1, :] * 16.0 + where[1:2, :]
    inv = [inv[:, t * 128 : t * 128 + 128] for t in range(4)]
    inv = jnp.concatenate(inv + inv, axis=0)
    inv_ref[...] = inv
    up_ref[2 * COLS * 8 :, :] = inv
    down_ref[2 * COLS * 8 :, :] = inv

    fill_halo(u_ref, up_ref, down_ref, mk)


def state_kernel(u_ref, before_ref, after_ref, base_ref, au, ag, hu, hg, m0):
    mk = Masks()
    mat = TIME_STEP * LINES[2]
    top, bottom = np.eye(4)[3], np.eye(4)[0]

    def unpack(col, carry):
        for part, (a, h) in enumerate(((au, hu), (ag, hg))):
            low = before_ref[rows8(part * COLS + col), :]
            high = after_ref[rows8(part * COLS + col), :]
            a[rows8(col), :] = jnp.where(mk.l0, low, high)
            h[rows8(col), :] = jnp.where(mk.l0, rolled(low, -2), rolled(high, 2))
        return carry

    lax.fori_loop(0, COLS, unpack, 0, unroll=8)
    apply_operator(u_ref, m0, au, ag, mk, TIME_STEP, 1.0)

    x_mat, coefs = TIME_STEP * LINES[0], y_coefs(mk, TIME_STEP * LINES[1])

    def halo(v, carry):
        for c in range(8):
            col = v * 8 + c
            u = [u_ref[rows8(col * 4 + k), :] for k in range(4)]
            g0 = combine((SLOPE[0, b], u[b]) for b in range(4))
            g3 = combine((SLOPE[3, b], u[b]) for b in range(4))
            for h, f_low, f_high in ((hu, top, bottom), (hg, SLOPE[3], SLOPE[0])):
                low = combine(((f_low @ mat[:, UP], u[0]), (f_low @ mat[:, GP], g0)))
                high = combine(((f_high @ mat[:, UM], u[3]), (f_high @ mat[:, GM], g3)))
                h[rows8(col), :] += jnp.where(mk.l0, low, high)
        for a, h in ((au, hu), (ag, hg)):
            for i in range(4):
                at = [rows8(v * 8 + 2 * i + jj) for jj in range(2)]
                new = y_line(a[at[0], :], a[at[1], :], mk, coefs)
                for jj in range(2):
                    h[at[jj], :] += new[jj]
            for jj in range(2):
                at = [rows8(v * 8 + 2 * i + jj) for i in range(4)]
                new = x_line([a[r, :] for r in at], mk, x_mat)
                for i in range(4):
                    h[at[i], :] += new[i]
        return carry

    lax.fori_loop(0, VARS, halo, 0)
    apply_operator(m0, base_ref, hu, hg, mk, 0.5 * TIME_STEP, 0.5)

    def finish(n, carry):
        base_ref[rows8(n), :] += 0.5 * u_ref[rows8(n), :]
        return carry

    lax.fori_loop(0, TILES, finish, 0, unroll=16)


def line_basis(coords):
    rows = []
    for a in range(4):
        term = None
        for k in range(4):
            if k != a:
                factor = (coords - NODE_POINTS[k]) * (1.0 / (NODE_POINTS[a] - NODE_POINTS[k]))
                term = factor if term is None else term * factor
        rows.append(term)
    return rows


def place_of(slots, table, row):
    number = slots.astype(jnp.int32)
    inner, outer = number & 127, number >> 7
    found = jnp.zeros((8, 128), F32)
    for t in range(4):
        line = jnp.broadcast_to(table[row + t : row + t + 1, :], (8, 128))
        found = jnp.where(outer == t, jnp.take_along_axis(line, inner, axis=1), found)
    return found.astype(jnp.int32)


def fill_hots(hots, places):
    ids = lax.broadcasted_iota(jnp.int32, (16, 128), 0)
    places = [[jnp.broadcast_to(p[c : c + 1, :], (16, 128)) for c in range(CAP)] for p in places]

    def body(n, carry):
        for hot, place in zip(hots, places):
            count = hot.shape[0] // 256
            for m in range(count):
                first = (n * count + m) * 16
                here = ids + first
                for c in range(CAP):
                    at = pl.ds(pl.multiple_of(first, 16), 16)
                    hot[at, c * 128 : c * 128 + 128] = jnp.where(here == place[c], 1.0, 0.0).astype(BF16)
        return carry

    lax.fori_loop(0, 16, body, 0)


def fill_terms(matrix, columns, nodes, strength, grid, group, first, count):
    if first == 0:
        for n, tile in enumerate(nodes):
            grid[group, n * 8 : n * 8 + 8, :] = tile
        for n, tile in enumerate(columns):
            strength[group, n * 8 : n * 8 + 8, :] = tile
    for c in range(CAP):
        here = slice(c * 128, c * 128 + 128)
        node_rows = grid[group, pl.ds(c, 16, stride=8), :]
        for n in range(first, first + count):
            hi, lo = split2(node_rows * strength[group, n * 8 + c : n * 8 + c + 1, :])
            at = (first + n) * 16
            matrix[at : at + 16, here] = hi
            matrix[at + count * 16 : at + count * 16 + 16, here] = lo


def trace_terms(field, node):
    bx, by, bz = [line_basis(field[5 + d]) for d in range(3)]
    slope = combine((SLOPE[node, b], bz[b]) for b in range(4))
    columns = [field[v] * bz[node] for v in range(VARS)]
    columns += [field[v] * slope for v in range(VARS)]
    pairs = [(i, j) for h in range(2) for i in range(4) for j in NODE_ROWS[2 * h : 2 * h + 2]]
    return columns, [by[j] * bx[i] for i, j in pairs]


SPANS = ((0, 3), (3, 2))


def source_kernel(
    pts_ref, inv_ref, before_ref, after_ref, base_ref, order, out_hbm,
    hot, hot_low, hot_up, lhs, lhs_low, lhs_up, grid, strength, su, sg, s_ref, new_ref,
    lhs_out, out_ref, sems,
):
    mk = Masks()
    halves = [pts_ref[pl.ds(h, 128, stride=2), :].T for h in range(2)]
    data = jnp.concatenate(halves, axis=0)
    field = [
        [data[g * GROUP + f * 8 : g * GROUP + f * 8 + 8] for f in range(FIELDS)] for g in range(3)
    ]
    fill_hots(
        (hot_low, hot_up, hot),
        (
            place_of(field[1][8], before_ref, 0) - 256,
            place_of(field[2][8], after_ref, 0),
            place_of(field[0][8], inv_ref, 0),
        ),
    )
    traces = []
    for group, node, matrix, goal in ((1, 3, lhs_low, hot_low), (2, 0, lhs_up, hot_up)):
        fill_terms(matrix, *trace_terms(field[group], node), strength, grid, group, 0, 10)
        traces.append(both(nt_dot(matrix[...], goal[...])))
    bx, by, bz = [line_basis(field[0][5 + d]) for d in range(3)]
    columns = [field[0][v] * bx[i] for v in range(VARS) for i in range(4)]
    nodes = [by[j] * bz[k] for j in NODE_ROWS for k in range(4)]
    vals = []
    for first, count in SPANS:
        fill_terms(lhs, columns, nodes, strength, grid, 0, first * 4, count * 4)
        vals.append(both(nt_dot(lhs[first * 128 : (first + count) * 128, :], hot[...])))
    for part, goal in ((0, su), (1, sg)):
        for v in range(VARS):
            for h in range(2):
                at = (part * VARS + v) * 16 + h * 8
                for t in range(4):
                    tile = traces[t // 2][at : at + 8, (t % 2) * 128 : (t % 2) * 128 + 128]
                    goal[pl.ds(v * 64 + h * 4 + t, 8, stride=8), :] = tile

    one = operator_of(s_ref, new_ref, su, sg, mk, 0.5 * TIME_STEP * TIME_STEP, TIME_STEP)
    for (first, count), val in zip(SPANS, vals):
        spread(val, s_ref, first * 4)
        for v in range(first, first + count):
            one(v)
    copies = []
    for n, (first, count) in enumerate(SPANS):
        for vi in range(first * 4, (first + count) * 4):
            at = (first * 4 + vi) * 16
            for t in range(4):
                rows = [pl.ds(vi * 64 + h * 4 + t, 8, stride=8) for h in range(2)]
                x = jnp.concatenate([new_ref[r, :] + base_ref[r, :] for r in rows], axis=0)
                hi, lo = split2(x)
                lhs_out[at : at + 16, t * 128 : t * 128 + 128] = hi
                at_lo = at + count * 64
                lhs_out[at_lo : at_lo + 16, t * 128 : t * 128 + 128] = lo
        val = both(nt_dot(lhs_out[first * 128 : (first + count) * 128, :], order[...]))
        for vi in range(first * 4, (first + count) * 4):
            for m, j in enumerate(NODE_ROWS):
                at = (vi - first * 4) * 16 + m * 4
                out_ref[vi * 4 + j] = val[at : at + 4, :]
        part = pl.ds(first * 16, count * 16)
        copies.append(pltpu.make_async_copy(out_ref.at[part], out_hbm.at[part], sems.at[n]))
        copies[-1].start()
    for copy in copies:
        copy.wait()


def call(kernel, outs, scratch, specs, place=pltpu.VMEM):
    return pl.pallas_call(
        kernel,
        out_shape=outs,
        in_specs=specs,
        out_specs=jax.tree.map(lambda _: pl.BlockSpec(memory_space=place), outs),
        scratch_shapes=scratch,
        compiler_params=pltpu.CompilerParams(vmem_limit_bytes=VMEM_LIMIT),
    )


def tile_array(count):
    return jax.ShapeDtypeStruct((count * 8, 128), F32)


VMEM = pl.BlockSpec(memory_space=pltpu.VMEM)


def entry_call(route, slots, forces, coords, lists, state):
    arrays = (route, slots, forces, coords, lists, state)
    return call(
        entry_kernel,
        (
            jax.ShapeDtypeStruct((256, 128), F32),
            tile_array(TILES),
            tile_array(2 * COLS + 1),
            tile_array(2 * COLS + 1),
            tile_array(1),
            jax.ShapeDtypeStruct((512, 512), BF16),
        ),
        [pltpu.VMEM(x.shape, x.dtype) for x in arrays]
        + [
            pltpu.VMEM((640, 512), BF16),
            pltpu.SemaphoreType.DMA((6,)),
        ],
        [pl.BlockSpec(memory_space=pltpu.HBM)] * 6,
    )(*[pltpu.with_memory_space_constraint(x, pltpu.HBM) for x in arrays])


def state_call(u, before, after):
    cols = pltpu.VMEM((COLS * 8, 128), F32)
    return call(
        state_kernel,
        tile_array(TILES),
        [cols, cols, cols, cols, pltpu.VMEM((TILES * 8, 128), F32)],
        [VMEM] * 3,
    )(u, before, after)


def source_call(pts, inv, before, after, base, order):
    cols = pltpu.VMEM((COLS * 8, 128), F32)
    field = pltpu.VMEM((TILES * 8, 128), F32)
    return call(
        source_kernel,
        jax.ShapeDtypeStruct((VARS * 16, 4, 512), F32),
        [
            pltpu.VMEM((512, 1024), BF16),
            pltpu.VMEM((256, 1024), BF16),
            pltpu.VMEM((256, 1024), BF16),
            pltpu.VMEM((640, 1024), BF16),
            pltpu.VMEM((320, 1024), BF16),
            pltpu.VMEM((320, 1024), BF16),
            pltpu.VMEM((3, 128, 128), F32),
            pltpu.VMEM((3, 160, 128), F32),
            cols,
            cols,
            field,
            field,
            pltpu.VMEM((640, 512), BF16),
            pltpu.VMEM((VARS * 16, 4, 512), F32),
            pltpu.SemaphoreType.DMA((2,)),
        ],
        [VMEM] * 6,
        pltpu.HBM,
    )(pts, inv, before, after, base, order)


def on_device(state, neighbour_map, layer_lists, forces, positions, route, element_slot):
    count = lax.axis_size("sfc")
    forward = [(d, (d + 1) % count) for d in range(count)]
    backward = [(target, source) for source, target in forward]
    pack, u, up, down, inv, order = entry_call(
        route.reshape(1, -1),
        element_slot.reshape(1, -1),
        forces,
        positions,
        layer_lists,
        state.reshape(VARS * 16, 4, -1),
    )
    before = lax.ppermute(up, "sfc", forward)
    after = lax.ppermute(down, "sfc", backward)
    pts = lax.all_to_all(pack, "sfc", split_axis=0, concat_axis=0, tiled=True)
    base = state_call(u, before, after)
    table = slice(2 * COLS * 8, None)
    out = source_call(pts, inv, before[table], after[table], base, order)
    return out.reshape(state.shape)


def solution(mesh):
    in_specs = (
        P(None, None, None, None, "sfc"),
        P(None, "sfc"),
        P(None, "sfc"),
        P(None, "sfc"),
        P(None, "sfc"),
        P("sfc", None),
        P("sfc"),
    )
    out_specs = P(None, None, None, None, "sfc")
    return jax.shard_map(
        on_device, mesh=mesh, in_specs=in_specs, out_specs=out_specs, check_vma=False
    )
```

```python
import functools

import jax
import jax.numpy as jnp
import numpy as np
from jax import lax
from jax.experimental import pallas as pl
from jax.experimental.pallas import tpu as pltpu
from jax.sharding import PartitionSpec as P

NODE_POINTS = (-1.0, -0.4472135954999579, 0.4472135954999579, 1.0)
GSCALE = 2.0
HALF_LIFT = 6.0
ADVECT = (0.6, -0.4, 0.8)
VISCOSITY = 0.02
TIME_STEP = 0.04

VARS = 5
CAP = 8
FIELDS = 9
GROUP = FIELDS * CAP
COLS = VARS * 4 * 2
TILES = COLS * 4
VMEM_LIMIT = 24 * 1024 * 1024
F32 = jnp.float32
BF16 = jnp.bfloat16


def diff_table():
    factor = [
        float(np.prod([NODE_POINTS[a] - NODE_POINTS[k] for k in range(4) if k != a]))
        for a in range(4)
    ]
    table = np.zeros((4, 4))
    for a in range(4):
        for b in range(4):
            if a != b:
                table[a, b] = factor[a] / factor[b] / (NODE_POINTS[a] - NODE_POINTS[b])
            else:
                table[a, b] = sum(
                    (1.0 / (NODE_POINTS[a] - NODE_POINTS[k]) for k in range(4) if k != a)
                )
    return table


SLOPE = GSCALE * diff_table()


def line_operator(direction):
    a, nu = ADVECT[direction], VISCOSITY
    out = np.zeros((4, 8))
    for col in range(8):
        value = np.zeros(8)
        value[col] = 1.0
        u, (um, gm, up, gp) = value[:4], value[4:]
        q = SLOPE @ u
        q[0] -= HALF_LIFT * (um - u[0])
        q[3] += HALF_LIFT * (up - u[3])
        qm = gm + HALF_LIFT * (u[0] - um)
        qp = gp - HALF_LIFT * (u[3] - up)
        res = -SLOPE @ (a * u - nu * q)
        for node, normal, ou, oq in ((0, -1.0, um, qm), (3, 1.0, up, qp)):
            along = normal * a
            res[node] += -HALF_LIFT * (along - abs(along)) * (ou - u[node])
            res[node] += HALF_LIFT * nu * normal * (oq - q[node])
        out[:, col] = res
    return out


LINES = [line_operator(d) for d in range(3)]
UM, GM, UP, GP = 4, 5, 6, 7


def rolled(x, shift):
    return pltpu.roll(x, shift % 8, 0)


def lanes(x, shift):
    return pltpu.roll(x, shift % 128, 1)


def combine(pairs):
    total = None
    for coef, value in pairs:
        if isinstance(coef, (float, np.floating)):
            if coef == 0.0:
                continue
            term = value if coef == 1.0 else value * float(coef)
        else:
            term = value * coef
        total = term if total is None else total + term
    return total


class Masks:
    def __init__(self):
        sub = lax.broadcasted_iota(jnp.int32, (8, 128), 0)
        lane = lax.broadcasted_iota(jnp.int32, (8, 128), 1)
        self.h0 = sub < 4
        self.l0 = (sub & 2) == 0
        self.r0 = (sub & 1) == 0
        self.x_first = (lane & 15) == 0
        self.x_last = (lane & 15) == 15
        self.y_wrap = (self.h0 & (lane < 16)) | (~self.h0 & (lane >= 112))
        self.sign = jnp.where(self.h0, 1.0, -1.0).astype(F32)

    def by_half(self, low, high):
        if low == high:
            return float(low)
        return jnp.where(self.h0, float(low), float(high)).astype(F32)


def rows8(index):
    if isinstance(index, int):
        return slice(index * 8, index * 8 + 8)
    return pl.ds(pl.multiple_of(index * 8, 8), 8)


def x_line(u, mk, mat):
    g0 = combine((SLOPE[0, b], u[b]) for b in range(4))
    g3 = combine((SLOPE[3, b], u[b]) for b in range(4))

    def before(t):
        return jnp.where(mk.x_first, lanes(t, -15), lanes(t, 1))

    def after(t):
        return jnp.where(mk.x_last, lanes(t, 15), lanes(t, -1))

    um, gm, up, gp = before(u[3]), before(g3), after(u[0]), after(g0)
    terms = list(u) + [um, gm, up, gp]
    return [combine((mat[a, c], terms[c]) for c in range(8)) for a in range(4)]


def y_coefs(mk, mat):
    out = []
    for jj in range(2):
        o = 3 - jj
        row = [mk.by_half(mat[jj, b], mat[o, 3 - b]) for b in range(4)]
        row.append(mk.by_half(mat[jj, UM], mat[o, UP]))
        row.append(mk.by_half(mat[jj, UP], mat[o, UM]))
        row.append(mk.by_half(mat[jj, GM], mat[o, GP]))
        out.append(row)
    return out


def y_line(u0, u1, mk, coefs):
    r0, r1 = rolled(u0, 4), rolled(u1, 4)
    g = combine(((SLOPE[0, 0], u0), (SLOPE[0, 1], u1), (SLOPE[0, 2], r1), (SLOPE[0, 3], r0)))
    g = rolled(g * mk.sign, 4)

    def outer(t):
        near = jnp.where(mk.h0, lanes(t, 16), lanes(t, -16))
        far = jnp.where(mk.r0, rolled(near, -1), rolled(near, 1))
        return jnp.where(mk.y_wrap, far, near)

    n, gn = outer(r0), outer(g)
    nr = rolled(n, 4)
    return [
        combine(zip(coefs[0], (u0, u1, r1, r0, n, nr, gn))),
        combine(zip(coefs[1][:6], (u0, u1, r1, r0, n, nr))),
    ]


def z_line(u, hu, hg, mk, mat):
    g0 = combine((SLOPE[0, b], u[b]) for b in range(4))
    g3 = combine((SLOPE[3, b], u[b]) for b in range(4))
    um = jnp.where(mk.l0, hu, rolled(u[3], 2))
    gm = jnp.where(mk.l0, hg, rolled(g3, 2))
    up = jnp.where(mk.l0, rolled(u[0], -2), hu)
    gp = jnp.where(mk.l0, rolled(g0, -2), hg)
    terms = list(u) + [um, gm, up, gp]
    return [combine((mat[a, c], terms[c]) for c in range(8)) for a in range(4)]


def operator_of(src, dst, hu, hg, mk, scale, ident):
    mats = [scale * m for m in LINES]
    mats[2][:, :4] += ident * np.eye(4)
    coefs = y_coefs(mk, mats[1])

    def in_layer(v):
        col = v * 8
        for jj in range(2):
            for k in range(4):
                at = [rows8((col + 2 * i + jj) * 4 + k) for i in range(4)]
                new = x_line([src[a, :] for a in at], mk, mats[0])
                for i in range(4):
                    dst[at[i], :] = new[i]
        for i in range(4):
            for k in range(4):
                at = [rows8((col + 2 * i + jj) * 4 + k) for jj in range(2)]
                new = y_line(src[at[0], :], src[at[1], :], mk, coefs)
                for jj in range(2):
                    dst[at[jj], :] += new[jj]

    def across(v):
        col = v * 8
        for c in range(8):
            at = [rows8((col + c) * 4 + k) for k in range(4)]
            u = [src[a, :] for a in at]
            new = z_line(u, hu[rows8(col + c), :], hg[rows8(col + c), :], mk, mats[2])
            for k in range(4):
                dst[at[k], :] += new[k]

    return in_layer, across


def apply_operator(*args):
    in_layer, across = operator_of(*args)

    def body(v, carry):
        in_layer(v)
        across(v)
        return carry

    lax.fori_loop(0, VARS, body, 0)


def split2(x):
    hi = x.astype(BF16)
    return hi, (x - hi.astype(F32)).astype(BF16)


def both(res):
    half = res.shape[0] // 2
    return res[:half] + res[half:]


NODE_ROWS = (0, 1, 3, 2)


def spread(val, goal, first):
    for vi in range(val.shape[0] // 16):
        for h in range(2):
            for t in range(4):
                tile = val[vi * 16 + h * 8 : vi * 16 + h * 8 + 8, t * 128 : t * 128 + 128]
                goal[pl.ds((first + vi) * 64 + h * 4 + t, 8, stride=8), :] = tile


def nt_dot(a, b):
    return lax.dot_general(a, b, (((1,), (1,)), ((), ())), preferred_element_type=F32)


def fill_order(rows, order):
    ids = lax.broadcasted_iota(jnp.int32, (16, 128), 0)
    one, none = jnp.ones((16, 128), BF16), jnp.zeros((16, 128), BF16)
    rows = [jnp.broadcast_to(row, (16, 128)).astype(jnp.int16) for row in rows]
    for first in range(0, 512, 16):
        here = (ids + first).astype(jnp.int16)
        for t in range(4):
            found = jnp.where(here == rows[t], one, none)
            order[first : first + 16, t * 128 : t * 128 + 128] = found


def pack_points(route, payload, pack_ref):
    dest = lax.broadcasted_iota(jnp.int32, (128, 128), 0)
    lane = lax.broadcasted_iota(jnp.int32, (128, 128), 1)
    slot = lax.broadcasted_iota(jnp.int32, (8, 128), 0).astype(F32)
    to_device = [jnp.where(dest == route[:, t * 128 : t * 128 + 128], 1.0, 0.0) for t in range(4)]
    narrow = [x.astype(BF16) for x in to_device]
    before = jnp.where(dest < lane, 1.0, 0.0).astype(BF16)
    steps = jnp.concatenate([before, jnp.ones((128, 128), BF16)], axis=1)
    counts = jnp.dot(jnp.concatenate(narrow, axis=0), steps, preferred_element_type=F32)
    base = None
    parts = [[], [], []]
    for t in range(4):
        here = slice(t * 128, t * 128 + 128)
        count = counts[here, :128] if base is None else counts[here, :128] + base
        base = counts[here, 128:] if base is None else base + counts[here, 128:]
        within = jnp.sum(count * to_device[t], axis=0, keepdims=True)
        chosen = slot == within
        rows = [jnp.where(chosen, p[:, here], 0.0) for p in payload]
        rows.append(jnp.zeros((8, 128), F32))
        rest = jnp.concatenate(rows, axis=0)
        for part in parts:
            part.append(rest.astype(BF16))
            rest = rest - part[-1].astype(F32)
    terms = jnp.concatenate([jnp.concatenate(part, axis=1) for part in parts], axis=1)
    terms = jnp.concatenate([terms, jnp.zeros((128 - GROUP - 8, 1536), BF16)], axis=0)
    out = nt_dot(jnp.concatenate(narrow * 3, axis=1), terms)
    low = pltpu.roll(pltpu.roll(out, 1, 0), GROUP, 1)
    up = pltpu.roll(pltpu.roll(out, 127, 0), 2 * GROUP - 128, 1)
    pack_ref[pl.ds(0, 128, stride=2), :] = jnp.where(lane < GROUP, out, low)
    pack_ref[pl.ds(1, 128, stride=2), :] = jnp.where(lane < 2 * GROUP - 128, low, up)


def fill_halo(u_ref, up_ref, down_ref, mk):
    mat = TIME_STEP * LINES[2]
    sides = ((3, 2, UM, GM, up_ref), (0, -2, UP, GP, down_ref))

    def per_variable(v):
        for c in range(8):
            col = v * 8 + c
            u = [u_ref[rows8(col * 4 + k), :] for k in range(4)]
            for node, shift, near, slope, goal in sides:
                g = combine((SLOPE[node, b], u[b]) for b in range(4))
                near_u, near_g = rolled(u[node], shift), rolled(g, shift)
                for part, (row, a) in enumerate(((np.eye(4)[node], u[node]), (SLOPE[node], g))):
                    b = combine(
                        list(zip(row + row @ mat[:, :4], u))
                        + [(row @ mat[:, near], near_u), (row @ mat[:, slope], near_g)]
                    )
                    a = rolled(a, -shift)
                    tile = jnp.where(mk.l0, a, b) if node == 3 else jnp.where(mk.l0, b, a)
                    goal[rows8(part * COLS + col), :] = tile

    for v in range(VARS):
        per_variable(v)


def entry_kernel(
    route_hbm, slot_hbm, forces_hbm, coords_hbm, lists_hbm, state_hbm,
    pack_ref, u_ref, up_ref, down_ref, inv_ref, order,
    route_ref, slot_ref, forces_ref, coords_ref, lists_ref, state_ref, lhs, sems,
):
    sources = (route_hbm, slot_hbm, forces_hbm, coords_hbm, lists_hbm, state_hbm)
    targets = (route_ref, slot_ref, forces_ref, coords_ref, lists_ref, state_ref)
    copies = [
        pltpu.make_async_copy(a, b, sems.at[n]) for n, (a, b) in enumerate(zip(sources, targets))
    ]
    for copy in copies:
        copy.start()
    mk = Masks()
    for copy in copies[:5]:
        copy.wait()
    payload = [forces_ref[f : f + 1, :] for f in range(5)]
    payload += [coords_ref[f : f + 1, :] for f in range(3)]
    payload.append(slot_ref[...].astype(F32))
    pack_points(route_ref[...], payload, pack_ref)

    rows = [
        lists_ref[t // 2 : t // 2 + 1, (t % 2) * 128 : (t % 2) * 128 + 128] for t in range(4)
    ]
    fill_order(rows, order)
    copies[5].wait()
    for vi in range(VARS * 4):
        x = jnp.concatenate([state_ref[vi * 4 + j] for j in NODE_ROWS], axis=0)
        hi, lo = split2(x)
        lhs[vi * 16 : vi * 16 + 16, :] = hi
        lhs[320 + vi * 16 : 336 + vi * 16, :] = lo
    res = jnp.dot(lhs[...], order[...], preferred_element_type=F32)
    spread(both(res), u_ref, 0)

    place = lax.broadcasted_iota(jnp.int32, (16, 512), 1)
    digit = lax.broadcasted_iota(jnp.int32, (16, 512), 0)
    digits = jnp.where(digit == 0, place >> 4, place & 15).astype(F32).astype(BF16)
    where = nt_dot(digits, order[...])
    inv = where[0:1, :] * 16.0 + where[1:2, :]
    inv = [inv[:, t * 128 : t * 128 + 128] for t in range(4)]
    inv = jnp.concatenate(inv + inv, axis=0)
    inv_ref[...] = inv
    up_ref[2 * COLS * 8 :, :] = inv
    down_ref[2 * COLS * 8 :, :] = inv

    fill_halo(u_ref, up_ref, down_ref, mk)


def state_kernel(u_ref, before_ref, after_ref, base_ref, au, ag, hu, hg, m0):
    mk = Masks()
    mat = TIME_STEP * LINES[2]
    top, bottom = np.eye(4)[3], np.eye(4)[0]

    def unpack(col, carry):
        for part, (a, h) in enumerate(((au, hu), (ag, hg))):
            low = before_ref[rows8(part * COLS + col), :]
            high = after_ref[rows8(part * COLS + col), :]
            a[rows8(col), :] = jnp.where(mk.l0, low, high)
            h[rows8(col), :] = jnp.where(mk.l0, rolled(low, -2), rolled(high, 2))
        return carry

    lax.fori_loop(0, COLS, unpack, 0, unroll=8)
    apply_operator(u_ref, m0, au, ag, mk, TIME_STEP, 1.0)

    x_mat, coefs = TIME_STEP * LINES[0], y_coefs(mk, TIME_STEP * LINES[1])

    def halo(v, carry):
        for c in range(8):
            col = v * 8 + c
            u = [u_ref[rows8(col * 4 + k), :] for k in range(4)]
            g0 = combine((SLOPE[0, b], u[b]) for b in range(4))
            g3 = combine((SLOPE[3, b], u[b]) for b in range(4))
            for h, f_low, f_high in ((hu, top, bottom), (hg, SLOPE[3], SLOPE[0])):
                low = combine(((f_low @ mat[:, UP], u[0]), (f_low @ mat[:, GP], g0)))
                high = combine(((f_high @ mat[:, UM], u[3]), (f_high @ mat[:, GM], g3)))
                h[rows8(col), :] += jnp.where(mk.l0, low, high)
        for a, h in ((au, hu), (ag, hg)):
            for i in range(4):
                at = [rows8(v * 8 + 2 * i + jj) for jj in range(2)]
                new = y_line(a[at[0], :], a[at[1], :], mk, coefs)
                for jj in range(2):
                    h[at[jj], :] += new[jj]
            for jj in range(2):
                at = [rows8(v * 8 + 2 * i + jj) for i in range(4)]
                new = x_line([a[r, :] for r in at], mk, x_mat)
                for i in range(4):
                    h[at[i], :] += new[i]
        return carry

    lax.fori_loop(0, VARS, halo, 0)
    apply_operator(m0, base_ref, hu, hg, mk, 0.5 * TIME_STEP, 0.5)

    def finish(n, carry):
        base_ref[rows8(n), :] += 0.5 * u_ref[rows8(n), :]
        return carry

    lax.fori_loop(0, TILES, finish, 0, unroll=16)


def line_basis(coords):
    rows = []
    for a in range(4):
        term = None
        for k in range(4):
            if k != a:
                factor = (coords - NODE_POINTS[k]) * (1.0 / (NODE_POINTS[a] - NODE_POINTS[k]))
                term = factor if term is None else term * factor
        rows.append(term)
    return rows


def place_of(slots, table, row):
    number = slots.astype(jnp.int32)
    inner, outer = number & 127, number >> 7
    found = jnp.zeros((8, 128), F32)
    for t in range(4):
        line = jnp.broadcast_to(table[row + t : row + t + 1, :], (8, 128))
        found = jnp.where(outer == t, jnp.take_along_axis(line, inner, axis=1), found)
    return found.astype(jnp.int32)


def fill_hot(hot, place):
    ids = lax.broadcasted_iota(jnp.int32, (16, 128), 0)
    one, none = jnp.ones((16, 128), BF16), jnp.zeros((16, 128), BF16)
    rows = [jnp.broadcast_to(place[c : c + 1, :], (16, 128)).astype(jnp.int16) for c in range(CAP)]
    for first in range(0, hot.shape[0], 16):
        here = (ids + first).astype(jnp.int16)
        for c in range(CAP):
            hot[first : first + 16, c * 128 : c * 128 + 128] = jnp.where(here == rows[c], one, none)


def fill_terms(matrix, columns, nodes, strength, grid, group, first, count):
    if first == 0:
        for n, tile in enumerate(nodes):
            grid[group, n * 8 : n * 8 + 8, :] = tile
        for n, tile in enumerate(columns):
            strength[group, n * 8 : n * 8 + 8, :] = tile
    for c in range(CAP):
        here = slice(c * 128, c * 128 + 128)
        node_rows = grid[group, pl.ds(c, 16, stride=8), :]
        for n in range(first, first + count):
            hi, lo = split2(node_rows * strength[group, n * 8 + c : n * 8 + c + 1, :])
            at = (first + n) * 16
            matrix[at : at + 16, here] = hi
            matrix[at + count * 16 : at + count * 16 + 16, here] = lo


def trace_terms(field, node):
    bx, by, bz = [line_basis(field[5 + d]) for d in range(3)]
    slope = combine((SLOPE[node, b], bz[b]) for b in range(4))
    columns = [field[v] * bz[node] for v in range(VARS)]
    columns += [field[v] * slope for v in range(VARS)]
    pairs = [(i, j) for h in range(2) for i in range(4) for j in NODE_ROWS[2 * h : 2 * h + 2]]
    return columns, [by[j] * bx[i] for i, j in pairs]


SPANS = ((0, 3), (3, 2))


def source_kernel(
    pts_ref, inv_ref, before_ref, after_ref, base_ref, order, out_hbm,
    hot, hot_low, hot_up, lhs, lhs_low, lhs_up, grid, strength, su, sg, s_ref, new_ref,
    lhs_out, out_ref, sems,
):
    mk = Masks()
    halves = [pts_ref[pl.ds(h, 128, stride=2), :].T for h in range(2)]
    data = jnp.concatenate(halves, axis=0)
    field = [
        [data[g * GROUP + f * 8 : g * GROUP + f * 8 + 8] for f in range(FIELDS)] for g in range(3)
    ]
    bx, by, bz = [line_basis(field[0][5 + d]) for d in range(3)]
    columns = [field[0][v] * bx[i] for v in range(VARS) for i in range(4)]
    nodes = [by[j] * bz[k] for j in NODE_ROWS for k in range(4)]
    vals, traces, copies = {}, {}, []
    in_layer, across = operator_of(
        s_ref, new_ref, su, sg, mk, 0.5 * TIME_STEP * TIME_STEP, TIME_STEP
    )

    def gather(n):
        first, count = SPANS[n]
        fill_terms(lhs, columns, nodes, strength, grid, 0, first * 4, count * 4)
        vals[n] = both(nt_dot(lhs[first * 128 : (first + count) * 128, :], hot[...]))

    def gather_traces(side):
        matrix, goal = ((lhs_low, hot_low), (lhs_up, hot_up))[side]
        table, shift = ((before_ref, 256), (after_ref, 0))[side]
        fill_hot(goal, place_of(field[1 + side][8], table, 0) - shift)
        fill_terms(matrix, *trace_terms(field[1 + side], 3 - 3 * side), strength, grid, 1 + side, 0, 10)
        traces[side] = both(nt_dot(matrix[...], goal[...]))

    def spread_traces():
        for part, goal in ((0, su), (1, sg)):
            for v in range(VARS):
                for h in range(2):
                    at = (part * VARS + v) * 16 + h * 8
                    for t in range(4):
                        tile = traces[t // 2][at : at + 8, (t % 2) * 128 : (t % 2) * 128 + 128]
                        goal[pl.ds(v * 64 + h * 4 + t, 8, stride=8), :] = tile

    def advance(n, step):
        first, count = SPANS[n]
        if step is in_layer:
            spread(vals[n], s_ref, first * 4)
        for v in range(first, first + count):
            step(v)

    def put_back(n):
        first, count = SPANS[n]
        for vi in range(first * 4, (first + count) * 4):
            at = (first * 4 + vi) * 16
            for t in range(4):
                rows = [pl.ds(vi * 64 + h * 4 + t, 8, stride=8) for h in range(2)]
                x = jnp.concatenate([new_ref[r, :] + base_ref[r, :] for r in rows], axis=0)
                hi, lo = split2(x)
                lhs_out[at : at + 16, t * 128 : t * 128 + 128] = hi
                at_lo = at + count * 64
                lhs_out[at_lo : at_lo + 16, t * 128 : t * 128 + 128] = lo
        val = both(nt_dot(lhs_out[first * 128 : (first + count) * 128, :], order[...]))
        for vi in range(first * 4, (first + count) * 4):
            for m, j in enumerate(NODE_ROWS):
                at = (vi - first * 4) * 16 + m * 4
                out_ref[vi * 4 + j] = val[at : at + 4, :]
        part = pl.ds(first * 16, count * 16)
        copies.append(pltpu.make_async_copy(out_ref.at[part], out_hbm.at[part], sems.at[n]))
        copies[-1].start()

    fill_hot(hot, place_of(field[0][8], inv_ref, 0))
    gather(0)
    gather_traces(0)
    gather_traces(1)
    gather(1)
    advance(0, in_layer)
    spread_traces()
    advance(0, across)
    advance(1, in_layer)
    put_back(0)
    advance(1, across)
    put_back(1)
    for copy in copies:
        copy.wait()


def call(kernel, outs, scratch, specs, place=pltpu.VMEM):
    return pl.pallas_call(
        kernel,
        out_shape=outs,
        in_specs=specs,
        out_specs=jax.tree.map(lambda _: pl.BlockSpec(memory_space=place), outs),
        scratch_shapes=scratch,
        compiler_params=pltpu.CompilerParams(vmem_limit_bytes=VMEM_LIMIT),
    )


def tile_array(count):
    return jax.ShapeDtypeStruct((count * 8, 128), F32)


VMEM = pl.BlockSpec(memory_space=pltpu.VMEM)


def entry_call(route, slots, forces, coords, lists, state):
    arrays = (route, slots, forces, coords, lists, state)
    return call(
        entry_kernel,
        (
            jax.ShapeDtypeStruct((256, 128), F32),
            tile_array(TILES),
            tile_array(2 * COLS + 1),
            tile_array(2 * COLS + 1),
            tile_array(1),
            jax.ShapeDtypeStruct((512, 512), BF16),
        ),
        [pltpu.VMEM(x.shape, x.dtype) for x in arrays]
        + [
            pltpu.VMEM((640, 512), BF16),
            pltpu.SemaphoreType.DMA((6,)),
        ],
        [pl.BlockSpec(memory_space=pltpu.HBM)] * 6,
    )(*[pltpu.with_memory_space_constraint(x, pltpu.HBM) for x in arrays])


def state_call(u, before, after):
    cols = pltpu.VMEM((COLS * 8, 128), F32)
    return call(
        state_kernel,
        tile_array(TILES),
        [cols, cols, cols, cols, pltpu.VMEM((TILES * 8, 128), F32)],
        [VMEM] * 3,
    )(u, before, after)


def source_call(pts, inv, before, after, base, order):
    cols = pltpu.VMEM((COLS * 8, 128), F32)
    field = pltpu.VMEM((TILES * 8, 128), F32)
    return call(
        source_kernel,
        jax.ShapeDtypeStruct((VARS * 16, 4, 512), F32),
        [
            pltpu.VMEM((512, 1024), BF16),
            pltpu.VMEM((256, 1024), BF16),
            pltpu.VMEM((256, 1024), BF16),
            pltpu.VMEM((640, 1024), BF16),
            pltpu.VMEM((320, 1024), BF16),
            pltpu.VMEM((320, 1024), BF16),
            pltpu.VMEM((3, 128, 128), F32),
            pltpu.VMEM((3, 160, 128), F32),
            cols,
            cols,
            field,
            field,
            pltpu.VMEM((640, 512), BF16),
            pltpu.VMEM((VARS * 16, 4, 512), F32),
            pltpu.SemaphoreType.DMA((2,)),
        ],
        [VMEM] * 6,
        pltpu.HBM,
    )(pts, inv, before, after, base, order)


def on_device(state, neighbour_map, layer_lists, forces, positions, route, element_slot):
    count = lax.axis_size("sfc")
    forward = [(d, (d + 1) % count) for d in range(count)]
    backward = [(target, source) for source, target in forward]
    pack, u, up, down, inv, order = entry_call(
        route.reshape(1, -1),
        element_slot.reshape(1, -1),
        forces,
        positions,
        layer_lists,
        state.reshape(VARS * 16, 4, -1),
    )
    before = lax.ppermute(up, "sfc", forward)
    after = lax.ppermute(down, "sfc", backward)
    pts = lax.all_to_all(pack, "sfc", split_axis=0, concat_axis=0, tiled=True)
    base = state_call(u, before, after)
    table = slice(2 * COLS * 8, None)
    out = source_call(pts, inv, before[table], after[table], base, order)
    return out.reshape(state.shape)


def solution(mesh):
    in_specs = (
        P(None, None, None, None, "sfc"),
        P(None, "sfc"),
        P(None, "sfc"),
        P(None, "sfc"),
        P(None, "sfc"),
        P("sfc", None),
        P("sfc"),
    )
    out_specs = P(None, None, None, None, "sfc")
    return jax.shard_map(
        on_device, mesh=mesh, in_specs=in_specs, out_specs=out_specs, check_vma=False
    )
```

```python
import functools

import jax
import jax.numpy as jnp
import numpy as np
from jax import lax
from jax.experimental import pallas as pl
from jax.experimental.pallas import tpu as pltpu
from jax.sharding import PartitionSpec as P

NODE_POINTS = (-1.0, -0.4472135954999579, 0.4472135954999579, 1.0)
GSCALE = 2.0
HALF_LIFT = 6.0
ADVECT = (0.6, -0.4, 0.8)
VISCOSITY = 0.02
TIME_STEP = 0.04

VARS = 5
CAP = 8
FIELDS = 9
GROUP = FIELDS * CAP
COLS = VARS * 4 * 2
TILES = COLS * 4
HALO_TILES = COLS * 3
VMEM_LIMIT = 24 * 1024 * 1024
F32 = jnp.float32
BF16 = jnp.bfloat16


def diff_table():
    factor = [
        float(np.prod([NODE_POINTS[a] - NODE_POINTS[k] for k in range(4) if k != a]))
        for a in range(4)
    ]
    table = np.zeros((4, 4))
    for a in range(4):
        for b in range(4):
            if a != b:
                table[a, b] = factor[a] / factor[b] / (NODE_POINTS[a] - NODE_POINTS[b])
            else:
                table[a, b] = sum(
                    (1.0 / (NODE_POINTS[a] - NODE_POINTS[k]) for k in range(4) if k != a)
                )
    return table


SLOPE = GSCALE * diff_table()


def line_operator(direction):
    a, nu = ADVECT[direction], VISCOSITY
    out = np.zeros((4, 8))
    for col in range(8):
        value = np.zeros(8)
        value[col] = 1.0
        u, (um, gm, up, gp) = value[:4], value[4:]
        q = SLOPE @ u
        q[0] -= HALF_LIFT * (um - u[0])
        q[3] += HALF_LIFT * (up - u[3])
        qm = gm + HALF_LIFT * (u[0] - um)
        qp = gp - HALF_LIFT * (u[3] - up)
        res = -SLOPE @ (a * u - nu * q)
        for node, normal, ou, oq in ((0, -1.0, um, qm), (3, 1.0, up, qp)):
            along = normal * a
            res[node] += -HALF_LIFT * (along - abs(along)) * (ou - u[node])
            res[node] += HALF_LIFT * nu * normal * (oq - q[node])
        out[:, col] = res
    return out


LINES = [line_operator(d) for d in range(3)]
UM, GM, UP, GP = 4, 5, 6, 7


def rolled(x, shift):
    return pltpu.roll(x, shift % 8, 0)


def lanes(x, shift):
    return pltpu.roll(x, shift % 128, 1)


def combine(pairs):
    total = None
    for coef, value in pairs:
        if isinstance(coef, (float, np.floating)):
            if coef == 0.0:
                continue
            term = value if coef == 1.0 else value * float(coef)
        else:
            term = value * coef
        total = term if total is None else total + term
    return total


class Masks:
    def __init__(self):
        sub = lax.broadcasted_iota(jnp.int32, (8, 128), 0)
        lane = lax.broadcasted_iota(jnp.int32, (8, 128), 1)
        self.h0 = sub < 4
        self.l0 = (sub & 2) == 0
        self.r0 = (sub & 1) == 0
        self.x_first = (lane & 15) == 0
        self.x_last = (lane & 15) == 15
        self.y_wrap = (self.h0 & (lane < 16)) | (~self.h0 & (lane >= 112))
        self.sign = jnp.where(self.h0, 1.0, -1.0).astype(F32)

    def by_layer(self, low, high):
        return jnp.where(self.l0, float(low), float(high)).astype(F32)

    def by_half(self, low, high):
        if low == high:
            return float(low)
        return jnp.where(self.h0, float(low), float(high)).astype(F32)


def rows8(index, pitch=8):
    if isinstance(index, int):
        return slice(index * pitch, index * pitch + 8)
    if pitch != 8:
        return pl.ds(index * pitch, 8)
    return pl.ds(pl.multiple_of(index * 8, 8), 8)


def x_line(u, mk, mat):
    g0 = combine((SLOPE[0, b], u[b]) for b in range(4))
    g3 = combine((SLOPE[3, b], u[b]) for b in range(4))

    def before(t):
        return jnp.where(mk.x_first, lanes(t, -15), lanes(t, 1))

    def after(t):
        return jnp.where(mk.x_last, lanes(t, 15), lanes(t, -1))

    um, gm, up, gp = before(u[3]), before(g3), after(u[0]), after(g0)
    terms = list(u) + [um, gm, up, gp]
    return [combine((mat[a, c], terms[c]) for c in range(8)) for a in range(4)]


def y_coefs(mk, mat):
    out = []
    for jj in range(2):
        o = 3 - jj
        row = [mk.by_half(mat[jj, b], mat[o, 3 - b]) for b in range(4)]
        row.append(mk.by_half(mat[jj, UM], mat[o, UP]))
        row.append(mk.by_half(mat[jj, UP], mat[o, UM]))
        row.append(mk.by_half(mat[jj, GM], mat[o, GP]))
        out.append(row)
    return out


def y_line(u0, u1, mk, coefs):
    r0, r1 = rolled(u0, 4), rolled(u1, 4)
    g = combine(((SLOPE[0, 0], u0), (SLOPE[0, 1], u1), (SLOPE[0, 2], r1), (SLOPE[0, 3], r0)))
    g = rolled(g * mk.sign, 4)

    def outer(t):
        near = jnp.where(mk.h0, lanes(t, 16), lanes(t, -16))
        far = jnp.where(mk.r0, rolled(near, -1), rolled(near, 1))
        return jnp.where(mk.y_wrap, far, near)

    n, gn = outer(r0), outer(g)
    nr = rolled(n, 4)
    return [
        combine(zip(coefs[0], (u0, u1, r1, r0, n, nr, gn))),
        combine(zip(coefs[1][:6], (u0, u1, r1, r0, n, nr))),
    ]


def z_line(u, hu, hg, mk, mat):
    g0 = combine((SLOPE[0, b], u[b]) for b in range(4))
    g3 = combine((SLOPE[3, b], u[b]) for b in range(4))
    um = jnp.where(mk.l0, hu, rolled(u[3], 2))
    gm = jnp.where(mk.l0, hg, rolled(g3, 2))
    up = jnp.where(mk.l0, rolled(u[0], -2), hu)
    gp = jnp.where(mk.l0, rolled(g0, -2), hg)
    terms = list(u) + [um, gm, up, gp]
    return [combine((mat[a, c], terms[c]) for c in range(8)) for a in range(4)]


def operator_of(src, dst, hu, hg, mk, scale, ident, base=None, pitches=(8, 8)):
    mats = [scale * m for m in LINES]
    mats[2][:, :4] += ident * np.eye(4)
    coefs = y_coefs(mk, mats[1])

    def read(index):
        return src[rows8(index, pitches[0]), :]

    def at_goal(index):
        return rows8(index, pitches[1])

    def in_layer(v):
        col = v * 8
        for jj in range(2):
            for k in range(4):
                at = [(col + 2 * i + jj) * 4 + k for i in range(4)]
                new = x_line([read(n) for n in at], mk, mats[0])
                for i in range(4):
                    dst[at_goal(at[i]), :] = new[i]
        for i in range(4):
            for k in range(4):
                at = [(col + 2 * i + jj) * 4 + k for jj in range(2)]
                new = y_line(read(at[0]), read(at[1]), mk, coefs)
                for jj in range(2):
                    dst[at_goal(at[jj]), :] += new[jj]

    def across(v):
        col = v * 8
        for c in range(8):
            at = [(col + c) * 4 + k for k in range(4)]
            new = z_line(
                [read(n) for n in at], hu[rows8(col + c), :], hg[rows8(col + c), :], mk, mats[2]
            )
            for k in range(4):
                more = new[k] if base is None else new[k] + base[rows8(at[k]), :]
                dst[at_goal(at[k]), :] += more

    return in_layer, across


def apply_operator(*args, **options):
    in_layer, across = operator_of(*args, **options)

    def body(v, carry):
        in_layer(v)
        across(v)
        return carry

    lax.fori_loop(0, VARS, body, 0)


def split2(x):
    hi = x.astype(BF16)
    return hi, (x - hi.astype(F32)).astype(BF16)


def both(res):
    half = res.shape[0] // 2
    return res[:half] + res[half:]


NODE_ROWS = (0, 1, 3, 2)


PITCH = 12


def spread(val, goal, first, pitch=8):
    for vi in range(val.shape[0] // 16):
        for h in range(2):
            for t in range(4):
                tile = val[vi * 16 + h * 8 : vi * 16 + h * 8 + 8, t * 128 : t * 128 + 128]
                goal[pl.ds((first + vi) * 8 * pitch + h * 4 + t, 8, stride=pitch), :] = tile


def nt_dot(a, b):
    return lax.dot_general(a, b, (((1,), (1,)), ((), ())), preferred_element_type=F32)


def fill_order(rows, order):
    ids = lax.broadcasted_iota(jnp.int32, (16, 128), 0)
    one, none = jnp.ones((16, 128), BF16), jnp.zeros((16, 128), BF16)
    rows = [jnp.broadcast_to(row, (16, 128)).astype(jnp.int16) for row in rows]
    for first in range(0, 512, 16):
        here = (ids + first).astype(jnp.int16)
        for t in range(4):
            found = jnp.where(here == rows[t], one, none)
            order[first : first + 16, t * 128 : t * 128 + 128] = found


def pack_points(route, payload, pack_ref):
    dest = lax.broadcasted_iota(jnp.int32, (128, 128), 0)
    lane = lax.broadcasted_iota(jnp.int32, (128, 128), 1)
    slot = lax.broadcasted_iota(jnp.int32, (8, 128), 0).astype(F32)
    to_device = [jnp.where(dest == route[:, t * 128 : t * 128 + 128], 1.0, 0.0) for t in range(4)]
    narrow = [x.astype(BF16) for x in to_device]
    before = jnp.where(dest < lane, 1.0, 0.0).astype(BF16)
    steps = jnp.concatenate([before, jnp.ones((128, 128), BF16)], axis=1)
    counts = jnp.dot(jnp.concatenate(narrow, axis=0), steps, preferred_element_type=F32)
    base = None
    parts = [[], [], []]
    for t in range(4):
        here = slice(t * 128, t * 128 + 128)
        count = counts[here, :128] if base is None else counts[here, :128] + base
        base = counts[here, 128:] if base is None else base + counts[here, 128:]
        within = jnp.sum(count * to_device[t], axis=0, keepdims=True)
        chosen = slot == within
        rows = [jnp.where(chosen, p[:, here], 0.0) for p in payload]
        rows.append(jnp.zeros((8, 128), F32))
        rest = jnp.concatenate(rows, axis=0)
        for part in parts:
            part.append(rest.astype(BF16))
            rest = rest - part[-1].astype(F32)
    terms = jnp.concatenate([jnp.concatenate(part, axis=1) for part in parts], axis=1)
    terms = jnp.concatenate([terms, jnp.zeros((128 - GROUP - 8, 1536), BF16)], axis=0)
    out = nt_dot(jnp.concatenate(narrow * 3, axis=1), terms)
    low = pltpu.roll(pltpu.roll(out, 1, 0), GROUP, 1)
    up = pltpu.roll(pltpu.roll(out, 127, 0), 2 * GROUP - 128, 1)
    pack_ref[pl.ds(0, 128, stride=2), :] = jnp.where(lane < GROUP, out, low)
    pack_ref[pl.ds(1, 128, stride=2), :] = jnp.where(lane < 2 * GROUP - 128, low, up)


def fill_halo(u_ref, up_ref, down_ref, mk):
    for col in range(COLS):
        u = [u_ref[rows8(col * 4 + k), :] for k in range(4)]
        g0 = combine((SLOPE[0, b], u[b]) for b in range(4))
        g3 = combine((SLOPE[3, b], u[b]) for b in range(4))
        ups = ((rolled(u[0], -2), u[1]), (rolled(u[2], -2), u[3]), (u[3], rolled(g3, 2)))
        downs = ((u[0], rolled(u[1], 2)), (u[2], rolled(u[3], 2)), (rolled(u[0], -2), g0))
        for part in range(3):
            up_ref[rows8(part * COLS + col), :] = jnp.where(mk.l0, *ups[part])
            down_ref[rows8(part * COLS + col), :] = jnp.where(mk.l0, *downs[part])


def entry_kernel(
    route_hbm, slot_hbm, forces_hbm, coords_hbm, lists_hbm, state_hbm,
    pack_ref, u_ref, up_ref, down_ref, inv_ref, order,
    route_ref, slot_ref, forces_ref, coords_ref, lists_ref, state_ref, lhs, sems,
):
    sources = (route_hbm, slot_hbm, forces_hbm, coords_hbm, lists_hbm, state_hbm)
    targets = (route_ref, slot_ref, forces_ref, coords_ref, lists_ref, state_ref)
    copies = [
        pltpu.make_async_copy(a, b, sems.at[n]) for n, (a, b) in enumerate(zip(sources, targets))
    ]
    for copy in copies:
        copy.start()
    mk = Masks()
    for copy in copies[:5]:
        copy.wait()
    payload = [forces_ref[f : f + 1, :] for f in range(5)]
    payload += [coords_ref[f : f + 1, :] for f in range(3)]
    payload.append(slot_ref[...].astype(F32))
    pack_points(route_ref[...], payload, pack_ref)

    rows = [
        lists_ref[t // 2 : t // 2 + 1, (t % 2) * 128 : (t % 2) * 128 + 128] for t in range(4)
    ]
    fill_order(rows, order)
    copies[5].wait()
    for vi in range(VARS * 4):
        x = jnp.concatenate([state_ref[vi * 4 + j] for j in NODE_ROWS], axis=0)
        hi, lo = split2(x)
        lhs[vi * 16 : vi * 16 + 16, :] = hi
        lhs[320 + vi * 16 : 336 + vi * 16, :] = lo
    res = jnp.dot(lhs[...], order[...], preferred_element_type=F32)
    spread(both(res), u_ref, 0)

    place = lax.broadcasted_iota(jnp.int32, (16, 512), 1)
    digit = lax.broadcasted_iota(jnp.int32, (16, 512), 0)
    digits = jnp.where(digit == 0, place >> 4, place & 15).astype(F32).astype(BF16)
    where = nt_dot(digits, order[...])
    inv = where[0:1, :] * 16.0 + where[1:2, :]
    inv = [inv[:, t * 128 : t * 128 + 128] for t in range(4)]
    inv = jnp.concatenate(inv + inv, axis=0)
    inv_ref[...] = inv
    up_ref[HALO_TILES * 8 :, :] = inv
    down_ref[HALO_TILES * 8 :, :] = inv

    fill_halo(u_ref, up_ref, down_ref, mk)


def state_kernel(u_ref, before_ref, after_ref, base_ref, au, ag, hu, hg, m0):
    mk = Masks()
    mat = TIME_STEP * LINES[2]
    top, bottom = np.eye(4)[3], np.eye(4)[0]

    def layered(row_low, row_high, near):
        order = ((0, 1), (1, 0), (2, 3), (3, 2)) + (((UM, UP), (GM, GP)) if near else ())
        return [mk.by_layer(row_low[low], row_high[high]) for low, high in order]

    step = np.eye(4, 8) + mat
    slopes = layered(SLOPE[3], SLOPE[0], False)
    later = layered(step[3], step[0], True)
    later_slopes = layered(SLOPE[3] @ step, SLOPE[0] @ step, True)

    def unpack(v, carry):
        for c in range(8):
            col = v * 8 + c
            low = [before_ref[rows8(part * COLS + col), :] for part in range(3)]
            high = [after_ref[rows8(part * COLS + col), :] for part in range(3)]
            tiles = []
            for part in range(2):
                tiles.append(jnp.where(mk.l0, low[part], high[part]))
                tiles.append(jnp.where(mk.l0, rolled(low[part], -2), rolled(high[part], 2)))
            tiles.append(jnp.where(mk.l0, low[2], rolled(high[2], 2)))
            tiles.append(jnp.where(mk.l0, rolled(low[2], -2), high[2]))
            at = rows8(col)
            au[at, :] = jnp.where(mk.l0, tiles[3], tiles[1])
            ag[at, :] = combine(zip(slopes, tiles))
            hu[at, :] = combine(zip(later, tiles))
            hg[at, :] = combine(zip(later_slopes, tiles))
        return carry

    lax.fori_loop(0, VARS, unpack, 0)
    apply_operator(u_ref, m0, au, ag, mk, TIME_STEP, 1.0, pitches=(8, 8))

    x_mat, coefs = TIME_STEP * LINES[0], y_coefs(mk, TIME_STEP * LINES[1])

    def halo(v, carry):
        for c in range(8):
            col = v * 8 + c
            u = [u_ref[rows8(col * 4 + k), :] for k in range(4)]
            g0 = combine((SLOPE[0, b], u[b]) for b in range(4))
            g3 = combine((SLOPE[3, b], u[b]) for b in range(4))
            for h, f_low, f_high in ((hu, top, bottom), (hg, SLOPE[3], SLOPE[0])):
                low = combine(((f_low @ mat[:, UP], u[0]), (f_low @ mat[:, GP], g0)))
                high = combine(((f_high @ mat[:, UM], u[3]), (f_high @ mat[:, GM], g3)))
                h[rows8(col), :] += jnp.where(mk.l0, low, high)
        for a, h in ((au, hu), (ag, hg)):
            for i in range(4):
                at = [rows8(v * 8 + 2 * i + jj) for jj in range(2)]
                new = y_line(a[at[0], :], a[at[1], :], mk, coefs)
                for jj in range(2):
                    h[at[jj], :] += new[jj]
            for jj in range(2):
                at = [rows8(v * 8 + 2 * i + jj) for i in range(4)]
                new = x_line([a[r, :] for r in at], mk, x_mat)
                for i in range(4):
                    h[at[i], :] += new[i]
        return carry

    lax.fori_loop(0, VARS, halo, 0)
    apply_operator(m0, base_ref, hu, hg, mk, 0.5 * TIME_STEP, 0.5)

    def finish(n, carry):
        base_ref[rows8(n), :] += 0.5 * u_ref[rows8(n), :]
        return carry

    lax.fori_loop(0, TILES, finish, 0, unroll=16)


def line_basis(coords):
    rows = []
    for a in range(4):
        term = None
        for k in range(4):
            if k != a:
                factor = (coords - NODE_POINTS[k]) * (1.0 / (NODE_POINTS[a] - NODE_POINTS[k]))
                term = factor if term is None else term * factor
        rows.append(term)
    return rows


def place_of(slots, table, row):
    number = slots.astype(jnp.int32)
    inner, outer = number & 127, number >> 7
    found = jnp.zeros((8, 128), F32)
    for t in range(4):
        line = jnp.broadcast_to(table[row + t : row + t + 1, :], (8, 128))
        found = jnp.where(outer == t, jnp.take_along_axis(line, inner, axis=1), found)
    return found.astype(jnp.int32)


def fill_hot(hot, place):
    ids = lax.broadcasted_iota(jnp.int32, (16, 128), 0)
    one, none = jnp.ones((16, 128), BF16), jnp.zeros((16, 128), BF16)
    rows = [jnp.broadcast_to(place[c : c + 1, :], (16, 128)).astype(jnp.int16) for c in range(CAP)]
    for first in range(0, hot.shape[0], 16):
        here = (ids + first).astype(jnp.int16)
        for c in range(CAP):
            hot[first : first + 16, c * 128 : c * 128 + 128] = jnp.where(here == rows[c], one, none)


def fill_terms(matrix, columns, nodes, strength, grid, group, first, count):
    if first == 0:
        for n, tile in enumerate(nodes):
            grid[group, n * 8 : n * 8 + 8, :] = tile
        for n, tile in enumerate(columns):
            strength[group, n * 8 : n * 8 + 8, :] = tile
    for c in range(CAP):
        here = slice(c * 128, c * 128 + 128)
        node_rows = grid[group, pl.ds(c, 16, stride=8), :]
        for n in range(first, first + count):
            hi, lo = split2(node_rows * strength[group, n * 8 + c : n * 8 + c + 1, :])
            at = (first + n) * 16
            matrix[at : at + 16, here] = hi
            matrix[at + count * 16 : at + count * 16 + 16, here] = lo


def trace_terms(field, node):
    bx, by, bz = [line_basis(field[5 + d]) for d in range(3)]
    slope = combine((SLOPE[node, b], bz[b]) for b in range(4))
    columns = [field[v] * bz[node] for v in range(VARS)]
    columns += [field[v] * slope for v in range(VARS)]
    pairs = [(i, j) for h in range(2) for i in range(4) for j in NODE_ROWS[2 * h : 2 * h + 2]]
    return columns, [by[j] * bx[i] for i, j in pairs]


SPANS = ((0, 3), (3, 2))
BACK = ((0, 3), (3, 2))


def source_kernel(
    pts_ref, inv_ref, before_ref, after_ref, base_ref, order, out_hbm,
    hot, hot_low, hot_up, lhs, lhs_low, lhs_up, grid, strength, su, sg, s_ref, new_ref,
    lhs_out, out_ref, sems,
):
    mk = Masks()
    halves = [pts_ref[pl.ds(h, 128, stride=2), :].T for h in range(2)]
    data = jnp.concatenate(halves, axis=0)
    field = [
        [data[g * GROUP + f * 8 : g * GROUP + f * 8 + 8] for f in range(FIELDS)] for g in range(3)
    ]
    bx, by, bz = [line_basis(field[0][5 + d]) for d in range(3)]
    columns = [field[0][v] * bx[i] for v in range(VARS) for i in range(4)]
    nodes = [by[j] * bz[k] for j in NODE_ROWS for k in range(4)]
    vals, traces, copies = {}, {}, []
    in_layer, across = operator_of(
        s_ref, new_ref, su, sg, mk, 0.5 * TIME_STEP * TIME_STEP, TIME_STEP, base_ref, (PITCH, PITCH)
    )

    def gather(n):
        first, count = SPANS[n]
        fill_terms(lhs, columns, nodes, strength, grid, 0, first * 4, count * 4)
        vals[n] = both(nt_dot(lhs[first * 128 : (first + count) * 128, :], hot[...]))

    def gather_traces(side):
        matrix, goal = ((lhs_low, hot_low), (lhs_up, hot_up))[side]
        table, shift = ((before_ref, 256), (after_ref, 0))[side]
        fill_hot(goal, place_of(field[1 + side][8], table, 0) - shift)
        fill_terms(matrix, *trace_terms(field[1 + side], 3 - 3 * side), strength, grid, 1 + side, 0, 10)
        traces[side] = both(nt_dot(matrix[...], goal[...]))

    def spread_traces():
        for part, goal in ((0, su), (1, sg)):
            for v in range(VARS):
                for h in range(2):
                    at = (part * VARS + v) * 16 + h * 8
                    for t in range(4):
                        tile = traces[t // 2][at : at + 8, (t % 2) * 128 : (t % 2) * 128 + 128]
                        goal[pl.ds(v * 64 + h * 4 + t, 8, stride=8), :] = tile

    def advance(n, step):
        first, count = SPANS[n]
        if step is in_layer:
            spread(vals[n], s_ref, first * 4, PITCH)
        for v in range(first, first + count):
            step(v)

    def put_back(n):
        first, count = SPANS[n]
        for vi in range(first * 4, (first + count) * 4):
            at = (first * 4 + vi) * 16
            for t in range(4):
                rows = [pl.ds(vi * 8 * PITCH + h * 4 + t, 8, stride=PITCH) for h in range(2)]
                x = jnp.concatenate([new_ref[r, :] for r in rows], axis=0)
                hi, lo = split2(x)
                lhs_out[at : at + 16, t * 128 : t * 128 + 128] = hi
                at_lo = at + count * 64
                lhs_out[at_lo : at_lo + 16, t * 128 : t * 128 + 128] = lo
        val = both(nt_dot(lhs_out[first * 128 : (first + count) * 128, :], order[...]))
        for vi in range(first * 4, (first + count) * 4):
            for m, j in enumerate(NODE_ROWS):
                at = (vi - first * 4) * 16 + m * 4
                out_ref[vi * 4 + j] = val[at : at + 4, :]
        part = pl.ds(first * 16, count * 16)
        copies.append(pltpu.make_async_copy(out_ref.at[part], out_hbm.at[part], sems.at[n]))
        copies[-1].start()

    fill_hot(hot, place_of(field[0][8], inv_ref, 0))
    gather(0)
    gather_traces(0)
    gather_traces(1)
    gather(1)
    advance(0, in_layer)
    spread_traces()
    advance(0, across)
    advance(1, in_layer)
    put_back(0)
    advance(1, across)
    put_back(1)
    for copy in copies:
        copy.wait()


def call(kernel, outs, scratch, specs, place=pltpu.VMEM):
    return pl.pallas_call(
        kernel,
        out_shape=outs,
        in_specs=specs,
        out_specs=jax.tree.map(lambda _: pl.BlockSpec(memory_space=place), outs),
        scratch_shapes=scratch,
        compiler_params=pltpu.CompilerParams(vmem_limit_bytes=VMEM_LIMIT),
    )


def tile_array(count):
    return jax.ShapeDtypeStruct((count * 8, 128), F32)


VMEM = pl.BlockSpec(memory_space=pltpu.VMEM)


def entry_call(route, slots, forces, coords, lists, state):
    arrays = (route, slots, forces, coords, lists, state)
    return call(
        entry_kernel,
        (
            jax.ShapeDtypeStruct((256, 128), F32),
            tile_array(TILES),
            tile_array(HALO_TILES + 1),
            tile_array(HALO_TILES + 1),
            tile_array(1),
            jax.ShapeDtypeStruct((512, 512), BF16),
        ),
        [pltpu.VMEM(x.shape, x.dtype) for x in arrays]
        + [
            pltpu.VMEM((640, 512), BF16),
            pltpu.SemaphoreType.DMA((6,)),
        ],
        [pl.BlockSpec(memory_space=pltpu.HBM)] * 6,
    )(*[pltpu.with_memory_space_constraint(x, pltpu.HBM) for x in arrays])


def state_call(u, before, after):
    cols = pltpu.VMEM((COLS * 8, 128), F32)
    return call(
        state_kernel,
        tile_array(TILES),
        [cols, cols, cols, cols, pltpu.VMEM((TILES * 8, 128), F32)],
        [VMEM] * 3,
    )(u, before, after)


def source_call(pts, inv, before, after, base, order):
    cols = pltpu.VMEM((COLS * 8, 128), F32)
    field = pltpu.VMEM((TILES * PITCH, 128), F32)
    return call(
        source_kernel,
        jax.ShapeDtypeStruct((VARS * 16, 4, 512), F32),
        [
            pltpu.VMEM((512, 1024), BF16),
            pltpu.VMEM((256, 1024), BF16),
            pltpu.VMEM((256, 1024), BF16),
            pltpu.VMEM((640, 1024), BF16),
            pltpu.VMEM((320, 1024), BF16),
            pltpu.VMEM((320, 1024), BF16),
            pltpu.VMEM((3, 128, 128), F32),
            pltpu.VMEM((3, 160, 128), F32),
            cols,
            cols,
            field,
            field,
            pltpu.VMEM((640, 512), BF16),
            pltpu.VMEM((VARS * 16, 4, 512), F32),
            pltpu.SemaphoreType.DMA((2,)),
        ],
        [VMEM] * 6,
        pltpu.HBM,
    )(pts, inv, before, after, base, order)


def on_device(state, neighbour_map, layer_lists, forces, positions, route, element_slot):
    count = lax.axis_size("sfc")
    forward = [(d, (d + 1) % count) for d in range(count)]
    backward = [(target, source) for source, target in forward]
    pack, u, up, down, inv, order = entry_call(
        route.reshape(1, -1),
        element_slot.reshape(1, -1),
        forces,
        positions,
        layer_lists,
        state.reshape(VARS * 16, 4, -1),
    )
    before = lax.ppermute(up, "sfc", forward)
    after = lax.ppermute(down, "sfc", backward)
    pts = lax.all_to_all(pack, "sfc", split_axis=0, concat_axis=0, tiled=True)
    base = state_call(u, before, after)
    table = slice(HALO_TILES * 8, None)
    out = source_call(pts, inv, before[table], after[table], base, order)
    return out.reshape(state.shape)


def solution(mesh):
    in_specs = (
        P(None, None, None, None, "sfc"),
        P(None, "sfc"),
        P(None, "sfc"),
        P(None, "sfc"),
        P(None, "sfc"),
        P("sfc", None),
        P("sfc"),
    )
    out_specs = P(None, None, None, None, "sfc")
    return jax.shard_map(
        on_device, mesh=mesh, in_specs=in_specs, out_specs=out_specs, check_vma=False
    )
```

```python
import functools

import jax
import jax.numpy as jnp
import numpy as np
from jax import lax
from jax.experimental import pallas as pl
from jax.experimental.pallas import tpu as pltpu
from jax.sharding import PartitionSpec as P

NODE_POINTS = (-1.0, -0.4472135954999579, 0.4472135954999579, 1.0)
GSCALE = 2.0
HALF_LIFT = 6.0
ADVECT = (0.6, -0.4, 0.8)
VISCOSITY = 0.02
TIME_STEP = 0.04

VARS = 5
CAP = 8
FIELDS = 9
GROUP = FIELDS * CAP
COLS = VARS * 4 * 2
TILES = COLS * 4
HALO_TILES = COLS * 3
VMEM_LIMIT = 24 * 1024 * 1024
F32 = jnp.float32
BF16 = jnp.bfloat16


def diff_table():
    factor = [
        float(np.prod([NODE_POINTS[a] - NODE_POINTS[k] for k in range(4) if k != a]))
        for a in range(4)
    ]
    table = np.zeros((4, 4))
    for a in range(4):
        for b in range(4):
            if a != b:
                table[a, b] = factor[a] / factor[b] / (NODE_POINTS[a] - NODE_POINTS[b])
            else:
                table[a, b] = sum(
                    (1.0 / (NODE_POINTS[a] - NODE_POINTS[k]) for k in range(4) if k != a)
                )
    return table


SLOPE = GSCALE * diff_table()


def line_operator(direction):
    a, nu = ADVECT[direction], VISCOSITY
    out = np.zeros((4, 8))
    for col in range(8):
        value = np.zeros(8)
        value[col] = 1.0
        u, (um, gm, up, gp) = value[:4], value[4:]
        q = SLOPE @ u
        q[0] -= HALF_LIFT * (um - u[0])
        q[3] += HALF_LIFT * (up - u[3])
        qm = gm + HALF_LIFT * (u[0] - um)
        qp = gp - HALF_LIFT * (u[3] - up)
        res = -SLOPE @ (a * u - nu * q)
        for node, normal, ou, oq in ((0, -1.0, um, qm), (3, 1.0, up, qp)):
            along = normal * a
            res[node] += -HALF_LIFT * (along - abs(along)) * (ou - u[node])
            res[node] += HALF_LIFT * nu * normal * (oq - q[node])
        out[:, col] = res
    return out


LINES = [line_operator(d) for d in range(3)]
UM, GM, UP, GP = 4, 5, 6, 7


def rolled(x, shift):
    return pltpu.roll(x, shift % 8, 0)


def lanes(x, shift):
    return pltpu.roll(x, shift % 128, 1)


def combine(pairs):
    total = None
    for coef, value in pairs:
        if isinstance(coef, (float, np.floating)):
            if coef == 0.0:
                continue
            term = value if coef == 1.0 else value * float(coef)
        else:
            term = value * coef
        total = term if total is None else total + term
    return total


class Masks:
    def __init__(self):
        sub = lax.broadcasted_iota(jnp.int32, (8, 128), 0)
        lane = lax.broadcasted_iota(jnp.int32, (8, 128), 1)
        self.h0 = sub < 4
        self.l0 = (sub & 2) == 0
        self.r0 = (sub & 1) == 0
        self.x_first = (lane & 15) == 0
        self.x_last = (lane & 15) == 15
        self.y_wrap = (self.h0 & (lane < 16)) | (~self.h0 & (lane >= 112))
        self.sign = jnp.where(self.h0, 1.0, -1.0).astype(F32)

    def by_layer(self, low, high):
        return jnp.where(self.l0, float(low), float(high)).astype(F32)

    def by_half(self, low, high):
        if low == high:
            return float(low)
        return jnp.where(self.h0, float(low), float(high)).astype(F32)


def rows8(index, pitch=8):
    if isinstance(index, int):
        return slice(index * pitch, index * pitch + 8)
    if pitch != 8:
        return pl.ds(index * pitch, 8)
    return pl.ds(pl.multiple_of(index * 8, 8), 8)


def x_line(u, mk, mat):
    g0 = combine((SLOPE[0, b], u[b]) for b in range(4))
    g3 = combine((SLOPE[3, b], u[b]) for b in range(4))

    def before(t):
        return jnp.where(mk.x_first, lanes(t, -15), lanes(t, 1))

    def after(t):
        return jnp.where(mk.x_last, lanes(t, 15), lanes(t, -1))

    um, gm, up, gp = before(u[3]), before(g3), after(u[0]), after(g0)
    terms = list(u) + [um, gm, up, gp]
    return [combine((mat[a, c], terms[c]) for c in range(8)) for a in range(4)]


def y_coefs(mk, mat):
    out = []
    for jj in range(2):
        o = 3 - jj
        row = [mk.by_half(mat[jj, b], mat[o, 3 - b]) for b in range(4)]
        row.append(mk.by_half(mat[jj, UM], mat[o, UP]))
        row.append(mk.by_half(mat[jj, UP], mat[o, UM]))
        row.append(mk.by_half(mat[jj, GM], mat[o, GP]))
        out.append(row)
    return out


def y_line(u0, u1, mk, coefs):
    r0, r1 = rolled(u0, 4), rolled(u1, 4)
    g = combine(((SLOPE[0, 0], u0), (SLOPE[0, 1], u1), (SLOPE[0, 2], r1), (SLOPE[0, 3], r0)))
    g = rolled(g * mk.sign, 4)

    def outer(t):
        near = jnp.where(mk.h0, lanes(t, 16), lanes(t, -16))
        far = jnp.where(mk.r0, rolled(near, -1), rolled(near, 1))
        return jnp.where(mk.y_wrap, far, near)

    n, gn = outer(r0), outer(g)
    nr = rolled(n, 4)
    return [
        combine(zip(coefs[0], (u0, u1, r1, r0, n, nr, gn))),
        combine(zip(coefs[1][:6], (u0, u1, r1, r0, n, nr))),
    ]


def z_line(u, hu, hg, mk, mat):
    g0 = combine((SLOPE[0, b], u[b]) for b in range(4))
    g3 = combine((SLOPE[3, b], u[b]) for b in range(4))
    um = jnp.where(mk.l0, hu, rolled(u[3], 2))
    gm = jnp.where(mk.l0, hg, rolled(g3, 2))
    up = jnp.where(mk.l0, rolled(u[0], -2), hu)
    gp = jnp.where(mk.l0, rolled(g0, -2), hg)
    terms = list(u) + [um, gm, up, gp]
    return [combine((mat[a, c], terms[c]) for c in range(8)) for a in range(4)]


def operator_of(src, dst, hu, hg, mk, scale, ident, base=None, pitches=(8, 8)):
    mats = [scale * m for m in LINES]
    mats[2][:, :4] += ident * np.eye(4)
    coefs = y_coefs(mk, mats[1])

    def read(index):
        return src[rows8(index, pitches[0]), :]

    def at_goal(index):
        return rows8(index, pitches[1])

    def in_layer(v):
        col = v * 8
        for jj in range(2):
            for k in range(4):
                at = [(col + 2 * i + jj) * 4 + k for i in range(4)]
                new = x_line([read(n) for n in at], mk, mats[0])
                for i in range(4):
                    dst[at_goal(at[i]), :] = new[i]
        for i in range(4):
            for k in range(4):
                at = [(col + 2 * i + jj) * 4 + k for jj in range(2)]
                new = y_line(read(at[0]), read(at[1]), mk, coefs)
                for jj in range(2):
                    dst[at_goal(at[jj]), :] += new[jj]

    def across(v):
        col = v * 8
        for c in range(8):
            at = [(col + c) * 4 + k for k in range(4)]
            new = z_line(
                [read(n) for n in at], hu[rows8(col + c), :], hg[rows8(col + c), :], mk, mats[2]
            )
            for k in range(4):
                more = new[k] if base is None else new[k] + base[rows8(at[k]), :]
                dst[at_goal(at[k]), :] += more

    return in_layer, across


def apply_operator(*args, **options):
    in_layer, across = operator_of(*args, **options)

    def body(v, carry):
        in_layer(v)
        across(v)
        return carry

    lax.fori_loop(0, VARS, body, 0)


def split2(x):
    hi = x.astype(BF16)
    return hi, (x - hi.astype(F32)).astype(BF16)


def both(res):
    half = res.shape[0] // 2
    return res[:half] + res[half:]


NODE_ROWS = (0, 1, 3, 2)


PITCH = 12


def spread(val, goal, first, pitch=8):
    for vi in range(val.shape[0] // 16):
        for h in range(2):
            for t in range(4):
                tile = val[vi * 16 + h * 8 : vi * 16 + h * 8 + 8, t * 128 : t * 128 + 128]
                goal[pl.ds((first + vi) * 8 * pitch + h * 4 + t, 8, stride=pitch), :] = tile


def nt_dot(a, b):
    return lax.dot_general(a, b, (((1,), (1,)), ((), ())), preferred_element_type=F32)


def fill_order(rows, order):
    ids = lax.broadcasted_iota(jnp.int32, (16, 128), 0)
    one, none = jnp.ones((16, 128), BF16), jnp.zeros((16, 128), BF16)
    rows = [jnp.broadcast_to(row, (16, 128)).astype(jnp.int16) for row in rows]
    for first in range(0, 512, 16):
        here = (ids + first).astype(jnp.int16)
        for t in range(4):
            found = jnp.where(here == rows[t], one, none)
            order[first : first + 16, t * 128 : t * 128 + 128] = found


def pack_points(route, payload, pack_ref):
    dest = lax.broadcasted_iota(jnp.int32, (128, 128), 0)
    lane = lax.broadcasted_iota(jnp.int32, (128, 128), 1)
    slot = lax.broadcasted_iota(jnp.int32, (8, 128), 0).astype(F32)
    to_device = [jnp.where(dest == route[:, t * 128 : t * 128 + 128], 1.0, 0.0) for t in range(4)]
    narrow = [x.astype(BF16) for x in to_device]
    before = jnp.where(dest < lane, 1.0, 0.0).astype(BF16)
    steps = jnp.concatenate([before, jnp.ones((128, 128), BF16)], axis=1)
    counts = jnp.dot(jnp.concatenate(narrow, axis=0), steps, preferred_element_type=F32)
    base = None
    parts = [[], [], []]
    for t in range(4):
        here = slice(t * 128, t * 128 + 128)
        count = counts[here, :128] if base is None else counts[here, :128] + base
        base = counts[here, 128:] if base is None else base + counts[here, 128:]
        within = jnp.sum(count * to_device[t], axis=0, keepdims=True)
        chosen = slot == within
        rows = [jnp.where(chosen, p[:, here], 0.0) for p in payload]
        rows.append(jnp.zeros((8, 128), F32))
        rest = jnp.concatenate(rows, axis=0)
        for part in parts:
            part.append(rest.astype(BF16))
            rest = rest - part[-1].astype(F32)
    terms = jnp.concatenate([jnp.concatenate(part, axis=1) for part in parts], axis=1)
    terms = jnp.concatenate([terms, jnp.zeros((128 - GROUP - 8, 1536), BF16)], axis=0)
    out = nt_dot(jnp.concatenate(narrow * 3, axis=1), terms)
    low = pltpu.roll(pltpu.roll(out, 1, 0), GROUP, 1)
    up = pltpu.roll(pltpu.roll(out, 127, 0), 2 * GROUP - 128, 1)
    pack_ref[pl.ds(0, 128, stride=2), :] = jnp.where(lane < GROUP, out, low)
    pack_ref[pl.ds(1, 128, stride=2), :] = jnp.where(lane < 2 * GROUP - 128, low, up)


def fill_halo(u_ref, up_ref, down_ref, mk):
    for col in range(COLS):
        u = [u_ref[rows8(col * 4 + k), :] for k in range(4)]
        g0 = combine((SLOPE[0, b], u[b]) for b in range(4))
        g3 = combine((SLOPE[3, b], u[b]) for b in range(4))
        ups = ((rolled(u[0], -2), u[1]), (rolled(u[2], -2), u[3]), (u[3], rolled(g3, 2)))
        downs = ((u[0], rolled(u[1], 2)), (u[2], rolled(u[3], 2)), (rolled(u[0], -2), g0))
        for part in range(3):
            up_ref[rows8(part * COLS + col), :] = jnp.where(mk.l0, *ups[part])
            down_ref[rows8(part * COLS + col), :] = jnp.where(mk.l0, *downs[part])


def entry_kernel(
    route_hbm, slot_hbm, forces_hbm, coords_hbm, lists_hbm, state_hbm,
    pack_ref, u_ref, up_ref, down_ref, inv_ref, order,
    route_ref, slot_ref, forces_ref, coords_ref, lists_ref, state_ref, lhs, sems,
):
    sources = (route_hbm, slot_hbm, forces_hbm, coords_hbm, lists_hbm, state_hbm)
    targets = (route_ref, slot_ref, forces_ref, coords_ref, lists_ref, state_ref)
    copies = [
        pltpu.make_async_copy(a, b, sems.at[n]) for n, (a, b) in enumerate(zip(sources, targets))
    ]
    for copy in copies:
        copy.start()
    mk = Masks()
    for copy in copies[:5]:
        copy.wait()
    payload = [forces_ref[f : f + 1, :] for f in range(5)]
    payload += [coords_ref[f : f + 1, :] for f in range(3)]
    payload.append(slot_ref[...].astype(F32))
    pack_points(route_ref[...], payload, pack_ref)

    rows = [
        lists_ref[t // 2 : t // 2 + 1, (t % 2) * 128 : (t % 2) * 128 + 128] for t in range(4)
    ]
    fill_order(rows, order)
    copies[5].wait()
    for vi in range(VARS * 4):
        x = jnp.concatenate([state_ref[vi * 4 + j] for j in NODE_ROWS], axis=0)
        hi, lo = split2(x)
        lhs[vi * 16 : vi * 16 + 16, :] = hi
        lhs[320 + vi * 16 : 336 + vi * 16, :] = lo
    res = jnp.dot(lhs[...], order[...], preferred_element_type=F32)
    spread(both(res), u_ref, 0)

    place = lax.broadcasted_iota(jnp.int32, (16, 512), 1)
    digit = lax.broadcasted_iota(jnp.int32, (16, 512), 0)
    digits = jnp.where(digit == 0, place >> 4, place & 15).astype(F32).astype(BF16)
    where = nt_dot(digits, order[...])
    inv = where[0:1, :] * 16.0 + where[1:2, :]
    inv = [inv[:, t * 128 : t * 128 + 128] for t in range(4)]
    inv = jnp.concatenate(inv + inv, axis=0)
    inv_ref[...] = inv
    up_ref[HALO_TILES * 8 :, :] = inv
    down_ref[HALO_TILES * 8 :, :] = inv

    fill_halo(u_ref, up_ref, down_ref, mk)


def state_kernel(u_ref, before_ref, after_ref, base_ref, au, ag, hu, hg, m0):
    mk = Masks()
    mat = TIME_STEP * LINES[2]
    top, bottom = np.eye(4)[3], np.eye(4)[0]

    def layered(row_low, row_high, near):
        order = ((0, 1), (1, 0), (2, 3), (3, 2)) + (((UM, UP), (GM, GP)) if near else ())
        return [mk.by_layer(row_low[low], row_high[high]) for low, high in order]

    step = np.eye(4, 8) + mat
    slopes = layered(SLOPE[3], SLOPE[0], False)
    later = layered(step[3], step[0], True)
    later_slopes = layered(SLOPE[3] @ step, SLOPE[0] @ step, True)

    def unpack(v, carry):
        for c in range(8):
            col = v * 8 + c
            low = [before_ref[rows8(part * COLS + col), :] for part in range(3)]
            high = [after_ref[rows8(part * COLS + col), :] for part in range(3)]
            tiles = []
            for part in range(2):
                tiles.append(jnp.where(mk.l0, low[part], high[part]))
                tiles.append(jnp.where(mk.l0, rolled(low[part], -2), rolled(high[part], 2)))
            tiles.append(jnp.where(mk.l0, low[2], rolled(high[2], 2)))
            tiles.append(jnp.where(mk.l0, rolled(low[2], -2), high[2]))
            at = rows8(col)
            au[at, :] = jnp.where(mk.l0, tiles[3], tiles[1])
            ag[at, :] = combine(zip(slopes, tiles))
            hu[at, :] = combine(zip(later, tiles))
            hg[at, :] = combine(zip(later_slopes, tiles))
        return carry

    lax.fori_loop(0, VARS, unpack, 0)
    apply_operator(u_ref, m0, au, ag, mk, TIME_STEP, 1.0, pitches=(8, 8))

    x_mat, coefs = TIME_STEP * LINES[0], y_coefs(mk, TIME_STEP * LINES[1])

    def halo(v, carry):
        for c in range(8):
            col = v * 8 + c
            u = [u_ref[rows8(col * 4 + k), :] for k in range(4)]
            g0 = combine((SLOPE[0, b], u[b]) for b in range(4))
            g3 = combine((SLOPE[3, b], u[b]) for b in range(4))
            for h, f_low, f_high in ((hu, top, bottom), (hg, SLOPE[3], SLOPE[0])):
                low = combine(((f_low @ mat[:, UP], u[0]), (f_low @ mat[:, GP], g0)))
                high = combine(((f_high @ mat[:, UM], u[3]), (f_high @ mat[:, GM], g3)))
                h[rows8(col), :] += jnp.where(mk.l0, low, high)
        for a, h in ((au, hu), (ag, hg)):
            for i in range(4):
                at = [rows8(v * 8 + 2 * i + jj) for jj in range(2)]
                new = y_line(a[at[0], :], a[at[1], :], mk, coefs)
                for jj in range(2):
                    h[at[jj], :] += new[jj]
            for jj in range(2):
                at = [rows8(v * 8 + 2 * i + jj) for i in range(4)]
                new = x_line([a[r, :] for r in at], mk, x_mat)
                for i in range(4):
                    h[at[i], :] += new[i]
        return carry

    lax.fori_loop(0, VARS, halo, 0)
    apply_operator(m0, base_ref, hu, hg, mk, 0.5 * TIME_STEP, 0.5)

    def finish(n, carry):
        base_ref[rows8(n), :] += 0.5 * u_ref[rows8(n), :]
        return carry

    lax.fori_loop(0, TILES, finish, 0, unroll=16)


def line_basis(coords):
    rows = []
    for a in range(4):
        term = None
        for k in range(4):
            if k != a:
                factor = (coords - NODE_POINTS[k]) * (1.0 / (NODE_POINTS[a] - NODE_POINTS[k]))
                term = factor if term is None else term * factor
        rows.append(term)
    return rows


def place_of(slots, table, row):
    number = slots.astype(jnp.int32)
    inner, outer = number & 127, number >> 7
    found = jnp.zeros((8, 128), F32)
    for t in range(4):
        line = jnp.broadcast_to(table[row + t : row + t + 1, :], (8, 128))
        found = jnp.where(outer == t, jnp.take_along_axis(line, inner, axis=1), found)
    return found.astype(jnp.int32)


def fill_hot(hot, place):
    ids = lax.broadcasted_iota(jnp.int32, (16, 128), 0)
    one, none = jnp.ones((16, 128), BF16), jnp.zeros((16, 128), BF16)
    rows = [jnp.broadcast_to(place[c : c + 1, :], (16, 128)).astype(jnp.int16) for c in range(CAP)]
    for first in range(0, hot.shape[0], 16):
        here = (ids + first).astype(jnp.int16)
        for c in range(CAP):
            hot[first : first + 16, c * 128 : c * 128 + 128] = jnp.where(here == rows[c], one, none)


def fill_terms(matrix, columns, nodes, strength, grid, group, first, count):
    if first == 0:
        for n, tile in enumerate(nodes):
            grid[group, n * 8 : n * 8 + 8, :] = tile
        for n, tile in enumerate(columns):
            strength[group, n * 8 : n * 8 + 8, :] = tile
    for c in range(CAP):
        here = slice(c * 128, c * 128 + 128)
        node_rows = grid[group, pl.ds(c, 16, stride=8), :]
        for n in range(first, first + count):
            hi, lo = split2(node_rows * strength[group, n * 8 + c : n * 8 + c + 1, :])
            at = (first + n) * 16
            matrix[at : at + 16, here] = hi
            matrix[at + count * 16 : at + count * 16 + 16, here] = lo


def trace_terms(field, node):
    bx, by, bz = [line_basis(field[5 + d]) for d in range(3)]
    slope = combine((SLOPE[node, b], bz[b]) for b in range(4))
    columns = [field[v] * bz[node] for v in range(VARS)]
    columns += [field[v] * slope for v in range(VARS)]
    pairs = [(i, j) for h in range(2) for i in range(4) for j in NODE_ROWS[2 * h : 2 * h + 2]]
    return columns, [by[j] * bx[i] for i, j in pairs]


SPANS = ((0, 3), (3, 2))
BACK = ((0, 3), (3, 1), (4, 1))


def source_kernel(
    pts_ref, inv_ref, before_ref, after_ref, base_ref, order, out_hbm,
    hot, hot_low, hot_up, lhs, lhs_low, lhs_up, grid, strength, su, sg, s_ref, new_ref,
    lhs_out, out_ref, sems,
):
    mk = Masks()
    halves = [pts_ref[pl.ds(h, 128, stride=2), :].T for h in range(2)]
    data = jnp.concatenate(halves, axis=0)
    field = [
        [data[g * GROUP + f * 8 : g * GROUP + f * 8 + 8] for f in range(FIELDS)] for g in range(3)
    ]
    bx, by, bz = [line_basis(field[0][5 + d]) for d in range(3)]
    columns = [field[0][v] * bx[i] for v in range(VARS) for i in range(4)]
    nodes = [by[j] * bz[k] for j in NODE_ROWS for k in range(4)]
    vals, traces, copies = {}, {}, []
    in_layer, across = operator_of(
        s_ref, new_ref, su, sg, mk, 0.5 * TIME_STEP * TIME_STEP, TIME_STEP, base_ref, (PITCH, PITCH)
    )

    def gather(n):
        first, count = SPANS[n]
        fill_terms(lhs, columns, nodes, strength, grid, 0, first * 4, count * 4)
        vals[n] = both(nt_dot(lhs[first * 128 : (first + count) * 128, :], hot[...]))

    def gather_traces(side):
        matrix, goal = ((lhs_low, hot_low), (lhs_up, hot_up))[side]
        table, shift = ((before_ref, 256), (after_ref, 0))[side]
        fill_hot(goal, place_of(field[1 + side][8], table, 0) - shift)
        fill_terms(matrix, *trace_terms(field[1 + side], 3 - 3 * side), strength, grid, 1 + side, 0, 10)
        traces[side] = both(nt_dot(matrix[...], goal[...]))

    def spread_traces():
        for part, goal in ((0, su), (1, sg)):
            for v in range(VARS):
                for h in range(2):
                    at = (part * VARS + v) * 16 + h * 8
                    for t in range(4):
                        tile = traces[t // 2][at : at + 8, (t % 2) * 128 : (t % 2) * 128 + 128]
                        goal[pl.ds(v * 64 + h * 4 + t, 8, stride=8), :] = tile

    def advance(n, step):
        first, count = SPANS[n]
        if step is in_layer:
            spread(vals[n], s_ref, first * 4, PITCH)
        for v in range(first, first + count):
            step(v)

    def put_back(n):
        first, count = BACK[n]
        for vi in range(first * 4, (first + count) * 4):
            at = (first * 4 + vi) * 16
            for t in range(4):
                rows = [pl.ds(vi * 8 * PITCH + h * 4 + t, 8, stride=PITCH) for h in range(2)]
                x = jnp.concatenate([new_ref[r, :] for r in rows], axis=0)
                hi, lo = split2(x)
                lhs_out[at : at + 16, t * 128 : t * 128 + 128] = hi
                at_lo = at + count * 64
                lhs_out[at_lo : at_lo + 16, t * 128 : t * 128 + 128] = lo
        val = both(nt_dot(lhs_out[first * 128 : (first + count) * 128, :], order[...]))
        for vi in range(first * 4, (first + count) * 4):
            for m, j in enumerate(NODE_ROWS):
                at = (vi - first * 4) * 16 + m * 4
                out_ref[vi * 4 + j] = val[at : at + 4, :]
        part = pl.ds(first * 16, count * 16)
        copies.append(pltpu.make_async_copy(out_ref.at[part], out_hbm.at[part], sems.at[n]))
        copies[-1].start()

    fill_hot(hot, place_of(field[0][8], inv_ref, 0))
    gather(0)
    gather_traces(0)
    gather_traces(1)
    gather(1)
    advance(0, in_layer)
    spread_traces()
    advance(0, across)
    advance(1, in_layer)
    put_back(0)
    advance(1, across)
    put_back(1)
    put_back(2)
    for copy in copies:
        copy.wait()


def call(kernel, outs, scratch, specs, place=pltpu.VMEM):
    return pl.pallas_call(
        kernel,
        out_shape=outs,
        in_specs=specs,
        out_specs=jax.tree.map(lambda _: pl.BlockSpec(memory_space=place), outs),
        scratch_shapes=scratch,
        compiler_params=pltpu.CompilerParams(vmem_limit_bytes=VMEM_LIMIT),
    )


def tile_array(count):
    return jax.ShapeDtypeStruct((count * 8, 128), F32)


VMEM = pl.BlockSpec(memory_space=pltpu.VMEM)


def entry_call(route, slots, forces, coords, lists, state):
    arrays = (route, slots, forces, coords, lists, state)
    return call(
        entry_kernel,
        (
            jax.ShapeDtypeStruct((256, 128), F32),
            tile_array(TILES),
            tile_array(HALO_TILES + 1),
            tile_array(HALO_TILES + 1),
            tile_array(1),
            jax.ShapeDtypeStruct((512, 512), BF16),
        ),
        [pltpu.VMEM(x.shape, x.dtype) for x in arrays]
        + [
            pltpu.VMEM((640, 512), BF16),
            pltpu.SemaphoreType.DMA((6,)),
        ],
        [pl.BlockSpec(memory_space=pltpu.HBM)] * 6,
    )(*[pltpu.with_memory_space_constraint(x, pltpu.HBM) for x in arrays])


def state_call(u, before, after):
    cols = pltpu.VMEM((COLS * 8, 128), F32)
    return call(
        state_kernel,
        tile_array(TILES),
        [cols, cols, cols, cols, pltpu.VMEM((TILES * 8, 128), F32)],
        [VMEM] * 3,
    )(u, before, after)


def source_call(pts, inv, before, after, base, order):
    cols = pltpu.VMEM((COLS * 8, 128), F32)
    field = pltpu.VMEM((TILES * PITCH, 128), F32)
    return call(
        source_kernel,
        jax.ShapeDtypeStruct((VARS * 16, 4, 512), F32),
        [
            pltpu.VMEM((512, 1024), BF16),
            pltpu.VMEM((256, 1024), BF16),
            pltpu.VMEM((256, 1024), BF16),
            pltpu.VMEM((640, 1024), BF16),
            pltpu.VMEM((320, 1024), BF16),
            pltpu.VMEM((320, 1024), BF16),
            pltpu.VMEM((3, 128, 128), F32),
            pltpu.VMEM((3, 160, 128), F32),
            cols,
            cols,
            field,
            field,
            pltpu.VMEM((640, 512), BF16),
            pltpu.VMEM((VARS * 16, 4, 512), F32),
            pltpu.SemaphoreType.DMA((3,)),
        ],
        [VMEM] * 6,
        pltpu.HBM,
    )(pts, inv, before, after, base, order)


def on_device(state, neighbour_map, layer_lists, forces, positions, route, element_slot):
    count = lax.axis_size("sfc")
    forward = [(d, (d + 1) % count) for d in range(count)]
    backward = [(target, source) for source, target in forward]
    pack, u, up, down, inv, order = entry_call(
        route.reshape(1, -1),
        element_slot.reshape(1, -1),
        forces,
        positions,
        layer_lists,
        state.reshape(VARS * 16, 4, -1),
    )
    before = lax.ppermute(up, "sfc", forward)
    after = lax.ppermute(down, "sfc", backward)
    pts = lax.all_to_all(pack, "sfc", split_axis=0, concat_axis=0, tiled=True)
    base = state_call(u, before, after)
    table = slice(HALO_TILES * 8, None)
    out = source_call(pts, inv, before[table], after[table], base, order)
    return out.reshape(state.shape)


def solution(mesh):
    in_specs = (
        P(None, None, None, None, "sfc"),
        P(None, "sfc"),
        P(None, "sfc"),
        P(None, "sfc"),
        P(None, "sfc"),
        P("sfc", None),
        P("sfc"),
    )
    out_specs = P(None, None, None, None, "sfc")
    return jax.shard_map(
        on_device, mesh=mesh, in_specs=in_specs, out_specs=out_specs, check_vma=False
    )
```

```python
import functools

import jax
import jax.numpy as jnp
import numpy as np
from jax import lax
from jax.experimental import pallas as pl
from jax.experimental.pallas import tpu as pltpu
from jax.sharding import PartitionSpec as P

NODE_POINTS = (-1.0, -0.4472135954999579, 0.4472135954999579, 1.0)
GSCALE = 2.0
HALF_LIFT = 6.0
ADVECT = (0.6, -0.4, 0.8)
VISCOSITY = 0.02
TIME_STEP = 0.04

VARS = 5
CAP = 8
FIELDS = 9
GROUP = FIELDS * CAP
COLS = VARS * 4 * 2
TILES = COLS * 4
HALO_TILES = COLS * 3
VMEM_LIMIT = 24 * 1024 * 1024
F32 = jnp.float32
BF16 = jnp.bfloat16


def diff_table():
    factor = [
        float(np.prod([NODE_POINTS[a] - NODE_POINTS[k] for k in range(4) if k != a]))
        for a in range(4)
    ]
    table = np.zeros((4, 4))
    for a in range(4):
        for b in range(4):
            if a != b:
                table[a, b] = factor[a] / factor[b] / (NODE_POINTS[a] - NODE_POINTS[b])
            else:
                table[a, b] = sum(
                    (1.0 / (NODE_POINTS[a] - NODE_POINTS[k]) for k in range(4) if k != a)
                )
    return table


SLOPE = GSCALE * diff_table()


def line_operator(direction):
    a, nu = ADVECT[direction], VISCOSITY
    out = np.zeros((4, 8))
    for col in range(8):
        value = np.zeros(8)
        value[col] = 1.0
        u, (um, gm, up, gp) = value[:4], value[4:]
        q = SLOPE @ u
        q[0] -= HALF_LIFT * (um - u[0])
        q[3] += HALF_LIFT * (up - u[3])
        qm = gm + HALF_LIFT * (u[0] - um)
        qp = gp - HALF_LIFT * (u[3] - up)
        res = -SLOPE @ (a * u - nu * q)
        for node, normal, ou, oq in ((0, -1.0, um, qm), (3, 1.0, up, qp)):
            along = normal * a
            res[node] += -HALF_LIFT * (along - abs(along)) * (ou - u[node])
            res[node] += HALF_LIFT * nu * normal * (oq - q[node])
        out[:, col] = res
    return out


LINES = [line_operator(d) for d in range(3)]
UM, GM, UP, GP = 4, 5, 6, 7


def rolled(x, shift):
    return pltpu.roll(x, shift % 8, 0)


def lanes(x, shift):
    return pltpu.roll(x, shift % 128, 1)


def combine(pairs):
    total = None
    for coef, value in pairs:
        if isinstance(coef, (float, np.floating)):
            if coef == 0.0:
                continue
            term = value if coef == 1.0 else value * float(coef)
        else:
            term = value * coef
        total = term if total is None else total + term
    return total


class Masks:
    def __init__(self):
        sub = lax.broadcasted_iota(jnp.int32, (8, 128), 0)
        lane = lax.broadcasted_iota(jnp.int32, (8, 128), 1)
        self.h0 = sub < 4
        self.l0 = (sub & 2) == 0
        self.r0 = (sub & 1) == 0
        self.x_first = (lane & 15) == 0
        self.x_last = (lane & 15) == 15
        self.y_wrap = (self.h0 & (lane < 16)) | (~self.h0 & (lane >= 112))
        self.sign = jnp.where(self.h0, 1.0, -1.0).astype(F32)

    def by_layer(self, low, high):
        return jnp.where(self.l0, float(low), float(high)).astype(F32)

    def by_half(self, low, high):
        if low == high:
            return float(low)
        return jnp.where(self.h0, float(low), float(high)).astype(F32)


def rows8(index, pitch=8):
    if isinstance(index, int):
        return slice(index * pitch, index * pitch + 8)
    if pitch != 8:
        return pl.ds(index * pitch, 8)
    return pl.ds(pl.multiple_of(index * 8, 8), 8)


def x_line(u, mk, mat):
    g0 = combine((SLOPE[0, b], u[b]) for b in range(4))
    g3 = combine((SLOPE[3, b], u[b]) for b in range(4))

    def before(t):
        return jnp.where(mk.x_first, lanes(t, -15), lanes(t, 1))

    def after(t):
        return jnp.where(mk.x_last, lanes(t, 15), lanes(t, -1))

    um, gm, up, gp = before(u[3]), before(g3), after(u[0]), after(g0)
    terms = list(u) + [um, gm, up, gp]
    return [combine((mat[a, c], terms[c]) for c in range(8)) for a in range(4)]


def y_coefs(mk, mat):
    out = []
    for jj in range(2):
        o = 3 - jj
        row = [mk.by_half(mat[jj, b], mat[o, 3 - b]) for b in range(4)]
        row.append(mk.by_half(mat[jj, UM], mat[o, UP]))
        row.append(mk.by_half(mat[jj, UP], mat[o, UM]))
        row.append(mk.by_half(mat[jj, GM], mat[o, GP]))
        out.append(row)
    return out


def y_line(u0, u1, mk, coefs):
    r0, r1 = rolled(u0, 4), rolled(u1, 4)
    g = combine(((SLOPE[0, 0], u0), (SLOPE[0, 1], u1), (SLOPE[0, 2], r1), (SLOPE[0, 3], r0)))
    g = rolled(g * mk.sign, 4)

    def outer(t):
        near = jnp.where(mk.h0, lanes(t, 16), lanes(t, -16))
        far = jnp.where(mk.r0, rolled(near, -1), rolled(near, 1))
        return jnp.where(mk.y_wrap, far, near)

    n, gn = outer(r0), outer(g)
    nr = rolled(n, 4)
    return [
        combine(zip(coefs[0], (u0, u1, r1, r0, n, nr, gn))),
        combine(zip(coefs[1][:6], (u0, u1, r1, r0, n, nr))),
    ]


def z_line(u, hu, hg, mk, mat):
    g0 = combine((SLOPE[0, b], u[b]) for b in range(4))
    g3 = combine((SLOPE[3, b], u[b]) for b in range(4))
    um = jnp.where(mk.l0, hu, rolled(u[3], 2))
    gm = jnp.where(mk.l0, hg, rolled(g3, 2))
    up = jnp.where(mk.l0, rolled(u[0], -2), hu)
    gp = jnp.where(mk.l0, rolled(g0, -2), hg)
    terms = list(u) + [um, gm, up, gp]
    return [combine((mat[a, c], terms[c]) for c in range(8)) for a in range(4)]


def operator_of(src, dst, hu, hg, mk, scale, ident, base=None, pitches=(8, 8)):
    mats = [scale * m for m in LINES]
    mats[2][:, :4] += ident * np.eye(4)
    coefs = y_coefs(mk, mats[1])

    def read(index):
        return src[rows8(index, pitches[0]), :]

    def at_goal(index):
        return rows8(index, pitches[1])

    def in_layer(v):
        col = v * 8
        for jj in range(2):
            for k in range(4):
                at = [(col + 2 * i + jj) * 4 + k for i in range(4)]
                new = x_line([read(n) for n in at], mk, mats[0])
                for i in range(4):
                    dst[at_goal(at[i]), :] = new[i]
        for i in range(4):
            for k in range(4):
                at = [(col + 2 * i + jj) * 4 + k for jj in range(2)]
                new = y_line(read(at[0]), read(at[1]), mk, coefs)
                for jj in range(2):
                    dst[at_goal(at[jj]), :] += new[jj]

    def across(v):
        col = v * 8
        for c in range(8):
            at = [(col + c) * 4 + k for k in range(4)]
            new = z_line(
                [read(n) for n in at], hu[rows8(col + c), :], hg[rows8(col + c), :], mk, mats[2]
            )
            for k in range(4):
                more = new[k] if base is None else new[k] + base[rows8(at[k]), :]
                dst[at_goal(at[k]), :] += more

    return in_layer, across


def apply_operator(*args, **options):
    in_layer, across = operator_of(*args, **options)

    def body(v, carry):
        in_layer(v)
        across(v)
        return carry

    lax.fori_loop(0, VARS, body, 0)


def split2(x):
    hi = x.astype(BF16)
    return hi, (x - hi.astype(F32)).astype(BF16)


def both(res):
    half = res.shape[0] // 2
    return res[:half] + res[half:]


NODE_ROWS = (0, 1, 3, 2)


PITCH = 12


def spread(val, goal, first, pitch=8):
    for vi in range(val.shape[0] // 16):
        for h in range(2):
            for t in range(4):
                tile = val[vi * 16 + h * 8 : vi * 16 + h * 8 + 8, t * 128 : t * 128 + 128]
                goal[pl.ds((first + vi) * 8 * pitch + h * 4 + t, 8, stride=pitch), :] = tile


def nt_dot(a, b):
    return lax.dot_general(a, b, (((1,), (1,)), ((), ())), preferred_element_type=F32)


def fill_order(rows, order):
    ids = lax.broadcasted_iota(jnp.int32, (16, 128), 0)
    one, none = jnp.ones((16, 128), BF16), jnp.zeros((16, 128), BF16)
    rows = [jnp.broadcast_to(row, (16, 128)).astype(jnp.int16) for row in rows]
    for first in range(0, 512, 16):
        here = (ids + first).astype(jnp.int16)
        for t in range(4):
            found = jnp.where(here == rows[t], one, none)
            order[first : first + 16, t * 128 : t * 128 + 128] = found


def pack_points(route, payload, pack_ref):
    dest = lax.broadcasted_iota(jnp.int32, (128, 128), 0)
    lane = lax.broadcasted_iota(jnp.int32, (128, 128), 1)
    slot = lax.broadcasted_iota(jnp.int32, (8, 128), 0).astype(F32)
    to_device = [jnp.where(dest == route[:, t * 128 : t * 128 + 128], 1.0, 0.0) for t in range(4)]
    narrow = [x.astype(BF16) for x in to_device]
    before = jnp.where(dest < lane, 1.0, 0.0).astype(BF16)
    steps = jnp.concatenate([before, jnp.ones((128, 128), BF16)], axis=1)
    counts = jnp.dot(jnp.concatenate(narrow, axis=0), steps, preferred_element_type=F32)
    base = None
    parts = [[], [], []]
    for t in range(4):
        here = slice(t * 128, t * 128 + 128)
        count = counts[here, :128] if base is None else counts[here, :128] + base
        base = counts[here, 128:] if base is None else base + counts[here, 128:]
        within = jnp.sum(count * to_device[t], axis=0, keepdims=True)
        chosen = slot == within
        rows = [jnp.where(chosen, p[:, here], 0.0) for p in payload]
        rows.append(jnp.zeros((8, 128), F32))
        rest = jnp.concatenate(rows, axis=0)
        for part in parts:
            part.append(rest.astype(BF16))
            rest = rest - part[-1].astype(F32)
    terms = jnp.concatenate([jnp.concatenate(part, axis=1) for part in parts], axis=1)
    terms = jnp.concatenate([terms, jnp.zeros((128 - GROUP - 8, 1536), BF16)], axis=0)
    out = nt_dot(jnp.concatenate(narrow * 3, axis=1), terms)
    low = pltpu.roll(pltpu.roll(out, 1, 0), GROUP, 1)
    up = pltpu.roll(pltpu.roll(out, 127, 0), 2 * GROUP - 128, 1)
    pack_ref[pl.ds(0, 128, stride=2), :] = jnp.where(lane < GROUP, out, low)
    pack_ref[pl.ds(1, 128, stride=2), :] = jnp.where(lane < 2 * GROUP - 128, low, up)


def fill_halo(u_ref, up_ref, down_ref, mk):
    for col in range(COLS):
        u = [u_ref[rows8(col * 4 + k), :] for k in range(4)]
        g0 = combine((SLOPE[0, b], u[b]) for b in range(4))
        g3 = combine((SLOPE[3, b], u[b]) for b in range(4))
        ups = ((rolled(u[0], -2), u[1]), (rolled(u[2], -2), u[3]), (u[3], rolled(g3, 2)))
        downs = ((u[0], rolled(u[1], 2)), (u[2], rolled(u[3], 2)), (rolled(u[0], -2), g0))
        for part in range(3):
            up_ref[rows8(part * COLS + col), :] = jnp.where(mk.l0, *ups[part])
            down_ref[rows8(part * COLS + col), :] = jnp.where(mk.l0, *downs[part])


def entry_kernel(
    route_hbm, slot_hbm, forces_hbm, coords_hbm, lists_hbm, state_hbm,
    pack_ref, u_ref, up_ref, down_ref, inv_ref, order,
    route_ref, slot_ref, forces_ref, coords_ref, lists_ref, state_ref, lhs, sems,
):
    sources = (route_hbm, slot_hbm, forces_hbm, coords_hbm, lists_hbm, state_hbm)
    targets = (route_ref, slot_ref, forces_ref, coords_ref, lists_ref, state_ref)
    copies = [
        pltpu.make_async_copy(a, b, sems.at[n]) for n, (a, b) in enumerate(zip(sources, targets))
    ]
    for copy in copies:
        copy.start()
    mk = Masks()
    for copy in copies[:5]:
        copy.wait()
    payload = [forces_ref[f : f + 1, :] for f in range(5)]
    payload += [coords_ref[f : f + 1, :] for f in range(3)]
    payload.append(slot_ref[...].astype(F32))
    pack_points(route_ref[...], payload, pack_ref)

    rows = [
        lists_ref[t // 2 : t // 2 + 1, (t % 2) * 128 : (t % 2) * 128 + 128] for t in range(4)
    ]
    fill_order(rows, order)
    copies[5].wait()
    for vi in range(VARS * 4):
        x = jnp.concatenate([state_ref[vi * 4 + j] for j in NODE_ROWS], axis=0)
        hi, lo = split2(x)
        lhs[vi * 16 : vi * 16 + 16, :] = hi
        lhs[320 + vi * 16 : 336 + vi * 16, :] = lo
    res = jnp.dot(lhs[...], order[...], preferred_element_type=F32)
    spread(both(res), u_ref, 0)

    place = lax.broadcasted_iota(jnp.int32, (16, 512), 1)
    digit = lax.broadcasted_iota(jnp.int32, (16, 512), 0)
    digits = jnp.where(digit == 0, place >> 4, place & 15).astype(F32).astype(BF16)
    where = nt_dot(digits, order[...])
    inv = where[0:1, :] * 16.0 + where[1:2, :]
    inv = [inv[:, t * 128 : t * 128 + 128] for t in range(4)]
    inv = jnp.concatenate(inv + inv, axis=0)
    inv_ref[...] = inv
    up_ref[HALO_TILES * 8 :, :] = inv
    down_ref[HALO_TILES * 8 :, :] = inv

    fill_halo(u_ref, up_ref, down_ref, mk)


def state_kernel(u_ref, before_ref, after_ref, base_ref, au, ag, hu, hg, m0):
    mk = Masks()
    mat = TIME_STEP * LINES[2]
    top, bottom = np.eye(4)[3], np.eye(4)[0]

    def layered(row_low, row_high, near):
        order = ((0, 1), (1, 0), (2, 3), (3, 2)) + (((UM, UP), (GM, GP)) if near else ())
        return [mk.by_layer(row_low[low], row_high[high]) for low, high in order]

    step = np.eye(4, 8) + mat
    slopes = layered(SLOPE[3], SLOPE[0], False)
    later = layered(step[3], step[0], True)
    later_slopes = layered(SLOPE[3] @ step, SLOPE[0] @ step, True)

    def unpack(v, carry):
        for c in range(8):
            col = v * 8 + c
            low = [before_ref[rows8(part * COLS + col), :] for part in range(3)]
            high = [after_ref[rows8(part * COLS + col), :] for part in range(3)]
            tiles = []
            for part in range(2):
                tiles.append(jnp.where(mk.l0, low[part], high[part]))
                tiles.append(jnp.where(mk.l0, rolled(low[part], -2), rolled(high[part], 2)))
            tiles.append(jnp.where(mk.l0, low[2], rolled(high[2], 2)))
            tiles.append(jnp.where(mk.l0, rolled(low[2], -2), high[2]))
            at = rows8(col)
            au[at, :] = jnp.where(mk.l0, tiles[3], tiles[1])
            ag[at, :] = combine(zip(slopes, tiles))
            hu[at, :] = combine(zip(later, tiles))
            hg[at, :] = combine(zip(later_slopes, tiles))
        return carry

    lax.fori_loop(0, VARS, unpack, 0)
    apply_operator(u_ref, m0, au, ag, mk, TIME_STEP, 1.0, pitches=(8, 8))

    x_mat, coefs = TIME_STEP * LINES[0], y_coefs(mk, TIME_STEP * LINES[1])

    def halo(v, carry):
        for c in range(8):
            col = v * 8 + c
            u = [u_ref[rows8(col * 4 + k), :] for k in range(4)]
            g0 = combine((SLOPE[0, b], u[b]) for b in range(4))
            g3 = combine((SLOPE[3, b], u[b]) for b in range(4))
            for h, f_low, f_high in ((hu, top, bottom), (hg, SLOPE[3], SLOPE[0])):
                low = combine(((f_low @ mat[:, UP], u[0]), (f_low @ mat[:, GP], g0)))
                high = combine(((f_high @ mat[:, UM], u[3]), (f_high @ mat[:, GM], g3)))
                h[rows8(col), :] += jnp.where(mk.l0, low, high)
        for a, h in ((au, hu), (ag, hg)):
            for i in range(4):
                at = [rows8(v * 8 + 2 * i + jj) for jj in range(2)]
                new = y_line(a[at[0], :], a[at[1], :], mk, coefs)
                for jj in range(2):
                    h[at[jj], :] += new[jj]
            for jj in range(2):
                at = [rows8(v * 8 + 2 * i + jj) for i in range(4)]
                new = x_line([a[r, :] for r in at], mk, x_mat)
                for i in range(4):
                    h[at[i], :] += new[i]
        return carry

    lax.fori_loop(0, VARS, halo, 0)
    apply_operator(m0, base_ref, hu, hg, mk, 0.5 * TIME_STEP, 0.5)

    def finish(n, carry):
        base_ref[rows8(n), :] += 0.5 * u_ref[rows8(n), :]
        return carry

    lax.fori_loop(0, TILES, finish, 0, unroll=16)


def line_basis(coords):
    rows = []
    for a in range(4):
        term = None
        for k in range(4):
            if k != a:
                factor = (coords - NODE_POINTS[k]) * (1.0 / (NODE_POINTS[a] - NODE_POINTS[k]))
                term = factor if term is None else term * factor
        rows.append(term)
    return rows


def place_of(slots, table, row):
    number = slots.astype(jnp.int32)
    inner, outer = number & 127, number >> 7
    found = jnp.zeros((8, 128), F32)
    for t in range(4):
        line = jnp.broadcast_to(table[row + t : row + t + 1, :], (8, 128))
        found = jnp.where(outer == t, jnp.take_along_axis(line, inner, axis=1), found)
    return found.astype(jnp.int32)


def fill_hot(hot, place):
    ids = lax.broadcasted_iota(jnp.int32, (16, 128), 0)
    one, none = jnp.ones((16, 128), BF16), jnp.zeros((16, 128), BF16)
    rows = [jnp.broadcast_to(place[c : c + 1, :], (16, 128)).astype(jnp.int16) for c in range(CAP)]
    for first in range(0, hot.shape[0], 16):
        here = (ids + first).astype(jnp.int16)
        for c in range(CAP):
            hot[first : first + 16, c * 128 : c * 128 + 128] = jnp.where(here == rows[c], one, none)


def fill_terms(matrix, columns, nodes, strength, grid, group, first, count, split=None):
    split = count if split is None else split
    if first == 0:
        for n, tile in enumerate(nodes):
            grid[group, n * 8 : n * 8 + 8, :] = tile
        for n, tile in enumerate(columns):
            strength[group, n * 8 : n * 8 + 8, :] = tile
    for c in range(CAP):
        here = slice(c * 128, c * 128 + 128)
        node_rows = grid[group, pl.ds(c, 16, stride=8), :]
        for n in range(first, first + count):
            hi, lo = split2(node_rows * strength[group, n * 8 + c : n * 8 + c + 1, :])
            at = (first + n) * 16
            matrix[at : at + 16, here] = hi
            if n - first < split:
                matrix[at + count * 16 : at + count * 16 + 16, here] = lo


def trace_terms(field, node):
    bx, by, bz = [line_basis(field[5 + d]) for d in range(3)]
    slope = combine((SLOPE[node, b], bz[b]) for b in range(4))
    columns = [field[v] * bz[node] for v in range(VARS)]
    columns += [field[v] * slope for v in range(VARS)]
    pairs = [(i, j) for h in range(2) for i in range(4) for j in NODE_ROWS[2 * h : 2 * h + 2]]
    return columns, [by[j] * bx[i] for i, j in pairs]


SPANS = ((0, 3), (3, 2))
BACK = ((0, 3), (3, 1), (4, 1))


def source_kernel(
    pts_ref, inv_ref, before_ref, after_ref, base_ref, order, out_hbm,
    hot, hot_low, hot_up, lhs, lhs_low, lhs_up, grid, strength, su, sg, s_ref, new_ref,
    lhs_out, out_ref, sems,
):
    mk = Masks()
    halves = [pts_ref[pl.ds(h, 128, stride=2), :].T for h in range(2)]
    data = jnp.concatenate(halves, axis=0)
    field = [
        [data[g * GROUP + f * 8 : g * GROUP + f * 8 + 8] for f in range(FIELDS)] for g in range(3)
    ]
    bx, by, bz = [line_basis(field[0][5 + d]) for d in range(3)]
    columns = [field[0][v] * bx[i] for v in range(VARS) for i in range(4)]
    nodes = [by[j] * bz[k] for j in NODE_ROWS for k in range(4)]
    vals, traces, copies = {}, {}, []
    in_layer, across = operator_of(
        s_ref, new_ref, su, sg, mk, 0.5 * TIME_STEP * TIME_STEP, TIME_STEP, base_ref, (PITCH, PITCH)
    )

    def gather(n):
        first, count = SPANS[n]
        fill_terms(lhs, columns, nodes, strength, grid, 0, first * 4, count * 4)
        vals[n] = both(nt_dot(lhs[first * 128 : (first + count) * 128, :], hot[...]))

    def gather_traces(side):
        matrix, goal = ((lhs_low, hot_low), (lhs_up, hot_up))[side]
        table, shift = ((before_ref, 256), (after_ref, 0))[side]
        fill_hot(goal, place_of(field[1 + side][8], table, 0) - shift)
        fill_terms(matrix, *trace_terms(field[1 + side], 3 - 3 * side), strength, grid, 1 + side, 0, 10, 5)
        res = nt_dot(matrix[...], goal[...])
        traces[side] = jnp.concatenate([res[:80] + res[160:], res[80:160]], axis=0)

    def spread_traces():
        for part, goal in ((0, su), (1, sg)):
            for v in range(VARS):
                for h in range(2):
                    at = (part * VARS + v) * 16 + h * 8
                    for t in range(4):
                        tile = traces[t // 2][at : at + 8, (t % 2) * 128 : (t % 2) * 128 + 128]
                        goal[pl.ds(v * 64 + h * 4 + t, 8, stride=8), :] = tile

    def advance(n, step):
        first, count = SPANS[n]
        if step is in_layer:
            spread(vals[n], s_ref, first * 4, PITCH)
        for v in range(first, first + count):
            step(v)

    def put_back(n):
        first, count = BACK[n]
        for vi in range(first * 4, (first + count) * 4):
            at = (first * 4 + vi) * 16
            for t in range(4):
                rows = [pl.ds(vi * 8 * PITCH + h * 4 + t, 8, stride=PITCH) for h in range(2)]
                x = jnp.concatenate([new_ref[r, :] for r in rows], axis=0)
                hi, lo = split2(x)
                lhs_out[at : at + 16, t * 128 : t * 128 + 128] = hi
                at_lo = at + count * 64
                lhs_out[at_lo : at_lo + 16, t * 128 : t * 128 + 128] = lo
        val = both(nt_dot(lhs_out[first * 128 : (first + count) * 128, :], order[...]))
        for vi in range(first * 4, (first + count) * 4):
            for m, j in enumerate(NODE_ROWS):
                at = (vi - first * 4) * 16 + m * 4
                out_ref[vi * 4 + j] = val[at : at + 4, :]
        part = pl.ds(first * 16, count * 16)
        copies.append(pltpu.make_async_copy(out_ref.at[part], out_hbm.at[part], sems.at[n]))
        copies[-1].start()

    fill_hot(hot, place_of(field[0][8], inv_ref, 0))
    gather(0)
    gather_traces(0)
    gather_traces(1)
    gather(1)
    advance(0, in_layer)
    spread_traces()
    advance(0, across)
    advance(1, in_layer)
    put_back(0)
    advance(1, across)
    put_back(1)
    put_back(2)
    for copy in copies:
        copy.wait()


def call(kernel, outs, scratch, specs, place=pltpu.VMEM):
    return pl.pallas_call(
        kernel,
        out_shape=outs,
        in_specs=specs,
        out_specs=jax.tree.map(lambda _: pl.BlockSpec(memory_space=place), outs),
        scratch_shapes=scratch,
        compiler_params=pltpu.CompilerParams(vmem_limit_bytes=VMEM_LIMIT),
    )


def tile_array(count):
    return jax.ShapeDtypeStruct((count * 8, 128), F32)


VMEM = pl.BlockSpec(memory_space=pltpu.VMEM)


def entry_call(route, slots, forces, coords, lists, state):
    arrays = (route, slots, forces, coords, lists, state)
    return call(
        entry_kernel,
        (
            jax.ShapeDtypeStruct((256, 128), F32),
            tile_array(TILES),
            tile_array(HALO_TILES + 1),
            tile_array(HALO_TILES + 1),
            tile_array(1),
            jax.ShapeDtypeStruct((512, 512), BF16),
        ),
        [pltpu.VMEM(x.shape, x.dtype) for x in arrays]
        + [
            pltpu.VMEM((640, 512), BF16),
            pltpu.SemaphoreType.DMA((6,)),
        ],
        [pl.BlockSpec(memory_space=pltpu.HBM)] * 6,
    )(*[pltpu.with_memory_space_constraint(x, pltpu.HBM) for x in arrays])


def state_call(u, before, after):
    cols = pltpu.VMEM((COLS * 8, 128), F32)
    return call(
        state_kernel,
        tile_array(TILES),
        [cols, cols, cols, cols, pltpu.VMEM((TILES * 8, 128), F32)],
        [VMEM] * 3,
    )(u, before, after)


def source_call(pts, inv, before, after, base, order):
    cols = pltpu.VMEM((COLS * 8, 128), F32)
    field = pltpu.VMEM((TILES * PITCH, 128), F32)
    return call(
        source_kernel,
        jax.ShapeDtypeStruct((VARS * 16, 4, 512), F32),
        [
            pltpu.VMEM((512, 1024), BF16),
            pltpu.VMEM((256, 1024), BF16),
            pltpu.VMEM((256, 1024), BF16),
            pltpu.VMEM((640, 1024), BF16),
            pltpu.VMEM((240, 1024), BF16),
            pltpu.VMEM((240, 1024), BF16),
            pltpu.VMEM((3, 128, 128), F32),
            pltpu.VMEM((3, 160, 128), F32),
            cols,
            cols,
            field,
            field,
            pltpu.VMEM((640, 512), BF16),
            pltpu.VMEM((VARS * 16, 4, 512), F32),
            pltpu.SemaphoreType.DMA((3,)),
        ],
        [VMEM] * 6,
        pltpu.HBM,
    )(pts, inv, before, after, base, order)


def on_device(state, neighbour_map, layer_lists, forces, positions, route, element_slot):
    count = lax.axis_size("sfc")
    forward = [(d, (d + 1) % count) for d in range(count)]
    backward = [(target, source) for source, target in forward]
    pack, u, up, down, inv, order = entry_call(
        route.reshape(1, -1),
        element_slot.reshape(1, -1),
        forces,
        positions,
        layer_lists,
        state.reshape(VARS * 16, 4, -1),
    )
    before = lax.ppermute(up, "sfc", forward)
    after = lax.ppermute(down, "sfc", backward)
    pts = lax.all_to_all(pack, "sfc", split_axis=0, concat_axis=0, tiled=True)
    base = state_call(u, before, after)
    table = slice(HALO_TILES * 8, None)
    out = source_call(pts, inv, before[table], after[table], base, order)
    return out.reshape(state.shape)


def solution(mesh):
    in_specs = (
        P(None, None, None, None, "sfc"),
        P(None, "sfc"),
        P(None, "sfc"),
        P(None, "sfc"),
        P(None, "sfc"),
        P("sfc", None),
        P("sfc"),
    )
    out_specs = P(None, None, None, None, "sfc")
    return jax.shard_map(
        on_device, mesh=mesh, in_specs=in_specs, out_specs=out_specs, check_vma=False
    )
```
